32 devices in a mesh: gx: 8 (over z, y), gy: 4 (over x, core).
Axes of the slice: x: 2, y: 2, z: 4, core: 2. Of those that a mesh axis runs over, the one named last changes fastest.
Arguments:
- jitter: float32 [4096, 3, 128], P(('gx', 'gy')), may hold values from -0.2 to 0.2
- displacement: float32 [4096, 3, 128], P(('gx', 'gy')), may hold values from -0.1 to 0.1
- modulus: float32 [4096, 128], P(('gx', 'gy')), may hold values from 0.1 to 1
- start_vec: float32 [4096, 3, 128], P(('gx', 'gy')), may hold values from -6 to 6
- old_home: int32 [4096], P(('gx', 'gy')), may hold values from 0 to 4095, as said below
- ghost_send: int32 [32, 9, 16], P(('gx', 'gy')), may hold values from -1 to 127, as said below
- pair_list: int32 [32, 4, 512], P(('gx', 'gy')), may hold values from -1 to 271, as said below
- pair_count: int32 [32], P(('gx', 'gy')), may hold values from 64 to 512, as said below
- broken: int32 [16384, 16, 128], P(('gx', 'gy')), may hold values from 0 to 255
Outputs:
- first_image: float32 [4096, 3, 128], P(('gx', 'gy'))
- second_image: float32 [4096, 3, 128], P(('gx', 'gy'))
The draws below stay inside these ranges and needn't reach their ends.
Inputs may be any that keep to these rules, and one draw needn't show every extreme that they name: `old_home`: A permutation. Row i of the old layout and row j of the rebalanced layout belong to devices i // 128 and j // 128; each device hands exactly 16 of its old tiles to each device beside it along gx or along gy (grid places differing by one in one coordinate, no wrap) and keeps the others. `ghost_send`: directions whose receiver lies outside the grid, and direction 4, hold only -1; for every other direction the first 1 to 16 slots hold rows below 128 and the rest -1; every device fills all 16 slots toward some neighbour along gx or gy. `pair_list`: tile is below 128; partner is below 128, or 128 + e * 16 + k where the device at offset (e // 3 - 1, e mod 3 - 1) exists and its slot k toward this device holds a row; shifts are -1, 0 or 1; when both shifts are 0, partner equals tile. Slots past the count are filled the same way. `pair_count`: at least 64; some device has 512.
All inputs are finite; a program needn't handle non-finite values.
Results may differ from the reference program's by a relative error of at most 0.0003.
Values sent between devices are 32-bit elements; how exact they have to be, the bound alone decides.
A program may use at most 64 MiB of HBM per device.

```python
import math
import jax
import jax.numpy as jnp
from jax import lax

P_SIZE = 128
TILES_DEV = 128
GCAP = 16
CAP = 16
TILES = 4096
PAIRS = 512
WORDS = 16
N_GX = 8
N_GY = 4
DEVICES = 32


def grid_valid():
    device_count = TILES // TILES_DEV
    device_ids = jnp.arange(device_count)
    place_x = device_ids // N_GY
    place_y = device_ids % N_GY
    cells = jnp.arange(9)
    near_x = place_x[:, None] + cells[None, :] // 3 - 1
    near_y = place_y[:, None] + cells[None, :] % 3 - 1
    inside = (near_x >= 0) & (near_x < N_GX) & (near_y >= 0) & (near_y < N_GY)
    return inside & (cells[None, :] != 4)


def ghost_counts(key):
    device_count = TILES // TILES_DEV
    key_count, key_coin = jax.random.split(jax.random.fold_in(key, 11))
    counts = jax.random.randint(key_count, (device_count, 9), 1, GCAP + 1)
    device_ids = jnp.arange(device_count)
    place_x = device_ids // N_GY
    place_y = device_ids % N_GY
    step_x = jnp.where(place_x < N_GX - 1, 1, -1)
    step_y = jnp.where(place_y < N_GY - 1, 1, -1)
    coin = jax.random.randint(key_coin, (device_count,), 0, 2)
    full_cell = jnp.where(coin == 0, (1 + step_x) * 3 + 1, 3 + (1 + step_y))
    counts = counts.at[device_ids, full_cell].set(GCAP)
    return jnp.where(grid_valid(), counts, 0)


def draw_ghost_send(key, part):
    device_count = TILES // TILES_DEV
    counts = ghost_counts(key)
    rows_drawn = jax.random.randint(jax.random.fold_in(key, 12), (device_count, 9, GCAP), 0, TILES_DEV)
    slot_index = jnp.arange(GCAP)
    return jnp.where(slot_index[None, None, :] < counts[:, :, None], rows_drawn, -1).astype(jnp.int32)


def draw_pair_list(key, part):
    device_count = TILES // TILES_DEV
    counts = ghost_counts(key)
    keys_all = jax.random.split(jax.random.fold_in(key, 13), 6)
    tile_row = jax.random.randint(keys_all[0], (device_count, PAIRS), 0, TILES_DEV)
    local_row = jax.random.randint(keys_all[1], (device_count, PAIRS), 0, TILES_DEV)
    drawn_dir = jax.random.randint(keys_all[2], (device_count, PAIRS), 0, 8)
    cell = drawn_dir + (drawn_dir >= 4).astype(jnp.int32)
    off_x = cell // 3 - 1
    off_y = cell % 3 - 1
    device_ids = jnp.arange(device_count)[:, None]
    near_x = device_ids // N_GY + off_x
    near_y = device_ids % N_GY + off_y
    exists = (near_x >= 0) & (near_x < N_GX) & (near_y >= 0) & (near_y < N_GY)
    source = jnp.clip(near_x * N_GY + near_y, 0, device_count - 1)
    limit = jnp.where(exists, counts[source, (1 - off_x) * 3 + (1 - off_y)], 0)
    slot_drawn = jax.random.randint(keys_all[3], (device_count, PAIRS), 0, jnp.maximum(limit, 1))
    ghost_ref = TILES_DEV + cell * GCAP + slot_drawn
    choose_kind = jax.random.randint(keys_all[4], (device_count, PAIRS), 0, 2)
    partner = jnp.where((choose_kind == 1) & (limit > 0), ghost_ref, local_row)
    shifts = jax.random.randint(keys_all[5], (device_count, 2, PAIRS), -1, 2)
    coincide = jnp.logical_and(shifts[:, 0] == 0, shifts[:, 1] == 0)
    partner = jnp.where(coincide, tile_row, partner)
    return jnp.stack([tile_row, partner, shifts[:, 0], shifts[:, 1]], axis=1).astype(jnp.int32)


def draw_pair_count(key, part):
    device_count = TILES // TILES_DEV
    key_level, key_top = jax.random.split(jax.random.fold_in(key, 14))
    level = jax.random.randint(key_level, (device_count,), 0, 65)
    level = level.at[jax.random.randint(key_top, (), 0, device_count)].set(64)
    return (PAIRS // 8 + (PAIRS - PAIRS // 8) * level * level // 4096).astype(jnp.int32)


def draw_old_home(key, part):
    device_count = TILES // TILES_DEV
    keys_all = jax.random.split(jax.random.fold_in(key, 15), 2)
    shuffles = jax.vmap(lambda sub_key: jax.random.permutation(sub_key, TILES_DEV))(jax.random.split(keys_all[0], device_count))
    block = jnp.minimum(shuffles // CAP, 4)
    step_x = jnp.array([-1, 1, 0, 0, 0])[block]
    step_y = jnp.array([0, 0, -1, 1, 0])[block]
    device_ids = jnp.arange(device_count)[:, None]
    near_x = device_ids // N_GY + step_x
    near_y = device_ids % N_GY + step_y
    exists = (block < 4) & (near_x >= 0) & (near_x < N_GX) & (near_y >= 0) & (near_y < N_GY)
    target = jnp.where(exists, near_x * N_GY + near_y, device_ids).reshape(-1)
    order_key = target * TILES + jax.random.permutation(keys_all[1], TILES)
    return jnp.argsort(order_key, stable=True).astype(jnp.int32)


def place_ends(values, rng, low, top_value):
    extent = values.shape
    place = [jax.random.randint(jax.random.fold_in(rng, axis), (), 0, extent[axis]) for axis in range(len(extent))]
    values = values.at[tuple(place)].set(low)
    longest = extent.index(max(extent))
    place[longest] = (place[longest] + 1) % extent[longest]
    return values.at[tuple(place)].set(top_value)


def steps_of(rng, extent, pieces, low, top_value):
    def one(axis_at, shards_of):
        steps = jax.random.uniform(jax.random.fold_in(jax.random.fold_in(rng, 6), axis_at), (shards_of,), jnp.float32, low / len(pieces), top_value / len(pieces))
        return jnp.repeat(jnp.exp(steps), extent[axis_at] // shards_of).reshape((-1,) + (1,) * (len(extent) - axis_at - 1))

    gain = one(*pieces[0])
    for cut in pieces[1:]:
        gain = gain * one(*cut)
    return gain


def centred(key, dims, scale, reach, shards=(), kind=jnp.bfloat16):
    values = jax.random.normal(key, dims, jnp.float32) * scale
    if len(shards) > 0:
        values = steps_of(key, dims, shards, -0.22, 0.18) * values
    return jnp.clip(values, min=-reach, max=reach).astype(kind)


def setup_inputs(seed: int = 0) -> dict:
    keys = jax.random.split(jax.random.key(seed), 10)
    jitter = jnp.clip(jax.random.uniform(keys[0], (TILES, 3, P_SIZE), jnp.float32, -0.2, 0.2) * steps_of(keys[0], (TILES, 3, P_SIZE), ((0, 32),), -0.4, 0.0), -0.2, 0.2)
    displacement = jnp.clip(jax.random.uniform(keys[1], (TILES, 3, P_SIZE), jnp.float32, -0.1, 0.1) * steps_of(keys[1], (TILES, 3, P_SIZE), ((0, 32),), -0.4, 0.0), -0.1, 0.1)
    modulus = jnp.clip(jnp.exp(math.log(1.0) - 2.3025851 * jax.random.uniform(keys[2], (TILES, P_SIZE), jnp.float32) ** steps_of(keys[2], (TILES, P_SIZE), ((0, 32),), -0.2, 0.2)), 0.1, 1.0)
    start_vec = centred(keys[3], (TILES, 3, P_SIZE), 1.0, 6.0, ((0, 32),), jnp.float32)
    old_home = draw_old_home(jax.random.fold_in(keys[9], 71), 0)
    ghost_send = draw_ghost_send(jax.random.fold_in(keys[9], 71), 0)
    pair_list = draw_pair_list(jax.random.fold_in(keys[9], 71), 0)
    pair_count = draw_pair_count(jax.random.fold_in(keys[9], 71), 0)
    broken = place_ends(jax.random.randint(keys[8], (DEVICES * PAIRS, WORDS, P_SIZE), 0, 256), jax.random.fold_in(keys[8], 1), 0, 255).astype(jnp.int32)
    return {"jitter": jitter, "displacement": displacement, "modulus": modulus, "start_vec": start_vec, "old_home": old_home, "ghost_send": ghost_send, "pair_list": pair_list, "pair_count": pair_count, "broken": broken}


def lattice(points):
    counter = jnp.arange(points, dtype=jnp.int32)
    return jnp.stack([counter % 8, counter // 8 % (points // 16), counter // (points // 2)]).astype(jnp.float32)

def pair_force(geom_a, geom_b, vector_a, vector_b, shifts, flag_words):
    placed_a, current_a, modulus_a = geom_a
    placed_b, current_b, modulus_b = geom_b
    points = placed_a.shape[1]
    offset = jnp.stack([shifts[0] * 8, shifts[1] * (points // 16), shifts[0] * 0]).astype(jnp.float32)
    coincide = jnp.logical_and(shifts[0] == 0, shifts[1] == 0)
    diagonal = jnp.where(coincide, jnp.eye(points, dtype=jnp.float32), jnp.zeros((points, points), jnp.float32))
    ref_bond = placed_b[:, :, None] + offset[:, None, None] - placed_a[:, None, :]
    cur_bond = ref_bond + current_b[:, :, None] - current_a[:, None, :]
    ref_square = lax.optimization_barrier(jnp.sum(ref_bond * ref_bond, axis=0)) + diagonal
    cur_square = lax.optimization_barrier(jnp.sum(cur_bond * cur_bond, axis=0)) + diagonal
    ref_len = jnp.sqrt(ref_square)
    cur_len = jnp.sqrt(cur_square)
    flag_bits = jnp.right_shift(flag_words[:, None, :], jnp.arange(8, dtype=jnp.int32)[None, :, None]) & 1
    intact = 1.0 - flag_bits.reshape(points, points).astype(jnp.float32)
    weight = jnp.maximum(1.0 - ref_square / 9.0, 0.0) * intact * (1.0 - diagonal)
    bond_scale = 0.05 * (modulus_b[:, None] + modulus_a[None, :]) * weight
    stiff_axial = bond_scale / ref_len
    stiff_cross = bond_scale * (cur_len - ref_len) / (ref_len * cur_len)
    direction = cur_bond / cur_len
    change = vector_b[:, :, None] - vector_a[:, None, :]
    projected = lax.optimization_barrier(jnp.sum(direction * change, axis=0))
    return lax.optimization_barrier(jnp.sum(stiff_cross * change + (stiff_axial - stiff_cross) * direction * projected, axis=1))

def reference(jitter, displacement, modulus, start_vec, old_home, ghost_send, pair_list, pair_count, broken):
    device_count = TILES // TILES_DEV
    placed = lattice(P_SIZE)[None] + jitter[old_home]
    current = displacement[old_home]
    moduli = modulus[old_home]
    vector = start_vec[old_home]
    owner = jnp.broadcast_to(jnp.arange(device_count, dtype=jnp.int32)[:, None], (device_count, PAIRS))
    grid_x = owner // N_GY
    grid_y = owner % N_GY
    tile_row = pair_list[:, 0]
    partner = pair_list[:, 1]
    ghost_ref = jnp.maximum(partner - TILES_DEV, 0)
    direction_in = ghost_ref // GCAP
    ghost_slot = ghost_ref % GCAP
    off_x = direction_in // 3 - 1
    off_y = direction_in % 3 - 1
    source = jnp.clip((grid_x + off_x) * N_GY + (grid_y + off_y), 0, device_count - 1).astype(jnp.int32)
    send_dir = ((1 - off_x) * 3 + (1 - off_y)).astype(jnp.int32)
    remote = ghost_send[source, send_dir, ghost_slot]
    row_b = jnp.where(partner < TILES_DEV, owner * TILES_DEV + partner, source * TILES_DEV + remote).reshape(-1).astype(jnp.int32)
    row_a = (owner * TILES_DEV + tile_row).reshape(-1).astype(jnp.int32)
    shifts = jnp.transpose(pair_list[:, 2:4], (0, 2, 1)).reshape(-1, 2)
    active = (jnp.arange(PAIRS, dtype=jnp.int32)[None, :] < pair_count[:, None]).reshape(-1).astype(jnp.float32)
    group_len = 64

    def tangent_apply(field):

        def pair_group(batch):
            rows_a, rows_b, group_shifts, group_words = batch
            geom_a = (placed[rows_a], current[rows_a], moduli[rows_a])
            geom_b = (placed[rows_b], current[rows_b], moduli[rows_b])
            return jax.vmap(pair_force)(geom_a, geom_b, field[rows_a], field[rows_b], group_shifts, group_words)
        pair_terms = lax.map(pair_group, (row_a.reshape(-1, group_len), row_b.reshape(-1, group_len), shifts.reshape(-1, group_len, 2), broken.reshape(-1, group_len, WORDS, P_SIZE)))
        pair_terms = pair_terms.reshape(-1, 3, P_SIZE) * active[:, None, None]
        return jax.ops.segment_sum(pair_terms, row_a, num_segments=TILES)
    first_image = tangent_apply(vector)
    second_image = tangent_apply(first_image)
    return (first_image, second_image)
```

```python
import functools
import jax
import jax.numpy as jnp
import numpy as np
from jax import lax
from jax.experimental import pallas as pl
from jax.experimental.pallas import tpu as pltpu
from jax.sharding import PartitionSpec as P

CAP = 16
F32 = jnp.float32
BF16 = jnp.bfloat16
VMEM = pl.BlockSpec(memory_space=pltpu.VMEM)
SMEM = pl.BlockSpec(memory_space=pltpu.SMEM)
LIMIT = pltpu.CompilerParams(vmem_limit_bytes=48 * 1024 * 1024)
DIRS = (0, 1, 2, 3, 5, 6, 7, 8)
FIELDS = 10
CHUNK = 16
LANES = 128


def near(dx, dy):
    return max(abs(dx) - 0.4, 0.0) ** 2 + max(abs(dy) - 0.4, 0.0) ** 2 < 9.0


def point(x, y, z):
    return x + 8 * y + 64 * z


HALF = [(dx, dy) for dy in range(4) for dx in range(-3, 4) if (dy > 0 or dx > 0) and near(dx, dy)]
OFFSETS = [(0, 0, 1)] + [(dx, dy, f) for dx, dy in HALF for f in (0, 1)]


def self_tables():
    sel = np.zeros((2 * LANES, len(OFFSETS) * LANES), np.float32)
    bits = np.zeros((-(-2 * len(OFFSETS) // 8) * 8, LANES), np.int32)
    for n, (dx, dy, f) in enumerate(OFFSETS):
        for lane in range(LANES):
            x, y, z = lane % 8, lane // 8 % 8, lane // 64
            if 0 <= x + dx < 8 and 0 <= y + dy < 8:
                for half in (0, LANES):
                    sel[half + point(x + dx, y + dy, z ^ f), n * LANES + lane] += 1
                    sel[half + lane, n * LANES + lane] -= 1
                bits[2 * n, lane] = 1 << (x + dx)
            if 0 <= x - dx < 8 and 0 <= y - dy < 8:
                bits[2 * n + 1, lane] = 1 << (x - dx)
    return sel, bits


OFFSET_LANES = (27, 28, 35)
NEAR = [(7, 0), (7, 1), (6, 0), (7, 2), (6, 1), (5, 0)]
FAR = [(7, 0, 2), (7, 1, 2), (6, 0, 2), (7, 0, 3), (7, 0, -2), (7, 1, -2), (6, 0, -2), (7, 0, -3)]


def fill(sel, col, a, b, shift):
    for half in (0, LANES):
        sel[half + point(*b), col] += 1
        sel[half + point(*a), col] -= 1
        for c in range(3):
            sel[half + OFFSET_LANES[c], col] = b[c] - a[c] + shift[c]


def face_tables():
    sels = np.zeros((4, 2 * LANES, 8 * LANES), np.float32)
    backs = np.zeros((4, 2 * LANES, LANES), np.float32)
    tabs = np.zeros((4, 16, LANES), np.int32)
    for k in range(4):
        axis, sign = k // 2, 1 - 2 * (k % 2)
        side = lambda u: u if sign > 0 else 7 - u
        place = lambda u, t, z: (u, t, z) if axis == 0 else (t, u, z)
        shift = place(8 * sign, 0, 0)
        sel, back, tab = sels[k], backs[k], tabs[k]
        for z in range(2):
            for t in range(8):
                for c in range(8):
                    lane = point(*place(c, t, z))
                    ua, ub, dt = FAR[c]
                    a = place(side(ua), t, z)
                    tab[9, lane] = point(*a)
                    tab[12, lane] = ub
                    tab[13, lane] = dt
                    back[LANES + lane, point(*a)] = 1
                    todo = [(6 + f, f, a, ub, dt) for f in range(2)]
                    if c < len(NEAR):
                        ua, ub = NEAR[c]
                        a = place(side(ua), t, z)
                        tab[8, lane] = point(*a)
                        tab[11, lane] = ub
                        back[lane, point(*a)] = 1
                        todo += [(2 * m + f, f, a, ub, m - 1) for m in range(3) for f in range(2)]
                    for v, f, a, ub, dt in todo:
                        if 0 <= t + dt < 8:
                            b = place(side(ub), t + dt, z ^ f)
                            fill(sel, v * LANES + lane, a, b, shift)
                            tab[v, lane] = 1 << b[0]
                for u in range(3):
                    tab[10, point(*place(side(7 - u), t, z))] = 1
                    tab[10, point(*place(side(u), t, z))] = 2
        for col in range(8 * LANES):
            if not sel[:, col].any():
                sel[OFFSET_LANES[0], col] = 4
    return sels, backs, tabs


def corner_tables():
    sels = np.zeros((4, 2 * LANES, LANES), np.float32)
    backs = np.zeros((4, 2 * LANES, LANES), np.float32)
    tabs = np.zeros((4, 8, LANES), np.int32)
    combos = []
    for (ua, ub) in NEAR:
        for (va, vb) in NEAR:
            if near(ub + 8 - ua, vb + 8 - va):
                combos.append((ua, va, ub, vb))
    for k in range(4):
        sign_x, sign_y = 1 - 2 * (k // 2), 1 - 2 * (k % 2)
        side_x = lambda u: u if sign_x > 0 else 7 - u
        side_y = lambda u: u if sign_y > 0 else 7 - u
        sel, back, tab = sels[k], backs[k], tabs[k]
        for n, (ua, va, ub, vb) in enumerate(combos):
            for z in range(2):
                for f in range(2):
                    lane = n + 16 * z + 32 * f
                    a, b = (side_x(ua), side_y(va), z), (side_x(ub), side_y(vb), z ^ f)
                    fill(sel, lane, a, b, (8 * sign_x, 8 * sign_y, 0))
                    back[lane, point(*a)] = 1
                    back[LANES + lane, point(*a)] = 1
                    tab[0, lane] = 1 << b[0]
                    tab[1, lane] = point(*a)
                    tab[3, lane] = vb
                    tab[4, lane] = z ^ f
        for col in range(LANES):
            if not sel[:, col].any():
                sel[OFFSET_LANES[0], col] = 4
        for z in range(2):
            for u in range(3):
                for v in range(3):
                    tab[2, point(side_x(7 - u), side_y(7 - v), z)] = 1
                    tab[2, point(side_x(u), side_y(v), z)] = 2
    return sels, backs, tabs


def hand_kernel(asked, jit, disp, mod, vec, *outs):
    for out in outs:
        out[...] = jnp.zeros_like(out)

    def body(i, carry):
        for d, out in enumerate(outs):
            row = asked[d, i]
            out[i, 0:3] = jit[row]
            out[i, 3:6] = disp[row]
            out[i, 6:7] = mod[pl.ds(row, 1)]
            out[i, 7:10] = vec[row]
        return carry

    lax.fori_loop(0, CAP, body, 0)


def settle_kernel(pick, send, jit, disp, mod, vec, in0, in1, in2, in3, local, *rest):
    outs, pool = rest[:8], rest[8]
    rows = jit.shape[0]
    pool[0:rows] = jnp.zeros((rows,) + pool.shape[1:], F32)
    pool[0:rows, 0:3, :] = jit[...]
    pool[0:rows, 3:6, :] = disp[...]
    pool[0:rows, 7:10, :] = vec[...]

    def put_mod(j, carry):
        pool[j, 6:7, :] = mod[pl.ds(j, 1)]
        return carry

    lax.fori_loop(0, rows, put_mod, 0, unroll=8)
    for d, arrived in enumerate((in0, in1, in2, in3)):
        pool[rows + d * CAP : rows + (d + 1) * CAP] = arrived[...]
    points = jit.shape[2]
    sub = lax.broadcasted_iota(jnp.int32, (8, points), 0)
    scale = jnp.where(sub == 6, 0.05 / 9.0, 1.0)
    moved = (sub >= 3) & (sub < 6)

    def settle(j, carry):
        held = pool[pick[j]]
        low = held[0:8]
        local[j, 0:8] = low * scale + jnp.where(moved, pltpu.roll(low, 3, 0), 0.0)
        local[j, 8:16] = held[8:16]
        return carry

    lax.fori_loop(0, rows, settle, 0, unroll=8)

    def ghosts(i, carry):
        for c, out in zip(DIRS, outs):
            out[i] = local[jnp.maximum(send[c, i], 0)]
        return carry

    lax.fori_loop(0, outs[0].shape[0], ghosts, 0)


def split(value):
    high = value.astype(BF16)
    return high, (value - high.astype(F32)).astype(BF16)


def bond_force(xi, y, moduli, dv, keep):
    r2 = xi[0] * xi[0] + xi[1] * xi[1] + xi[2] * xi[2]
    l2 = y[0] * y[0] + y[1] * y[1] + y[2] * y[2]
    c = moduli * jnp.maximum(9.0 - r2, 0.0)
    if keep is not None:
        c = jnp.where(keep, c, 0.0)
    r_inv = lax.rsqrt(r2)
    l_inv = lax.rsqrt(l2)
    cl = c * l_inv
    k2 = c * r_inv - cl
    along = cl * (l_inv * l_inv) * (y[0] * dv[0] + y[1] * dv[1] + y[2] * dv[2])
    return [k2 * dv[i] + along * y[i] for i in range(3)]


def apply_kernel(first, pairs, order, bounds, send, owner, sel0, bits0, sel1, back1, tab1, sel2, back2, tab2, words, local, *rest):
    ghosts, rest = rest[:8], rest[8:]
    if not first:
        field, field_ghosts, rest = rest[0], rest[1:9], rest[9:]
    image, rest = rest[0], rest[1:]
    if first:
        sends, rest = rest[:8], rest[8:]
    full, side_a, side_b, flags, force = rest
    rows, depth, points = local.shape
    cap = ghosts[0].shape[0]
    full[0 : rows * depth] = local[...].reshape(rows * depth, points)
    for e, ghost in zip(DIRS, ghosts):
        full[(rows + e * cap) * depth : (rows + (e + 1) * cap) * depth] = ghost[...].reshape(cap * depth, points)
    if not first:
        for c in range(3):
            for j in range(0, rows, 8):
                full[pl.ds(j * depth + 7 + c, 8, stride=depth)] = field[c, j : j + 8]
            for e, ghost in zip(DIRS, field_ghosts):
                for j in range(0, cap, 8):
                    full[pl.ds((rows + e * cap + j) * depth + 7 + c, 8, stride=depth)] = ghost[c, j : j + 8]
    force[...] = jnp.zeros_like(force)

    def build(g, carry):
        for u in range(CHUNK):
            q = jnp.maximum(order[g * CHUNK + u], 0)
            for ref, row in ((side_a, pairs[0, q]), (side_b, pairs[1, q])):
                state = full[pl.ds(pl.multiple_of(row * depth, depth), depth)]
                ref[g, pl.ds(u, 8, stride=CHUNK)] = state[0:8]
                ref[g, pl.ds(8 * CHUNK + u, 2, stride=CHUNK)] = state[8:10]
            word = jnp.bitwise_not(words[q])
            flags[g, pl.ds(u, 8, stride=CHUNK)] = word[0:8]
            flags[g, pl.ds(8 * CHUNK + u, 8, stride=CHUNK)] = word[8:16]
        return carry

    lax.fori_loop(0, bounds[9], build, 0)

    lane = lax.broadcasted_iota(jnp.int32, (8, points), 1)
    lane_y = lane // 8 % 8
    low_z = lane < 64

    def row_of(ref, *at):
        return jnp.broadcast_to(ref[at], (8, points))

    def pick(value, index):
        return jnp.take_along_axis(value, index, axis=1, mode="promise_in_bounds")

    def word_of(g, h, y, z):
        start = (y + 8 * z) * CHUNK + 8 * h
        if not isinstance(start, int):
            start = pl.multiple_of(start, 8)
        return flags[g, pl.ds(start, 8)]

    def by_row(g, h):
        turned = []
        for z in range(2):
            held = [word_of(g, h, y, z) for y in range(8)]
            for bit in (1, 2, 4):
                odd = (lane_y & bit) != 0
                held = [jnp.where(odd, held[(s + bit) % 8], held[s]) for s in range(8)]
            turned.append(held)
        same = [jnp.where(low_z, turned[0][s], turned[1][s]) for s in range(8)]
        flip = [jnp.where(low_z, turned[1][s], turned[0][s]) for s in range(8)]
        return same, flip

    def left_side(values):
        parts = [split(v) for v in values]
        high = jnp.concatenate([p[0] for p in parts], axis=0)
        low = jnp.concatenate([p[1] for p in parts], axis=0)
        return jnp.concatenate([high, low], axis=1)

    def block(wide, c, h, v):
        return wide[c * CHUNK + 8 * h : c * CHUNK + 8 * h + 8, v * points : (v + 1) * points]

    def put(g, c, value):
        force[c, pl.ds(pl.multiple_of(g * CHUNK, CHUNK), CHUNK)] = value

    def same_tile(g, carry):
        left = left_side([side_a[g, c * CHUNK : (c + 1) * CHUNK] for c in range(FIELDS)])
        words_of = [by_row(g, h) for h in range(2)]
        twice = [2.0 * side_a[g, 6 * CHUNK + 8 * h : 6 * CHUNK + 8 * h + 8] for h in range(2)]
        acc = [[jnp.zeros((8, points), F32)] * 3 for _ in range(2)]
        other = jnp.where(low_z, 1.0, -1.0)
        for start in range(0, len(OFFSETS), 2):
            some = OFFSETS[start : start + 2]
            wide = jnp.dot(left, sel0[:, start * points : (start + len(some)) * points], preferred_element_type=F32)
            for v, (dx, dy, f) in enumerate(some):
                n = start + v
                base = (float(dx), float(dy), other if f else 0.0)
                for h in range(2):
                    part = lambda c: block(wide, c, h, v)
                    xi = [part(c) + base[c] for c in range(3)]
                    y = [part(3 + c) + base[c] for c in range(3)]
                    dv = [part(7 + c) for c in range(3)]
                    term = bond_force(xi, y, part(6) + twice[h], dv, None)
                    keep = (words_of[h][f][dy % 8] & row_of(bits0, pl.ds(2 * n, 1))) != 0
                    acc[h] = [acc[h][i] + jnp.where(keep, term[i], 0.0) for i in range(3)]
                    if (dx, dy) != (0, 0):
                        keep = (words_of[h][f][-dy % 8] & row_of(bits0, pl.ds(2 * n + 1, 1))) != 0
                        off = (dx + 8 * dy + 64 * f) % points
                        acc[h] = [acc[h][i] - jnp.where(keep, pltpu.roll(term[i], off, 1), 0.0) for i in range(3)]
        for c in range(3):
            put(g, c, jnp.concatenate([acc[0][c], acc[1][c]], axis=0))
        return carry

    lax.fori_loop(bounds[0], bounds[1], same_tile, 0)

    def joined(g, code):
        wide_lane = lax.broadcasted_iota(jnp.int32, (CHUNK, points), 1)
        take_a = jnp.broadcast_to(code == 1, (CHUNK, points))
        take_b = jnp.broadcast_to(code == 2, (CHUNK, points))
        values = []
        for c in range(FIELDS):
            a = side_a[g, c * CHUNK : (c + 1) * CHUNK]
            b = side_b[g, c * CHUNK : (c + 1) * CHUNK]
            rest_of = jnp.where(wide_lane == OFFSET_LANES[c % 3], 1.0, 0.0) if c < 6 else 0.0
            values.append(jnp.where(take_a, -a if c == 6 else a, jnp.where(take_b, b, rest_of)))
        return left_side(values)

    def of_block(wide, h, v, keep):
        part = lambda c: block(wide, c, h, v)
        xi = [part(c) for c in range(3)]
        y = [part(3 + c) for c in range(3)]
        dv = [part(7 + c) for c in range(3)]
        return bond_force(xi, y, part(6), dv, keep)

    def face(axis, g, carry):
        k = 2 * axis + jnp.where(g >= bounds[2 * axis + 2], 1, 0)
        left = joined(g, tab1[k, 10:11])
        index_near = row_of(tab1, k, pl.ds(8, 1))
        index_far = row_of(tab1, k, pl.ds(9, 1))
        near_words, far_words = [], []
        for h in range(2):
            if axis == 0:
                rel = by_row(g, h)
                dt = row_of(tab1, k, pl.ds(13, 1))
                near_words.append([[pick(rel[f][(m - 1) % 8], index_near) for f in range(2)] for m in range(3)])
                far = []
                for f in range(2):
                    chosen = pick(rel[f][2], index_far)
                    for d in (3, -2, -3):
                        chosen = jnp.where(dt == d, pick(rel[f][d % 8], index_far), chosen)
                    far.append(chosen)
                far_words.append(far)
            else:
                both = []
                for index, code in ((index_near, row_of(tab1, k, pl.ds(11, 1))), (index_far, row_of(tab1, k, pl.ds(12, 1)))):
                    got = []
                    for z in range(2):
                        chosen = None
                        for j in range(3):
                            y = jnp.where(k == 3, 7 - j, j)
                            word = pick(word_of(g, h, y, z), index)
                            chosen = word if j == 0 else jnp.where(code == j, word, chosen)
                        got.append(chosen)
                    both.append([jnp.where(low_z, got[0], got[1]), jnp.where(low_z, got[1], got[0])])
                near_words.append([both[0]] * 3)
                far_words.append(both[1])
        close = [[jnp.zeros((8, points), F32)] * 3 for _ in range(2)]
        distant = [[jnp.zeros((8, points), F32)] * 3 for _ in range(2)]
        for m in range(4):
            wide = jnp.dot(left, sel1[k, :, 2 * m * points : 2 * (m + 1) * points], preferred_element_type=F32)
            for f in range(2):
                for h in range(2):
                    word = near_words[h][m][f] if m < 3 else far_words[h][f]
                    keep = (word & row_of(tab1, k, pl.ds(2 * m + f, 1))) != 0
                    term = of_block(wide, h, f, keep)
                    acc = close if m < 3 else distant
                    acc[h] = [acc[h][i] + term[i] for i in range(3)]
        total = []
        for acc in (close, distant):
            stacked = jnp.concatenate([acc[h][c] for c in range(3) for h in range(2)], axis=0)
            high, low = split(stacked)
            total.append(jnp.concatenate([high, low], axis=0))
        back = jnp.dot(jnp.concatenate(total, axis=1), back1[k], preferred_element_type=F32)
        for c in range(3):
            at = c * CHUNK
            put(g, c, back[at : at + CHUNK] + back[3 * CHUNK + at : 3 * CHUNK + at + CHUNK])
        return carry

    for axis in range(2):
        lax.fori_loop(bounds[2 * axis + 1], bounds[2 * axis + 3], functools.partial(face, axis), 0)

    def corner(g, carry):
        k = sum(jnp.where(g >= bounds[c], 1, 0) for c in (6, 7, 8))
        left = joined(g, tab2[k, 2:3])
        index = row_of(tab2, k, pl.ds(1, 1))
        code = row_of(tab2, k, pl.ds(3, 1)) + 3 * row_of(tab2, k, pl.ds(4, 1))
        wide = jnp.dot(left, sel2[k], preferred_element_type=F32)
        terms = []
        for h in range(2):
            word = None
            for z in range(2):
                for j in range(3):
                    y = jnp.where((k & 1) == 1, 7 - j, j)
                    one = pick(word_of(g, h, y, z), index)
                    word = one if word is None else jnp.where(code == j + 3 * z, one, word)
            keep = (word & row_of(tab2, k, pl.ds(0, 1))) != 0
            terms.append(of_block(wide, h, 0, keep))
        stacked = jnp.concatenate([terms[h][c] for c in range(3) for h in range(2)], axis=0)
        back = jnp.dot(jnp.concatenate(split(stacked), axis=1), back2[k], preferred_element_type=F32)
        for c in range(3):
            put(g, c, back[c * CHUNK : (c + 1) * CHUNK])
        return carry

    lax.fori_loop(bounds[5], bounds[9], corner, 0)

    image[...] = jnp.zeros_like(image)
    tile_at = lax.broadcasted_iota(jnp.int32, (rows, LANES), 0)

    def gather_tiles(b, carry):
        hot = jnp.where(tile_at == owner[pl.ds(b, 1)], 1.0, 0.0).astype(BF16)
        parts = [split(force[c, pl.ds(pl.multiple_of(b * LANES, LANES), LANES)]) for c in range(3)]
        high = jnp.concatenate([p[0] for p in parts], axis=1)
        low = jnp.concatenate([p[1] for p in parts], axis=1)
        out = jnp.dot(
            jnp.concatenate([hot, hot], axis=1), jnp.concatenate([high, low], axis=0), preferred_element_type=F32
        )
        for c in range(3):
            image[c] += out[:, c * points : (c + 1) * points]
        return carry

    lax.fori_loop(0, (bounds[9] * CHUNK + LANES - 1) // LANES, gather_tiles, 0)
    if first:

        def ghost_rows(i, carry):
            for c, out in zip(DIRS, sends):
                row = jnp.maximum(send[c, i], 0)
                for n in range(3):
                    out[n, pl.ds(i, 1)] = image[n, pl.ds(row, 1)]
            return carry

        lax.fori_loop(0, cap, ghost_rows, 0)


def exchange_kernel(offsets, *refs):
    n = len(offsets)
    ins, outs, send_sem, recv_sem = refs[:n], refs[n : 2 * n], refs[2 * n], refs[2 * n + 1]
    n_x, n_y = lax.axis_size("gx"), lax.axis_size("gy")
    x, y = lax.axis_index("gx"), lax.axis_index("gy")

    def exists(ox, oy):
        return (x + ox >= 0) & (x + ox < n_x) & (y + oy >= 0) & (y + oy < n_y)

    barrier = pltpu.get_barrier_semaphore()
    for ox, oy in offsets:

        @pl.when(exists(ox, oy))
        def _():
            pl.semaphore_signal(
                barrier, inc=1, device_id=(x + ox, y + oy), device_id_type=pl.DeviceIdType.MESH
            )

    peers = sum(jnp.where(exists(ox, oy), 1, 0) for ox, oy in offsets)
    pl.semaphore_wait(barrier, peers)

    def copy(d):
        ox, oy = offsets[d]
        back = offsets.index((-ox, -oy))
        return pltpu.make_async_remote_copy(
            src_ref=ins[d],
            dst_ref=outs[back],
            send_sem=send_sem.at[d],
            recv_sem=recv_sem.at[back],
            device_id=(x + ox, y + oy),
            device_id_type=pl.DeviceIdType.MESH,
        )

    for d, (ox, oy) in enumerate(offsets):

        @pl.when(exists(ox, oy))
        def _():
            copy(d).start()

        @pl.when(jnp.logical_not(exists(ox, oy)))
        def _():
            outs[d][...] = jnp.zeros_like(outs[d])

    for d, (ox, oy) in enumerate(offsets):

        @pl.when(exists(ox, oy))
        def _():
            copy(d).wait_send()
            copy(offsets.index((-ox, -oy))).wait_recv()


def exchange(blocks, offsets, ident):
    n = len(offsets)
    return pl.pallas_call(
        functools.partial(exchange_kernel, offsets),
        out_shape=[jax.ShapeDtypeStruct(b.shape, b.dtype) for b in blocks],
        in_specs=[VMEM] * n,
        out_specs=[VMEM] * n,
        scratch_shapes=[pltpu.SemaphoreType.DMA((n,)), pltpu.SemaphoreType.DMA((n,))],
        compiler_params=pltpu.CompilerParams(
            collective_id=ident, has_side_effects=True, vmem_limit_bytes=16 * 1024 * 1024
        ),
    )(*blocks)


SIDES = ((-1, 0), (1, 0), (0, -1), (0, 1))
AROUND = tuple((e // 3 - 1, e % 3 - 1) for e in DIRS)
CLASSES = 9


def plan(pair_list, count):
    pairs = pair_list.shape[1]
    slots = -(-(pairs + CLASSES * (CHUNK - 1)) // LANES) * LANES
    slot = jnp.arange(pairs, dtype=jnp.int32)
    sx, sy = pair_list[2], pair_list[3]
    flat_x = jnp.where(sx > 0, 1, 2)
    flat_y = jnp.where(sy > 0, 3, 4)
    slant = 5 + 2 * (sx < 0) + (sy < 0)
    kind = jnp.where(sx == 0, jnp.where(sy == 0, 0, flat_y), jnp.where(sy == 0, flat_x, slant))
    kind = jnp.where(slot < count, kind, 15).astype(jnp.int32)
    ids = jnp.arange(16, dtype=jnp.int32)
    earlier = (kind[:, None] == kind[None, :]) & (slot[:, None] < slot[None, :])
    rank = jnp.sum(earlier.astype(jnp.int32), axis=0)
    before = (kind[:, None] < ids[None, :]) & (ids[None, :] < 15)
    member = kind[:, None] == ids[None, :]
    chunks = (jnp.sum(member.astype(jnp.int32), axis=0) + CHUNK - 1) // CHUNK
    start = jnp.sum(jnp.where(ids[:, None] < ids[None, :], chunks[:, None], 0), axis=0)
    place = rank + CHUNK * jnp.sum(jnp.where(member, start[None, :], 0), axis=1)
    place = jnp.where(kind < CLASSES, place, -1)
    hit = place[:, None] == jnp.arange(slots, dtype=jnp.int32)[None, :]
    order = jnp.sum(jnp.where(hit, slot[:, None] + 1, 0), axis=0) - 1
    owner = jnp.sum(jnp.where(hit, pair_list[0][:, None] + 1, 0), axis=0) - 1
    return order, start, owner.reshape(slots // LANES, LANES)


def on_device(jitter, displacement, modulus, start_vec, old_home, ghost_send, pair_list, pair_count, broken):
    tiles = old_home.shape[0]
    points = jitter.shape[2]
    cap = ghost_send.shape[2]
    width_y = lax.axis_size("gy")
    anchor = old_home // tiles
    old_slot = old_home % tiles
    off_x = anchor // width_y - lax.axis_index("gx")
    off_y = anchor % width_y - lax.axis_index("gy")
    side = jnp.where(off_x == -1, 0, jnp.where(off_x == 1, 1, jnp.where(off_y == -1, 2, jnp.where(off_y == 1, 3, 4))))
    index = jnp.arange(tiles, dtype=jnp.int32)
    earlier = (side[:, None] == side[None, :]) & (index[:, None] < index[None, :])
    ranked = jnp.sum(earlier.astype(jnp.int32), axis=0)
    cell = jnp.where(side < 4, side * CAP + ranked, -1)
    hit = cell[:, None] == jnp.arange(4 * CAP, dtype=jnp.int32)[None, :]
    wanted = jnp.sum(jnp.where(hit, old_slot[:, None], 0), axis=0).reshape(4, CAP)
    requests = [jnp.pad(wanted[d : d + 1], ((0, 7), (0, 128 - CAP))) for d in range(4)]
    asked = jnp.concatenate([r[0:1] for r in exchange(requests, SIDES, 0)], axis=0)
    pick = jnp.where(side < 4, tiles + cell, old_slot)

    state = (jitter, displacement, modulus, start_vec)
    handed = pl.pallas_call(
        hand_kernel,
        out_shape=[jax.ShapeDtypeStruct((CAP, 16, points), F32)] * 4,
        in_specs=[SMEM] + [VMEM] * 4,
        out_specs=[VMEM] * 4,
        compiler_params=LIMIT,
    )(asked, *state)
    arrived = exchange(handed, SIDES, 1)
    ghost_shape = jax.ShapeDtypeStruct((cap, 16, points), F32)
    local, *sends = pl.pallas_call(
        settle_kernel,
        out_shape=[jax.ShapeDtypeStruct((tiles, 16, points), F32)] + [ghost_shape] * 8,
        in_specs=[SMEM] * 2 + [VMEM] * 8,
        out_specs=[VMEM] * 9,
        scratch_shapes=[pltpu.VMEM((tiles + 4 * CAP, 16, points), F32)],
        compiler_params=LIMIT,
    )(pick, ghost_send[0], *state, *arrived)
    ghosts = exchange(sends, AROUND, 2)
    order, bounds, owner = plan(pair_list[0], pair_count[0])
    slots = order.shape[0]
    chunks = slots // CHUNK
    scratch = [
        pltpu.VMEM(((tiles + 9 * cap) * 16, points), F32),
        pltpu.VMEM((chunks, FIELDS * CHUNK, points), F32),
        pltpu.VMEM((chunks, FIELDS * CHUNK, points), F32),
        pltpu.VMEM((chunks, 16 * CHUNK, points), jnp.int32),
        pltpu.VMEM((3, slots, points), F32),
    ]
    image_shape = jax.ShapeDtypeStruct((3, tiles, points), F32)
    sel0, bits0 = self_tables()
    sel1, back1, tab1 = face_tables()
    sel2, back2, tab2 = corner_tables()
    half = lambda t: jnp.asarray(t, BF16)
    tables = (half(sel0), jnp.asarray(bits0), half(sel1), half(back1), jnp.asarray(tab1), half(sel2), half(back2), jnp.asarray(tab2))
    head = (pair_list[0], order, bounds, ghost_send[0], owner, *tables, broken, local, *ghosts)
    first_image, *image_sends = pl.pallas_call(
        functools.partial(apply_kernel, True),
        out_shape=[image_shape] + [jax.ShapeDtypeStruct((3, cap, points), F32)] * 8,
        in_specs=[SMEM] * 4 + [VMEM] * 19,
        out_specs=[VMEM] * 9,
        scratch_shapes=scratch,
        compiler_params=LIMIT,
    )(*head)
    image_ghosts = exchange(image_sends, AROUND, 3)
    second_image = pl.pallas_call(
        functools.partial(apply_kernel, False),
        out_shape=image_shape,
        in_specs=[SMEM] * 4 + [VMEM] * 28,
        out_specs=VMEM,
        scratch_shapes=scratch,
        compiler_params=LIMIT,
    )(*head, first_image, *image_ghosts)
    return tuple(jnp.transpose(image, (1, 0, 2)) for image in (first_image, second_image))


def solution(mesh):
    split = ("gx", "gy")
    spec3, spec2, spec1 = P(split, None, None), P(split, None), P(split)
    return jax.shard_map(
        on_device,
        mesh=mesh,
        in_specs=(spec3, spec3, spec2, spec3, spec1, spec3, spec3, spec1, spec3),
        out_specs=(spec3, spec3),
        check_vma=False,
    )
```

```python
import functools
import jax
import jax.numpy as jnp
import numpy as np
from jax import lax
from jax.experimental import pallas as pl
from jax.experimental.pallas import tpu as pltpu
from jax.sharding import PartitionSpec as P

CAP = 16
F32 = jnp.float32
BF16 = jnp.bfloat16
VMEM = pl.BlockSpec(memory_space=pltpu.VMEM)
SMEM = pl.BlockSpec(memory_space=pltpu.SMEM)
LIMIT = pltpu.CompilerParams(vmem_limit_bytes=48 * 1024 * 1024)
DIRS = (0, 1, 2, 3, 5, 6, 7, 8)
SIDES = ((-1, 0), (1, 0), (0, -1), (0, 1))
AROUND = tuple((e // 3 - 1, e % 3 - 1) for e in DIRS)
CLASSES = 9
FIELDS = 10
CHUNK = 16
LANES = 128
FACE_WIDTH = 2
CORNER_WIDTH = 4


def near(dx, dy):
    return max(abs(dx) - 0.4, 0.0) ** 2 + max(abs(dy) - 0.4, 0.0) ** 2 < 9.0


def point(x, y, z):
    return x + 8 * y + 64 * z


HALF = [(dx, dy) for dy in range(4) for dx in range(-3, 4) if (dy > 0 or dx > 0) and near(dx, dy)]
OFFSETS = [(0, 0, 1)] + [(dx, dy, f) for dx, dy in HALF for f in (0, 1)]


def self_tables():
    sel = np.zeros((2 * LANES, len(OFFSETS) * LANES), np.float32)
    bits = np.zeros((-(-2 * len(OFFSETS) // 8) * 8, LANES), np.int32)
    for n, (dx, dy, f) in enumerate(OFFSETS):
        for lane in range(LANES):
            x, y, z = lane % 8, lane // 8 % 8, lane // 64
            if 0 <= x + dx < 8 and 0 <= y + dy < 8:
                for half in (0, LANES):
                    sel[half + point(x + dx, y + dy, z ^ f), n * LANES + lane] += 1
                    sel[half + lane, n * LANES + lane] -= 1
                bits[2 * n, lane] = 1 << (x + dx + 8 * (z ^ f))
            if 0 <= x - dx < 8 and 0 <= y - dy < 8:
                bits[2 * n + 1, lane] = 1 << (x - dx + 8 * (z ^ f))
    return sel, bits


OFFSET_LANES = (27, 28, 35)
NEAR = [(7, 0), (7, 1), (6, 0), (7, 2), (6, 1), (5, 0)]
FAR = [(7, 0, 2), (7, 1, 2), (6, 0, 2), (7, 0, 3), (7, 0, -2), (7, 1, -2), (6, 0, -2), (7, 0, -3)]


def fill(sel, col, a, b, shift):
    for half in (0, LANES):
        sel[half + point(*b), col] += 1
        sel[half + point(*a), col] -= 1
        for c in range(3):
            sel[half + OFFSET_LANES[c], col] = b[c] - a[c] + shift[c]


def face_tables():
    sels = np.zeros((4, 2 * LANES, 8 * LANES), np.float32)
    backs = np.zeros((4, 2 * LANES, LANES), np.float32)
    tabs = np.zeros((4, 16, LANES), np.int32)
    for k in range(4):
        axis, sign = k // 2, 1 - 2 * (k % 2)
        side = lambda u: u if sign > 0 else 7 - u
        place = lambda u, t, z: (u, t, z) if axis == 0 else (t, u, z)
        shift = place(8 * sign, 0, 0)
        sel, back, tab = sels[k], backs[k], tabs[k]
        for z in range(2):
            for t in range(8):
                for c in range(8):
                    lane = point(*place(c, t, z))
                    ua, ub, dt = FAR[c]
                    a = place(side(ua), t, z)
                    tab[9, lane] = point(*a)
                    tab[12, lane] = ub
                    tab[13, lane] = dt
                    back[LANES + lane, point(*a)] = 1
                    todo = [(6 + f, f, a, ub, dt) for f in range(2)]
                    if c < len(NEAR):
                        ua, ub = NEAR[c]
                        a = place(side(ua), t, z)
                        tab[8, lane] = point(*a)
                        tab[11, lane] = ub
                        back[lane, point(*a)] = 1
                        todo += [(2 * m + f, f, a, ub, m - 1) for m in range(3) for f in range(2)]
                    for v, f, a, ub, dt in todo:
                        if 0 <= t + dt < 8:
                            b = place(side(ub), t + dt, z ^ f)
                            fill(sel, v * LANES + lane, a, b, shift)
                            tab[v, lane] = 1 << (b[0] + 8 * b[2])
                for u in range(3):
                    tab[10, point(*place(side(7 - u), t, z))] = 1
                    tab[10, point(*place(side(u), t, z))] = 2
        for col in range(8 * LANES):
            if not sel[:, col].any():
                sel[OFFSET_LANES[0], col] = 4
    return sels, backs, tabs


def corner_tables():
    sels = np.zeros((4, 2 * LANES, LANES), np.float32)
    backs = np.zeros((4, 2 * LANES, LANES), np.float32)
    tabs = np.zeros((4, 8, LANES), np.int32)
    combos = []
    for (ua, ub) in NEAR:
        for (va, vb) in NEAR:
            if near(ub + 8 - ua, vb + 8 - va):
                combos.append((ua, va, ub, vb))
    for k in range(4):
        sign_x, sign_y = 1 - 2 * (k // 2), 1 - 2 * (k % 2)
        side_x = lambda u: u if sign_x > 0 else 7 - u
        side_y = lambda u: u if sign_y > 0 else 7 - u
        sel, back, tab = sels[k], backs[k], tabs[k]
        for n, (ua, va, ub, vb) in enumerate(combos):
            for z in range(2):
                for f in range(2):
                    lane = n + 16 * z + 32 * f
                    a, b = (side_x(ua), side_y(va), z), (side_x(ub), side_y(vb), z ^ f)
                    fill(sel, lane, a, b, (8 * sign_x, 8 * sign_y, 0))
                    back[lane, point(*a)] = 1
                    back[LANES + lane, point(*a)] = 1
                    tab[0, lane] = 1 << (b[0] + 8 * b[2])
                    tab[1, lane] = point(*a)
                    tab[3, lane] = vb
        for col in range(LANES):
            if not sel[:, col].any():
                sel[OFFSET_LANES[0], col] = 4
        for z in range(2):
            for u in range(3):
                for v in range(3):
                    tab[2, point(side_x(7 - u), side_y(7 - v), z)] = 1
                    tab[2, point(side_x(u), side_y(v), z)] = 2
    return sels, backs, tabs


def split(value):
    high = value.astype(BF16)
    return high, (value - high.astype(F32)).astype(BF16)


def bond_force(xi, y, moduli, dv, keep):
    r2 = xi[0] * xi[0] + xi[1] * xi[1] + xi[2] * xi[2]
    l2 = y[0] * y[0] + y[1] * y[1] + y[2] * y[2]
    c = moduli * jnp.maximum(9.0 - r2, 0.0)
    if keep is not None:
        c = jnp.where(keep, c, 0.0)
    r_inv = lax.rsqrt(r2)
    l_inv = lax.rsqrt(l2)
    cl = c * l_inv
    k2 = c * r_inv - cl
    along = cl * (l_inv * l_inv) * (y[0] * dv[0] + y[1] * dv[1] + y[2] * dv[2])
    return [k2 * dv[i] + along * y[i] for i in range(3)]


def gather_kernel(
    jit, disp, mod, vec, wanted, source, shape_full, moved_full, state, own, asked, hand, arrived, ghost, landed, sent, got
):
    n_x, n_y = lax.axis_size("gx"), lax.axis_size("gy")
    x, y = lax.axis_index("gx"), lax.axis_index("gy")
    tiles, points = mod.shape
    cap = landed.shape[2]

    def exists(offset):
        ox, oy = offset
        return (x + ox >= 0) & (x + ox < n_x) & (y + oy >= 0) & (y + oy < n_y)

    barrier = pltpu.get_barrier_semaphore()
    for offset in AROUND:

        @pl.when(exists(offset))
        def _():
            pl.semaphore_signal(
                barrier, inc=1, device_id=(x + offset[0], y + offset[1]), device_id_type=pl.DeviceIdType.MESH
            )

    pl.semaphore_wait(barrier, sum(jnp.where(exists(offset), 1, 0) for offset in AROUND))

    def copy(offsets, base, source_ref, target_ref, d):
        ox, oy = offsets[d]
        back = offsets.index((-ox, -oy))
        return pltpu.make_async_remote_copy(
            src_ref=source_ref.at[d],
            dst_ref=target_ref.at[back],
            send_sem=sent.at[base + d],
            recv_sem=got.at[base + back],
            device_id=(x + ox, y + oy),
            device_id_type=pl.DeviceIdType.MESH,
        )

    def start(*args):
        for d, offset in enumerate(args[0]):

            @pl.when(exists(offset))
            def _():
                copy(*args, d).start()

    def finish(*args):
        for d, (ox, oy) in enumerate(args[0]):

            @pl.when(exists((ox, oy)))
            def _():
                copy(*args, d).wait_send()
                copy(*args, args[0].index((-ox, -oy))).wait_recv()

    asking = (SIDES, 0, wanted, asked)
    handing = (SIDES, 4, hand, arrived)
    ghosting = (AROUND, 8, ghost, landed)
    start(*asking)
    for offsets, refs in ((SIDES, (asked, arrived)), (AROUND, (landed,))):
        for d, offset in enumerate(offsets):

            @pl.when(jnp.logical_not(exists(offset)))
            def _():
                for ref in refs:
                    ref[d] = jnp.zeros_like(ref[d])

    for c in range(FIELDS):
        if c < 3:
            value = jit[c]
        elif c < 6:
            value = jit[c - 3] + disp[c - 3]
        elif c == 6:
            value = mod[...] * (0.05 / 9.0)
        else:
            value = vec[c - 7]
        high, low = split(value)
        state[0:tiles, c * points : (c + 1) * points] = high
        state[tiles : 2 * tiles, c * points : (c + 1) * points] = low

    def hot(index, base, width):
        ids = lax.broadcasted_iota(jnp.int32, index.shape, 1) % width + base
        return jnp.where(index == ids, 1.0, 0.0).astype(BF16)

    def twice(value):
        return jnp.concatenate([value, value], axis=1)

    finish(*asking)
    left = twice(jnp.concatenate([hot(asked[d], 0, tiles) for d in range(4)], axis=0))
    for p in range(FIELDS // 2):
        out = jnp.dot(left, state[:, 2 * p * points : 2 * (p + 1) * points], preferred_element_type=F32)
        for f in range(2):
            for d in range(4):
                hand[d, 2 * p + f] = out[d * CAP : (d + 1) * CAP, f * points : (f + 1) * points]
    start(*handing)
    left = twice(hot(source[...], 0, tiles))
    for p in range(FIELDS // 2):
        at = slice(2 * p * points, 2 * (p + 1) * points)
        own[:, at] = jnp.dot(left, state[:, at], preferred_element_type=F32)
    finish(*handing)
    left = hot(source[...], tiles, 4 * CAP)
    right = []
    for c in range(FIELDS):
        right.append(jnp.concatenate(split(jnp.concatenate([arrived[d, c] for d in range(4)], axis=0)), axis=0))

    def settled(low_row, p):
        rows = slice(low_row, low_row + tiles)
        both = jnp.concatenate([right[2 * p], right[2 * p + 1]], axis=1)
        return own[rows, 2 * p * points : 2 * (p + 1) * points] + jnp.dot(left[rows], both, preferred_element_type=F32)

    for p in range(FIELDS // 2):
        out = settled(tiles, p)
        for f in range(2):
            for n in range(8):
                ghost[n, 2 * p + f] = out[n * cap : (n + 1) * cap, f * points : (f + 1) * points]
    start(*ghosting)

    def spread(row, c, value):
        target = shape_full if c < 7 else moved_full
        for j in range(0, value.shape[0], 8):
            target[pl.ds((row + j) * 8 + c % 7, 8, stride=8)] = value[j : j + 8]

    for p in range(FIELDS // 2):
        out = settled(0, p)
        for f in range(2):
            spread(0, 2 * p + f, out[:, f * points : (f + 1) * points])
    finish(*ghosting)
    for n, e in enumerate(DIRS):
        for c in range(FIELDS):
            spread(tiles + e * cap, c, landed[n, c])


def apply_kernel(first, pairs, order, bounds, owner, target, sel0, bits0, sel1, back1, tab1, sel2, back2, tab2, code, *rest):
    if first:
        words, shape_full, moved_full, image, sends, shape, flags, moved, force = *rest[:4], rest[4:12], *rest[12:]
    else:
        field, field_ghosts, shape, flags, image, moved_full, moved, force = rest[0], rest[1:9], *rest[9:]
    _, rows, points = image.shape
    if first:
        cap = sends[0].shape[1]
    else:
        cap = field_ghosts[0].shape[1]
        for c in range(3):
            for j in range(0, rows, 8):
                moved_full[pl.ds(j * 8 + c, 8, stride=8)] = field[c, j : j + 8]
            for e, ghost in zip(DIRS, field_ghosts):
                for j in range(0, cap, 8):
                    moved_full[pl.ds((rows + e * cap + j) * 8 + c, 8, stride=8)] = ghost[c, j : j + 8]

    lane = lax.broadcasted_iota(jnp.int32, (8, points), 1)
    sub = lax.broadcasted_iota(jnp.int32, (8, points), 0)
    lane_y = lane // 8 % 8
    low_z = lane < 64
    unit = jnp.zeros((8, points), F32)
    for c in range(6):
        unit = jnp.where((sub == c) & (lane == OFFSET_LANES[c % 3]), 1.0, unit)
    turn = jnp.where(sub == 6, -1.0, 1.0)

    def tile_of(row, ref):
        return ref[pl.ds(pl.multiple_of(row * 8, 8), 8)]

    def build(shifted, g, carry):
        if shifted:
            k = sum(jnp.where(g >= bounds[c], 1, 0) for c in range(2, 9))
            held = jnp.broadcast_to(code[pl.ds(k, 1)], (8, points))
            take_a, take_b = held == 1, held == 2
        for u in range(CHUNK):
            q = jnp.maximum(order[g * CHUNK + u], 0)
            tile, partner = pairs[0, q], pairs[1, q]
            if first:
                state = tile_of(tile, shape_full)
                if shifted:
                    state = jnp.where(take_a, state * turn, jnp.where(take_b, tile_of(partner, shape_full), unit))
                shape[g, pl.ds(u, 8, stride=CHUNK)] = state
                word = jnp.bitwise_not(words[q, 0:8] | jnp.left_shift(words[q, 8:16], 8))
                flags[g, pl.ds(u, 8, stride=CHUNK)] = word
            state = tile_of(tile, moved_full)
            if shifted:
                state = jnp.where(take_a, state, jnp.where(take_b, tile_of(partner, moved_full), 0.0))
            moved[g, pl.ds(u, 3, stride=CHUNK)] = state[0:3]
        return carry

    lax.fori_loop(bounds[0], bounds[1], functools.partial(build, False), 0)
    lax.fori_loop(bounds[1], bounds[9], functools.partial(build, True), 0)

    def row_of(ref, *at):
        return jnp.broadcast_to(ref[at], (8, points))

    def pick(value, index):
        return jnp.take_along_axis(value, index, axis=1, mode="promise_in_bounds")

    def word_of(g, h, y):
        start = y * CHUNK + 8 * h
        if not isinstance(start, int):
            start = pl.multiple_of(start, 8)
        return flags[g, pl.ds(start, 8)]

    def by_row(g, h):
        held = [word_of(g, h, y) for y in range(8)]
        for bit in (1, 2, 4):
            odd = (lane_y & bit) != 0
            held = [jnp.where(odd, held[(s + bit) % 8], held[s]) for s in range(8)]
        return held

    def left_side(g):
        values = [shape[g, c * CHUNK : (c + 1) * CHUNK] for c in range(7)]
        values += [moved[g, c * CHUNK : (c + 1) * CHUNK] for c in range(3)]
        parts = [split(v) for v in values]
        high = jnp.concatenate([p[0] for p in parts], axis=0)
        low = jnp.concatenate([p[1] for p in parts], axis=0)
        return jnp.concatenate([high, low], axis=1)

    def block(wide, c, h, v):
        return wide[c * CHUNK + 8 * h : c * CHUNK + 8 * h + 8, v * points : (v + 1) * points]

    def put(g, c, value):
        force[c, pl.ds(pl.multiple_of(g * CHUNK, CHUNK), CHUNK)] = value

    def same_tile(g, carry):
        left = left_side(g)
        words_of = [by_row(g, h) for h in range(2)]
        twice = [2.0 * shape[g, 6 * CHUNK + 8 * h : 6 * CHUNK + 8 * h + 8] for h in range(2)]
        acc = [[jnp.zeros((8, points), F32)] * 3 for _ in range(2)]
        other = jnp.where(low_z, 1.0, -1.0)
        for start in range(0, len(OFFSETS), 2):
            some = OFFSETS[start : start + 2]
            wide = jnp.dot(left, sel0[:, start * points : (start + len(some)) * points], preferred_element_type=F32)
            for v, (dx, dy, f) in enumerate(some):
                n = start + v
                base = (float(dx), float(dy), other if f else 0.0)
                for h in range(2):
                    part = lambda c: block(wide, c, h, v)
                    xi = [part(c) + base[c] for c in range(3)]
                    y = [part(3 + c) + base[c] for c in range(3)]
                    dv = [part(7 + c) for c in range(3)]
                    term = bond_force(xi, y, part(6) + twice[h], dv, None)
                    keep = (words_of[h][dy % 8] & row_of(bits0, pl.ds(2 * n, 1))) != 0
                    acc[h] = [acc[h][i] + jnp.where(keep, term[i], 0.0) for i in range(3)]
                    if (dx, dy) != (0, 0):
                        keep = (words_of[h][-dy % 8] & row_of(bits0, pl.ds(2 * n + 1, 1))) != 0
                        off = (dx + 8 * dy + 64 * f) % points
                        acc[h] = [acc[h][i] - jnp.where(keep, pltpu.roll(term[i], off, 1), 0.0) for i in range(3)]
        for c in range(3):
            put(g, c, jnp.concatenate([acc[0][c], acc[1][c]], axis=0))
        return carry

    lax.fori_loop(bounds[0], bounds[1], same_tile, 0)

    def of_block(wide, h, v, keep):
        part = lambda c: block(wide, c, h, v)
        xi = [part(c) for c in range(3)]
        y = [part(3 + c) for c in range(3)]
        dv = [part(7 + c) for c in range(3)]
        return bond_force(xi, y, part(6), dv, keep)

    def face(axis, g):
        k = 2 * axis + jnp.where(g >= bounds[2 * axis + 2], 1, 0)
        left = left_side(g)
        index_near = row_of(tab1, k, pl.ds(8, 1))
        index_far = row_of(tab1, k, pl.ds(9, 1))
        close = [[jnp.zeros((8, points), F32)] * 3 for _ in range(2)]
        distant = [[jnp.zeros((8, points), F32)] * 3 for _ in range(2)]
        near_words, far_words = [], []
        for h in range(2):
            if axis == 0:
                rel = by_row(g, h)
                dt = row_of(tab1, k, pl.ds(13, 1))
                near_words.append([pick(rel[(m - 1) % 8], index_near) for m in range(3)])
                chosen = pick(rel[2], index_far)
                for d in (3, -2, -3):
                    chosen = jnp.where(dt == d, pick(rel[d % 8], index_far), chosen)
                far_words.append(chosen)
            else:
                for at, index, into in ((11, index_near, near_words), (12, index_far, far_words)):
                    row = row_of(tab1, k, pl.ds(at, 1))
                    chosen = None
                    for j in range(3):
                        word = pick(word_of(g, h, jnp.where(k == 3, 7 - j, j)), index)
                        chosen = word if j == 0 else jnp.where(row == j, word, chosen)
                    into.append([chosen] * 3 if at == 11 else chosen)
        for m in range(4):
            wide = jnp.dot(left, sel1[k, :, 2 * m * points : 2 * (m + 1) * points], preferred_element_type=F32)
            for f in range(2):
                for h in range(2):
                    word = near_words[h][m] if m < 3 else far_words[h]
                    keep = (word & row_of(tab1, k, pl.ds(2 * m + f, 1))) != 0
                    term = of_block(wide, h, f, keep)
                    acc = close if m < 3 else distant
                    acc[h] = [acc[h][i] + term[i] for i in range(3)]
        total = []
        for acc in (close, distant):
            stacked = jnp.concatenate([acc[h][c] for c in range(3) for h in range(2)], axis=0)
            high, low = split(stacked)
            total.append(jnp.concatenate([high, low], axis=0))
        back = jnp.dot(jnp.concatenate(total, axis=1), back1[k], preferred_element_type=F32)
        for c in range(3):
            at = c * CHUNK
            put(g, c, back[at : at + CHUNK] + back[3 * CHUNK + at : 3 * CHUNK + at + CHUNK])

    def corner(g):
        k = sum(jnp.where(g >= bounds[c], 1, 0) for c in (6, 7, 8))
        left = left_side(g)
        index = row_of(tab2, k, pl.ds(1, 1))
        row = row_of(tab2, k, pl.ds(3, 1))
        wide = jnp.dot(left, sel2[k], preferred_element_type=F32)
        terms = []
        for h in range(2):
            chosen = None
            for j in range(3):
                word = pick(word_of(g, h, jnp.where((k & 1) == 1, 7 - j, j)), index)
                chosen = word if j == 0 else jnp.where(row == j, word, chosen)
            keep = (chosen & row_of(tab2, k, pl.ds(0, 1))) != 0
            terms.append(of_block(wide, h, 0, keep))
        stacked = jnp.concatenate([terms[h][c] for c in range(3) for h in range(2)], axis=0)
        back = jnp.dot(jnp.concatenate(split(stacked), axis=1), back2[k], preferred_element_type=F32)
        for c in range(3):
            put(g, c, back[c * CHUNK : (c + 1) * CHUNK])

    def over(low, high, width, body):
        def step(i, carry):
            for u in range(width):
                body(jnp.minimum(low + i * width + u, high - 1))
            return carry

        lax.fori_loop(0, (high - low + width - 1) // width, step, 0)

    over(bounds[1], bounds[3], FACE_WIDTH, functools.partial(face, 0))
    over(bounds[3], bounds[5], FACE_WIDTH, functools.partial(face, 1))
    over(bounds[5], bounds[9], CORNER_WIDTH, corner)

    blocks = (bounds[9] * CHUNK + LANES - 1) // LANES

    def clear(g, carry):
        for c in range(3):
            put(g, c, jnp.zeros((CHUNK, points), F32))
        return carry

    lax.fori_loop(bounds[9], blocks * (LANES // CHUNK), clear, 0)
    image[...] = jnp.zeros_like(image)
    if first:
        for out in sends:
            out[...] = jnp.zeros_like(out)
    tile_at = lax.broadcasted_iota(jnp.int32, (rows, LANES), 0)
    if first:
        tile_at = jnp.concatenate([tile_at, target[...]], axis=0)

    def gather_tiles(b, carry):
        hot = jnp.where(tile_at == owner[pl.ds(b, 1)], 1.0, 0.0).astype(BF16)
        parts = [split(force[c, pl.ds(pl.multiple_of(b * LANES, LANES), LANES)]) for c in range(3)]
        high = jnp.concatenate([p[0] for p in parts], axis=1)
        low = jnp.concatenate([p[1] for p in parts], axis=1)
        out = jnp.dot(
            jnp.concatenate([hot, hot], axis=1), jnp.concatenate([high, low], axis=0), preferred_element_type=F32
        )
        for c in range(3):
            image[c] += out[:rows, c * points : (c + 1) * points]
            if first:
                for n, send in enumerate(sends):
                    send[c] += out[rows + n * cap : rows + (n + 1) * cap, c * points : (c + 1) * points]
        return carry

    lax.fori_loop(0, blocks, gather_tiles, 0)


def exchange_kernel(offsets, *refs):
    n = len(offsets)
    ins, outs, send_sem, recv_sem = refs[:n], refs[n : 2 * n], refs[2 * n], refs[2 * n + 1]
    n_x, n_y = lax.axis_size("gx"), lax.axis_size("gy")
    x, y = lax.axis_index("gx"), lax.axis_index("gy")

    def exists(ox, oy):
        return (x + ox >= 0) & (x + ox < n_x) & (y + oy >= 0) & (y + oy < n_y)

    barrier = pltpu.get_barrier_semaphore()
    for ox, oy in offsets:

        @pl.when(exists(ox, oy))
        def _():
            pl.semaphore_signal(
                barrier, inc=1, device_id=(x + ox, y + oy), device_id_type=pl.DeviceIdType.MESH
            )

    peers = sum(jnp.where(exists(ox, oy), 1, 0) for ox, oy in offsets)
    pl.semaphore_wait(barrier, peers)

    def copy(d):
        ox, oy = offsets[d]
        back = offsets.index((-ox, -oy))
        return pltpu.make_async_remote_copy(
            src_ref=ins[d],
            dst_ref=outs[back],
            send_sem=send_sem.at[d],
            recv_sem=recv_sem.at[back],
            device_id=(x + ox, y + oy),
            device_id_type=pl.DeviceIdType.MESH,
        )

    for d, (ox, oy) in enumerate(offsets):

        @pl.when(exists(ox, oy))
        def _():
            copy(d).start()

        @pl.when(jnp.logical_not(exists(ox, oy)))
        def _():
            outs[d][...] = jnp.zeros_like(outs[d])

    for d, (ox, oy) in enumerate(offsets):

        @pl.when(exists(ox, oy))
        def _():
            copy(d).wait_send()
            copy(offsets.index((-ox, -oy))).wait_recv()


def exchange(blocks, offsets, ident):
    n = len(offsets)
    return pl.pallas_call(
        functools.partial(exchange_kernel, offsets),
        out_shape=[jax.ShapeDtypeStruct(b.shape, b.dtype) for b in blocks],
        in_specs=[VMEM] * n,
        out_specs=[VMEM] * n,
        scratch_shapes=[pltpu.SemaphoreType.DMA((n,)), pltpu.SemaphoreType.DMA((n,))],
        compiler_params=pltpu.CompilerParams(
            collective_id=ident, has_side_effects=True, vmem_limit_bytes=4 * 1024 * 1024
        ),
    )(*blocks)


def plan(pair_list, count):
    pairs = pair_list.shape[1]
    slots = -(-(pairs + CLASSES * (CHUNK - 1)) // LANES) * LANES
    slot = jnp.arange(pairs, dtype=jnp.int32)
    sx, sy = pair_list[2], pair_list[3]
    flat_x = jnp.where(sx > 0, 1, 2)
    flat_y = jnp.where(sy > 0, 3, 4)
    slant = 5 + 2 * (sx < 0) + (sy < 0)
    kind = jnp.where(sx == 0, jnp.where(sy == 0, 0, flat_y), jnp.where(sy == 0, flat_x, slant))
    kind = jnp.where(slot < count, kind, 15).astype(jnp.int32)
    ids = jnp.arange(16, dtype=jnp.int32)
    earlier = (kind[:, None] == kind[None, :]) & (slot[:, None] < slot[None, :])
    rank = jnp.sum(earlier.astype(jnp.int32), axis=0)
    before = (kind[:, None] < ids[None, :]) & (ids[None, :] < 15)
    member = kind[:, None] == ids[None, :]
    chunks = (jnp.sum(member.astype(jnp.int32), axis=0) + CHUNK - 1) // CHUNK
    start = jnp.sum(jnp.where(ids[:, None] < ids[None, :], chunks[:, None], 0), axis=0)
    place = rank + CHUNK * jnp.sum(jnp.where(member, start[None, :], 0), axis=1)
    place = jnp.where(kind < CLASSES, place, -1)
    hit = place[:, None] == jnp.arange(slots, dtype=jnp.int32)[None, :]
    order = jnp.sum(jnp.where(hit, slot[:, None] + 1, 0), axis=0) - 1
    owner = jnp.sum(jnp.where(hit, pair_list[0][:, None] + 1, 0), axis=0) - 1
    return order, start, owner.reshape(slots // LANES, LANES)


def tangents(pairs, order, bounds, owner, send, broken, shape_full, moved_full, swap):
    cap, points = send.shape[1], broken.shape[2]
    tiles = shape_full.shape[0] // 8 - 9 * cap
    slots = order.shape[0]
    chunks = slots // CHUNK
    sel0, bits0 = self_tables()
    sel1, back1, tab1 = face_tables()
    sel2, back2, tab2 = corner_tables()
    code = np.concatenate([tab1[:, 10], tab2[:, 2]], axis=0)
    half = lambda t: jnp.asarray(t, BF16)
    tables = (half(sel0), jnp.asarray(bits0), half(sel1), half(back1), jnp.asarray(tab1))
    tables += (half(sel2), half(back2), jnp.asarray(tab2), jnp.asarray(code))
    target = jnp.broadcast_to(send.reshape(-1)[:, None], (send.size, LANES))
    head = (pairs, order, bounds, owner, target, *tables)
    image_shape = jax.ShapeDtypeStruct((3, tiles, points), F32)
    kept = [
        jax.ShapeDtypeStruct((chunks, 8 * CHUNK, points), F32),
        jax.ShapeDtypeStruct((chunks, 8 * CHUNK, points), jnp.int32),
    ]
    scratch = [
        pltpu.VMEM((chunks, 3 * CHUNK, points), F32),
        pltpu.VMEM((3, slots, points), F32),
    ]
    limit = pltpu.CompilerParams(vmem_limit_bytes=16 * 1024 * 1024)
    first_image, *rest = pl.pallas_call(
        functools.partial(apply_kernel, True),
        out_shape=[image_shape] + [jax.ShapeDtypeStruct((3, cap, points), F32)] * 8 + kept,
        in_specs=[SMEM] * 3 + [VMEM] * 14,
        out_specs=[VMEM] * 11,
        scratch_shapes=scratch,
        compiler_params=limit,
    )(*head, broken, shape_full, moved_full)
    image_sends, kept = rest[:8], rest[8:]
    image_ghosts = swap(image_sends)
    second_image = pl.pallas_call(
        functools.partial(apply_kernel, False),
        out_shape=image_shape,
        in_specs=[SMEM] * 3 + [VMEM] * 22,
        out_specs=VMEM,
        scratch_shapes=[pltpu.VMEM(moved_full.shape, F32)] + scratch,
        compiler_params=limit,
    )(*head, first_image, *image_ghosts, *kept)
    return first_image, second_image


def on_device(jitter, displacement, modulus, start_vec, old_home, ghost_send, pair_list, pair_count, broken):
    tiles = old_home.shape[0]
    points = jitter.shape[2]
    cap = ghost_send.shape[2]
    width_y = lax.axis_size("gy")
    anchor = old_home // tiles
    old_slot = old_home % tiles
    off_x = anchor // width_y - lax.axis_index("gx")
    off_y = anchor % width_y - lax.axis_index("gy")
    side = jnp.where(off_x == -1, 0, jnp.where(off_x == 1, 1, jnp.where(off_y == -1, 2, jnp.where(off_y == 1, 3, 4))))
    index = jnp.arange(tiles, dtype=jnp.int32)
    earlier = (side[:, None] == side[None, :]) & (index[:, None] < index[None, :])
    ranked = jnp.sum(earlier.astype(jnp.int32), axis=0)
    cell = jnp.where(side < 4, side * CAP + ranked, -1)
    hit = cell[:, None] == jnp.arange(4 * CAP, dtype=jnp.int32)[None, :]
    wanted = jnp.sum(jnp.where(hit, old_slot[:, None], 0), axis=0)
    wanted = jnp.broadcast_to(wanted.reshape(4, CAP)[:, :, None], (4, CAP, LANES))
    pick = jnp.where(side < 4, tiles + cell, old_slot)
    send = jnp.maximum(jnp.concatenate([ghost_send[0, :4], ghost_send[0, 5:]], axis=0), 0)
    sent = send.reshape(-1)
    sent_pick = jnp.sum(jnp.where(sent[:, None] == index[None, :], pick[None, :], 0), axis=1)
    source = jnp.broadcast_to(jnp.concatenate([pick, sent_pick])[:, None], (tiles + sent.shape[0], LANES))
    turned = lambda value: jnp.transpose(value, (1, 0, 2))
    rows = tiles + 9 * cap
    full = jax.ShapeDtypeStruct((rows * 8, points), F32)
    shape_full, moved_full = pl.pallas_call(
        gather_kernel,
        out_shape=[full, full],
        in_specs=[VMEM] * 6,
        out_specs=[VMEM] * 2,
        scratch_shapes=[
            pltpu.VMEM((2 * tiles, FIELDS * points), BF16),
            pltpu.VMEM((tiles + 8 * cap, FIELDS * points), F32),
            pltpu.VMEM((4, CAP, LANES), jnp.int32),
            pltpu.VMEM((4, FIELDS, CAP, points), F32),
            pltpu.VMEM((4, FIELDS, CAP, points), F32),
            pltpu.VMEM((8, FIELDS, cap, points), F32),
            pltpu.VMEM((8, FIELDS, cap, points), F32),
            pltpu.SemaphoreType.DMA((16,)),
            pltpu.SemaphoreType.DMA((16,)),
        ],
        compiler_params=pltpu.CompilerParams(
            collective_id=0, has_side_effects=True, vmem_limit_bytes=16 * 1024 * 1024
        ),
    )(turned(jitter), turned(displacement), modulus, turned(start_vec), wanted, source)
    order, bounds, owner = plan(pair_list[0], pair_count[0])
    first_image, second_image = tangents(
        pair_list[0], order, bounds, owner, send, broken, shape_full, moved_full, lambda sends: exchange(sends, AROUND, 1)
    )
    return turned(first_image), turned(second_image)


def solution(mesh):
    split = ("gx", "gy")
    spec3, spec2, spec1 = P(split, None, None), P(split, None), P(split)
    return jax.shard_map(
        on_device,
        mesh=mesh,
        in_specs=(spec3, spec3, spec2, spec3, spec1, spec3, spec3, spec1, spec3),
        out_specs=(spec3, spec3),
        check_vma=False,
    )
```

```python
import functools
import jax
import jax.numpy as jnp
import numpy as np
from jax import lax
from jax.experimental import pallas as pl
from jax.experimental.pallas import tpu as pltpu
from jax.sharding import PartitionSpec as P

CAP = 16
F32 = jnp.float32
BF16 = jnp.bfloat16
VMEM = pl.BlockSpec(memory_space=pltpu.VMEM)
SMEM = pl.BlockSpec(memory_space=pltpu.SMEM)
HBM = pl.BlockSpec(memory_space=pltpu.HBM)
DIRS = (0, 1, 2, 3, 5, 6, 7, 8)
SIDES = ((-1, 0), (1, 0), (0, -1), (0, 1))
AROUND = tuple((e // 3 - 1, e % 3 - 1) for e in DIRS)
CLASSES = 9
FIELDS = 10
CHUNK = 16
LANES = 128
FACE_WIDTH = 2
CORNER_WIDTH = 4


def near(dx, dy):
    return max(abs(dx) - 0.4, 0.0) ** 2 + max(abs(dy) - 0.4, 0.0) ** 2 < 9.0


def point(x, y, z):
    return x + 8 * y + 64 * z


HALF = [(dx, dy) for dy in range(4) for dx in range(-3, 4) if (dy > 0 or dx > 0) and near(dx, dy)]
OFFSETS = [(0, 0, 1)] + [(dx, dy, f) for dx, dy in HALF for f in (0, 1)]


def self_tables():
    sel = np.zeros((2 * LANES, len(OFFSETS) * LANES), np.float32)
    bits = np.zeros((-(-2 * len(OFFSETS) // 8) * 8, LANES), np.int32)
    for n, (dx, dy, f) in enumerate(OFFSETS):
        for lane in range(LANES):
            x, y, z = lane % 8, lane // 8 % 8, lane // 64
            if 0 <= x + dx < 8 and 0 <= y + dy < 8:
                for half in (0, LANES):
                    sel[half + point(x + dx, y + dy, z ^ f), n * LANES + lane] += 1
                    sel[half + lane, n * LANES + lane] -= 1
                bits[2 * n, lane] = 1 << (x + dx + 8 * (z ^ f))
            if 0 <= x - dx < 8 and 0 <= y - dy < 8:
                bits[2 * n + 1, lane] = 1 << (x - dx + 8 * (z ^ f))
    return sel, bits


OFFSET_LANES = (27, 28, 35)
NEAR = [(7, 0), (7, 1), (6, 0), (7, 2), (6, 1), (5, 0)]
FAR = [(7, 0, 2), (7, 1, 2), (6, 0, 2), (7, 0, 3), (7, 0, -2), (7, 1, -2), (6, 0, -2), (7, 0, -3)]


def fill(sel, col, a, b, shift):
    for half in (0, LANES):
        sel[half + point(*b), col] += 1
        sel[half + point(*a), col] -= 1
        for c in range(3):
            sel[half + OFFSET_LANES[c], col] = b[c] - a[c] + shift[c]


def face_tables():
    sels = np.zeros((4, 2 * LANES, 8 * LANES), np.float32)
    backs = np.zeros((4, 2 * LANES, LANES), np.float32)
    tabs = np.zeros((4, 16, LANES), np.int32)
    for k in range(4):
        axis, sign = k // 2, 1 - 2 * (k % 2)
        side = lambda u: u if sign > 0 else 7 - u
        place = lambda u, t, z: (u, t, z) if axis == 0 else (t, u, z)
        shift = place(8 * sign, 0, 0)
        sel, back, tab = sels[k], backs[k], tabs[k]
        for z in range(2):
            for t in range(8):
                for c in range(8):
                    lane = point(*place(c, t, z))
                    ua, ub, dt = FAR[c]
                    a = place(side(ua), t, z)
                    tab[9, lane] = point(*a)
                    tab[12, lane] = ub
                    tab[13, lane] = dt
                    back[LANES + lane, point(*a)] = 1
                    todo = [(6 + f, f, a, ub, dt) for f in range(2)]
                    if c < len(NEAR):
                        ua, ub = NEAR[c]
                        a = place(side(ua), t, z)
                        tab[8, lane] = point(*a)
                        tab[11, lane] = ub
                        back[lane, point(*a)] = 1
                        todo += [(2 * m + f, f, a, ub, m - 1) for m in range(3) for f in range(2)]
                    for v, f, a, ub, dt in todo:
                        if 0 <= t + dt < 8:
                            b = place(side(ub), t + dt, z ^ f)
                            fill(sel, v * LANES + lane, a, b, shift)
                            tab[v, lane] = 1 << (b[0] + 8 * b[2])
                for u in range(3):
                    tab[10, point(*place(side(7 - u), t, z))] = 1
                    tab[10, point(*place(side(u), t, z))] = 2
        for col in range(8 * LANES):
            if not sel[:, col].any():
                sel[OFFSET_LANES[0], col] = 4
    return sels, backs, tabs


def corner_tables():
    sels = np.zeros((4, 2 * LANES, LANES), np.float32)
    backs = np.zeros((4, 2 * LANES, LANES), np.float32)
    tabs = np.zeros((4, 8, LANES), np.int32)
    combos = []
    for (ua, ub) in NEAR:
        for (va, vb) in NEAR:
            if near(ub + 8 - ua, vb + 8 - va):
                combos.append((ua, va, ub, vb))
    for k in range(4):
        sign_x, sign_y = 1 - 2 * (k // 2), 1 - 2 * (k % 2)
        side_x = lambda u: u if sign_x > 0 else 7 - u
        side_y = lambda u: u if sign_y > 0 else 7 - u
        sel, back, tab = sels[k], backs[k], tabs[k]
        for n, (ua, va, ub, vb) in enumerate(combos):
            for z in range(2):
                for f in range(2):
                    lane = n + 16 * z + 32 * f
                    a, b = (side_x(ua), side_y(va), z), (side_x(ub), side_y(vb), z ^ f)
                    fill(sel, lane, a, b, (8 * sign_x, 8 * sign_y, 0))
                    back[lane, point(*a)] = 1
                    back[LANES + lane, point(*a)] = 1
                    tab[0, lane] = 1 << (b[0] + 8 * b[2])
                    tab[1, lane] = point(*a)
                    tab[3, lane] = vb
        for col in range(LANES):
            if not sel[:, col].any():
                sel[OFFSET_LANES[0], col] = 4
        for z in range(2):
            for u in range(3):
                for v in range(3):
                    tab[2, point(side_x(7 - u), side_y(7 - v), z)] = 1
                    tab[2, point(side_x(u), side_y(v), z)] = 2
    return sels, backs, tabs


SELF_AT = 0
FACE_AT = SELF_AT + len(OFFSETS)
FACE_BACK = FACE_AT + 4 * 8
CORNER_AT = FACE_BACK + 4
CORNER_BACK = CORNER_AT + 4
SELF_ROW = 0
FACE_ROW = SELF_ROW + -(-2 * len(OFFSETS) // 8) * 8
CORNER_ROW = FACE_ROW + 4 * 16
CODE_ROW = CORNER_ROW + 4 * 8


def all_tables():
    sel0, bits0 = self_tables()
    sel1, back1, tab1 = face_tables()
    sel2, back2, tab2 = corner_tables()
    blocks = [sel0[:, n * LANES : (n + 1) * LANES] for n in range(len(OFFSETS))]
    blocks += [sel1[k, :, n * LANES : (n + 1) * LANES] for k in range(4) for n in range(8)]
    blocks += list(back1) + list(sel2) + list(back2)
    rows = [bits0, tab1.reshape(-1, LANES), tab2.reshape(-1, LANES), tab1[:, 10], tab2[:, 2]]
    return jnp.asarray(np.stack(blocks), BF16), jnp.asarray(np.concatenate(rows, axis=0))


def split(value):
    high = value.astype(BF16)
    return high, (value - high.astype(F32)).astype(BF16)


def bond_force(xi, y, moduli, dv, keep):
    r2 = xi[0] * xi[0] + xi[1] * xi[1] + xi[2] * xi[2]
    l2 = y[0] * y[0] + y[1] * y[1] + y[2] * y[2]
    c = moduli * jnp.maximum(9.0 - r2, 0.0)
    if keep is not None:
        c = jnp.where(keep, c, 0.0)
    r_inv = lax.rsqrt(r2)
    l_inv = lax.rsqrt(l2)
    cl = c * l_inv
    k2 = c * r_inv - cl
    along = cl * (l_inv * l_inv) * (y[0] * dv[0] + y[1] * dv[1] + y[2] * dv[2])
    return [k2 * dv[i] + along * y[i] for i in range(3)]


def gather_kernel(*refs):
    far, (wanted, source, shape_full, moved_full), near_copy = refs[:7], refs[7:11], refs[11:14]
    jit, disp, mod, vec, state, own, asked, hand, arrived, ghost, landed, sent, got, fetched = refs[14:]
    fetches = [
        pltpu.make_async_copy(a, b, fetched.at[n]) for n, (a, b) in enumerate(zip(far, (jit, disp, mod, vec) + near_copy))
    ]
    for fetch in fetches:
        fetch.start()
    n_x, n_y = lax.axis_size("gx"), lax.axis_size("gy")
    x, y = lax.axis_index("gx"), lax.axis_index("gy")
    tiles, points = mod.shape
    cap = landed.shape[2]

    def exists(offset):
        ox, oy = offset
        return (x + ox >= 0) & (x + ox < n_x) & (y + oy >= 0) & (y + oy < n_y)

    barrier = pltpu.get_barrier_semaphore()
    for offset in AROUND:

        @pl.when(exists(offset))
        def _():
            pl.semaphore_signal(
                barrier, inc=1, device_id=(x + offset[0], y + offset[1]), device_id_type=pl.DeviceIdType.MESH
            )

    pl.semaphore_wait(barrier, sum(jnp.where(exists(offset), 1, 0) for offset in AROUND))

    def copy(offsets, base, source_ref, target_ref, d):
        ox, oy = offsets[d]
        back = offsets.index((-ox, -oy))
        return pltpu.make_async_remote_copy(
            src_ref=source_ref.at[d],
            dst_ref=target_ref.at[back],
            send_sem=sent.at[base + d],
            recv_sem=got.at[base + back],
            device_id=(x + ox, y + oy),
            device_id_type=pl.DeviceIdType.MESH,
        )

    def start(*args):
        for d, offset in enumerate(args[0]):

            @pl.when(exists(offset))
            def _():
                copy(*args, d).start()

    def finish(*args):
        for d, (ox, oy) in enumerate(args[0]):

            @pl.when(exists((ox, oy)))
            def _():
                copy(*args, d).wait_send()
                copy(*args, args[0].index((-ox, -oy))).wait_recv()

    asking = (SIDES, 0, wanted, asked)
    handing = (SIDES, 4, hand, arrived)
    ghosting = (AROUND, 8, ghost, landed)
    start(*asking)
    for offsets, refs in ((SIDES, (asked, arrived)), (AROUND, (landed,))):
        for d, offset in enumerate(offsets):

            @pl.when(jnp.logical_not(exists(offset)))
            def _():
                for ref in refs:
                    ref[d] = jnp.zeros_like(ref[d])

    for fetch in fetches[:4]:
        fetch.wait()
    for c in range(FIELDS):
        if c < 3:
            value = jit[c]
        elif c < 6:
            value = jit[c - 3] + disp[c - 3]
        elif c == 6:
            value = mod[...] * (0.05 / 9.0)
        else:
            value = vec[c - 7]
        high, low = split(value)
        state[0:tiles, c * points : (c + 1) * points] = high
        state[tiles : 2 * tiles, c * points : (c + 1) * points] = low

    def hot(index, base, width):
        ids = lax.broadcasted_iota(jnp.int32, index.shape, 1) % width + base
        return jnp.where(index == ids, 1.0, 0.0).astype(BF16)

    def twice(value):
        return jnp.concatenate([value, value], axis=1)

    finish(*asking)
    left = twice(jnp.concatenate([hot(asked[d], 0, tiles) for d in range(4)], axis=0))
    for p in range(FIELDS // 2):
        out = jnp.dot(left, state[:, 2 * p * points : 2 * (p + 1) * points], preferred_element_type=F32)
        for f in range(2):
            for d in range(4):
                hand[d, 2 * p + f] = out[d * CAP : (d + 1) * CAP, f * points : (f + 1) * points]
    start(*handing)
    left = twice(hot(source[...], 0, tiles))
    for p in range(FIELDS // 2):
        at = slice(2 * p * points, 2 * (p + 1) * points)
        own[:, at] = jnp.dot(left, state[:, at], preferred_element_type=F32)
    finish(*handing)
    left = hot(source[...], tiles, 4 * CAP)
    right = []
    for c in range(FIELDS):
        right.append(jnp.concatenate(split(jnp.concatenate([arrived[d, c] for d in range(4)], axis=0)), axis=0))

    def settled(low_row, p):
        rows = slice(low_row, low_row + tiles)
        both = jnp.concatenate([right[2 * p], right[2 * p + 1]], axis=1)
        return own[rows, 2 * p * points : 2 * (p + 1) * points] + jnp.dot(left[rows], both, preferred_element_type=F32)

    for p in range(FIELDS // 2):
        out = settled(tiles, p)
        for f in range(2):
            for n in range(8):
                ghost[n, 2 * p + f] = out[n * cap : (n + 1) * cap, f * points : (f + 1) * points]
    start(*ghosting)

    def spread(row, c, value):
        target = shape_full if c < 7 else moved_full
        for j in range(0, value.shape[0], 8):
            target[pl.ds((row + j) * 8 + c % 7, 8, stride=8)] = value[j : j + 8]

    for p in range(FIELDS // 2):
        out = settled(0, p)
        for f in range(2):
            spread(0, 2 * p + f, out[:, f * points : (f + 1) * points])
    for fetch in fetches[4:]:
        fetch.wait()
    finish(*ghosting)
    for n, e in enumerate(DIRS):
        for c in range(FIELDS):
            spread(tiles + e * cap, c, landed[n, c])


def apply_kernel(first, pairs, order, bounds, owner, target, blocks_of, table, *rest):
    if first:
        words, shape_full, moved_full, image, echo, sends, shape, flags, moved, force = *rest[:5], rest[5:13], *rest[13:]
    else:
        field, field_ghosts, shape, flags, image, moved_full, moved, force = rest[0], rest[1:9], *rest[9:]
    _, rows, points = image.shape
    if first:
        cap = sends[0].shape[1]
    else:
        cap = field_ghosts[0].shape[1]
        for c in range(3):
            for j in range(0, rows, 8):
                moved_full[pl.ds(j * 8 + c, 8, stride=8)] = field[c, j : j + 8]
            for e, ghost in zip(DIRS, field_ghosts):
                for j in range(0, cap, 8):
                    moved_full[pl.ds((rows + e * cap + j) * 8 + c, 8, stride=8)] = ghost[c, j : j + 8]

    lane = lax.broadcasted_iota(jnp.int32, (8, points), 1)
    sub = lax.broadcasted_iota(jnp.int32, (8, points), 0)
    lane_y = lane // 8 % 8
    low_z = lane < 64
    unit = jnp.zeros((8, points), F32)
    for c in range(6):
        unit = jnp.where((sub == c) & (lane == OFFSET_LANES[c % 3]), 1.0, unit)
    turn = jnp.where(sub == 6, -1.0, 1.0)

    def tile_of(row, ref):
        return ref[pl.ds(pl.multiple_of(row * 8, 8), 8)]

    def build(shifted, g, carry):
        if shifted:
            k = sum(jnp.where(g >= bounds[c], 1, 0) for c in range(2, 9))
            held = jnp.broadcast_to(table[pl.ds(CODE_ROW + k, 1)], (8, points))
            take_a, take_b = held == 1, held == 2
        for u in range(CHUNK):
            q = jnp.maximum(order[g * CHUNK + u], 0)
            tile, partner = pairs[0, q], pairs[1, q]
            if first:
                state = tile_of(tile, shape_full)
                if shifted:
                    state = jnp.where(take_a, state * turn, jnp.where(take_b, tile_of(partner, shape_full), unit))
                shape[g, pl.ds(u, 8, stride=CHUNK)] = state
                word = jnp.bitwise_not(words[q, 0:8] | jnp.left_shift(words[q, 8:16], 8))
                flags[g, pl.ds(u, 8, stride=CHUNK)] = word
            state = tile_of(tile, moved_full)
            if shifted:
                state = jnp.where(take_a, state, jnp.where(take_b, tile_of(partner, moved_full), 0.0))
            moved[g, pl.ds(u, 3, stride=CHUNK)] = state[0:3]
        return carry

    lax.fori_loop(bounds[0], bounds[1], functools.partial(build, False), 0)
    lax.fori_loop(bounds[1], bounds[9], functools.partial(build, True), 0)

    def row_of(at):
        return jnp.broadcast_to(table[pl.ds(at, 1)], (8, points))

    def two_blocks(at):
        return jnp.concatenate([blocks_of[at], blocks_of[at + 1]], axis=1)

    def pick(value, index):
        return jnp.take_along_axis(value, index, axis=1, mode="promise_in_bounds")

    def word_of(g, h, y):
        start = y * CHUNK + 8 * h
        if not isinstance(start, int):
            start = pl.multiple_of(start, 8)
        return flags[g, pl.ds(start, 8)]

    def by_row(g, h):
        held = [word_of(g, h, y) for y in range(8)]
        for bit in (1, 2, 4):
            odd = (lane_y & bit) != 0
            held = [jnp.where(odd, held[(s + bit) % 8], held[s]) for s in range(8)]
        return held

    def left_side(g):
        values = [shape[g, c * CHUNK : (c + 1) * CHUNK] for c in range(7)]
        values += [moved[g, c * CHUNK : (c + 1) * CHUNK] for c in range(3)]
        parts = [split(v) for v in values]
        high = jnp.concatenate([p[0] for p in parts], axis=0)
        low = jnp.concatenate([p[1] for p in parts], axis=0)
        return jnp.concatenate([high, low], axis=1)

    def block(wide, c, h, v):
        return wide[c * CHUNK + 8 * h : c * CHUNK + 8 * h + 8, v * points : (v + 1) * points]

    def put(g, c, value):
        force[c, pl.ds(pl.multiple_of(g * CHUNK, CHUNK), CHUNK)] = value

    def same_tile(g, carry):
        left = left_side(g)
        words_of = [by_row(g, h) for h in range(2)]
        twice = [2.0 * shape[g, 6 * CHUNK + 8 * h : 6 * CHUNK + 8 * h + 8] for h in range(2)]
        acc = [[jnp.zeros((8, points), F32)] * 3 for _ in range(2)]
        other = jnp.where(low_z, 1.0, -1.0)
        for start in range(0, len(OFFSETS), 2):
            some = OFFSETS[start : start + 2]
            right = two_blocks(SELF_AT + start) if len(some) == 2 else blocks_of[SELF_AT + start]
            wide = jnp.dot(left, right, preferred_element_type=F32)
            for v, (dx, dy, f) in enumerate(some):
                n = start + v
                base = (float(dx), float(dy), other if f else 0.0)
                for h in range(2):
                    part = lambda c: block(wide, c, h, v)
                    xi = [part(c) + base[c] for c in range(3)]
                    y = [part(3 + c) + base[c] for c in range(3)]
                    dv = [part(7 + c) for c in range(3)]
                    term = bond_force(xi, y, part(6) + twice[h], dv, None)
                    keep = (words_of[h][dy % 8] & row_of(SELF_ROW + 2 * n)) != 0
                    acc[h] = [acc[h][i] + jnp.where(keep, term[i], 0.0) for i in range(3)]
                    if (dx, dy) != (0, 0):
                        keep = (words_of[h][-dy % 8] & row_of(SELF_ROW + 2 * n + 1)) != 0
                        off = (dx + 8 * dy + 64 * f) % points
                        acc[h] = [acc[h][i] - jnp.where(keep, pltpu.roll(term[i], off, 1), 0.0) for i in range(3)]
        for c in range(3):
            put(g, c, jnp.concatenate([acc[0][c], acc[1][c]], axis=0))
        return carry

    lax.fori_loop(bounds[0], bounds[1], same_tile, 0)

    def of_block(wide, h, v, keep):
        part = lambda c: block(wide, c, h, v)
        xi = [part(c) for c in range(3)]
        y = [part(3 + c) for c in range(3)]
        dv = [part(7 + c) for c in range(3)]
        return bond_force(xi, y, part(6), dv, keep)

    def face(axis, g):
        k = 2 * axis + jnp.where(g >= bounds[2 * axis + 2], 1, 0)
        left = left_side(g)
        index_near = row_of(FACE_ROW + 16 * k + 8)
        index_far = row_of(FACE_ROW + 16 * k + 9)
        close = [[jnp.zeros((8, points), F32)] * 3 for _ in range(2)]
        distant = [[jnp.zeros((8, points), F32)] * 3 for _ in range(2)]
        near_words, far_words = [], []
        for h in range(2):
            if axis == 0:
                rel = by_row(g, h)
                dt = row_of(FACE_ROW + 16 * k + 13)
                near_words.append([pick(rel[(m - 1) % 8], index_near) for m in range(3)])
                chosen = pick(rel[2], index_far)
                for d in (3, -2, -3):
                    chosen = jnp.where(dt == d, pick(rel[d % 8], index_far), chosen)
                far_words.append(chosen)
            else:
                for at, index, into in ((11, index_near, near_words), (12, index_far, far_words)):
                    row = row_of(FACE_ROW + 16 * k + at)
                    chosen = None
                    for j in range(3):
                        word = pick(word_of(g, h, jnp.where(k == 3, 7 - j, j)), index)
                        chosen = word if j == 0 else jnp.where(row == j, word, chosen)
                    into.append([chosen] * 3 if at == 11 else chosen)
        for m in range(4):
            wide = jnp.dot(left, two_blocks(FACE_AT + 8 * k + 2 * m), preferred_element_type=F32)
            for f in range(2):
                for h in range(2):
                    word = near_words[h][m] if m < 3 else far_words[h]
                    keep = (word & row_of(FACE_ROW + 16 * k + 2 * m + f)) != 0
                    term = of_block(wide, h, f, keep)
                    acc = close if m < 3 else distant
                    acc[h] = [acc[h][i] + term[i] for i in range(3)]
        total = []
        for acc in (close, distant):
            stacked = jnp.concatenate([acc[h][c] for c in range(3) for h in range(2)], axis=0)
            high, low = split(stacked)
            total.append(jnp.concatenate([high, low], axis=0))
        back = jnp.dot(jnp.concatenate(total, axis=1), blocks_of[FACE_BACK + k], preferred_element_type=F32)
        for c in range(3):
            at = c * CHUNK
            put(g, c, back[at : at + CHUNK] + back[3 * CHUNK + at : 3 * CHUNK + at + CHUNK])

    def corner(g):
        k = sum(jnp.where(g >= bounds[c], 1, 0) for c in (6, 7, 8))
        left = left_side(g)
        index = row_of(CORNER_ROW + 8 * k + 1)
        row = row_of(CORNER_ROW + 8 * k + 3)
        wide = jnp.dot(left, blocks_of[CORNER_AT + k], preferred_element_type=F32)
        terms = []
        for h in range(2):
            chosen = None
            for j in range(3):
                word = pick(word_of(g, h, jnp.where((k & 1) == 1, 7 - j, j)), index)
                chosen = word if j == 0 else jnp.where(row == j, word, chosen)
            keep = (chosen & row_of(CORNER_ROW + 8 * k)) != 0
            terms.append(of_block(wide, h, 0, keep))
        stacked = jnp.concatenate([terms[h][c] for c in range(3) for h in range(2)], axis=0)
        back = jnp.dot(jnp.concatenate(split(stacked), axis=1), blocks_of[CORNER_BACK + k], preferred_element_type=F32)
        for c in range(3):
            put(g, c, back[c * CHUNK : (c + 1) * CHUNK])

    def over(low, high, width, body):
        def step(i, carry):
            for u in range(width):
                body(jnp.minimum(low + i * width + u, high - 1))
            return carry

        lax.fori_loop(0, (high - low + width - 1) // width, step, 0)

    over(bounds[1], bounds[3], FACE_WIDTH, functools.partial(face, 0))
    over(bounds[3], bounds[5], FACE_WIDTH, functools.partial(face, 1))
    over(bounds[5], bounds[9], CORNER_WIDTH, corner)

    blocks = (bounds[9] * CHUNK + LANES - 1) // LANES

    def clear(g, carry):
        for c in range(3):
            put(g, c, jnp.zeros((CHUNK, points), F32))
        return carry

    lax.fori_loop(bounds[9], blocks * (LANES // CHUNK), clear, 0)
    image[...] = jnp.zeros_like(image)
    if first:
        for out in sends:
            out[...] = jnp.zeros_like(out)
    tile_at = lax.broadcasted_iota(jnp.int32, (rows, LANES), 0)
    if first:
        tile_at = jnp.concatenate([tile_at, target[...]], axis=0)

    def gather_tiles(b, carry):
        hot = jnp.where(tile_at == owner[pl.ds(b, 1)], 1.0, 0.0).astype(BF16)
        parts = [split(force[c, pl.ds(pl.multiple_of(b * LANES, LANES), LANES)]) for c in range(3)]
        high = jnp.concatenate([p[0] for p in parts], axis=1)
        low = jnp.concatenate([p[1] for p in parts], axis=1)
        out = jnp.dot(
            jnp.concatenate([hot, hot], axis=1), jnp.concatenate([high, low], axis=0), preferred_element_type=F32
        )
        for c in range(3):
            image[c] += out[:rows, c * points : (c + 1) * points]
            if first:
                for n, send in enumerate(sends):
                    send[c] += out[rows + n * cap : rows + (n + 1) * cap, c * points : (c + 1) * points]
        return carry

    lax.fori_loop(0, blocks, gather_tiles, 0)
    if first:
        echo[...] = image[...]


def exchange_kernel(offsets, *refs):
    n = len(offsets)
    ins, outs, send_sem, recv_sem = refs[:n], refs[n : 2 * n], refs[2 * n], refs[2 * n + 1]
    n_x, n_y = lax.axis_size("gx"), lax.axis_size("gy")
    x, y = lax.axis_index("gx"), lax.axis_index("gy")

    def exists(ox, oy):
        return (x + ox >= 0) & (x + ox < n_x) & (y + oy >= 0) & (y + oy < n_y)

    barrier = pltpu.get_barrier_semaphore()
    for ox, oy in offsets:

        @pl.when(exists(ox, oy))
        def _():
            pl.semaphore_signal(
                barrier, inc=1, device_id=(x + ox, y + oy), device_id_type=pl.DeviceIdType.MESH
            )

    peers = sum(jnp.where(exists(ox, oy), 1, 0) for ox, oy in offsets)
    pl.semaphore_wait(barrier, peers)

    def copy(d):
        ox, oy = offsets[d]
        back = offsets.index((-ox, -oy))
        return pltpu.make_async_remote_copy(
            src_ref=ins[d],
            dst_ref=outs[back],
            send_sem=send_sem.at[d],
            recv_sem=recv_sem.at[back],
            device_id=(x + ox, y + oy),
            device_id_type=pl.DeviceIdType.MESH,
        )

    for d, (ox, oy) in enumerate(offsets):

        @pl.when(exists(ox, oy))
        def _():
            copy(d).start()

        @pl.when(jnp.logical_not(exists(ox, oy)))
        def _():
            outs[d][...] = jnp.zeros_like(outs[d])

    for d, (ox, oy) in enumerate(offsets):

        @pl.when(exists(ox, oy))
        def _():
            copy(d).wait_send()
            copy(offsets.index((-ox, -oy))).wait_recv()


def exchange(blocks, offsets, ident):
    n = len(offsets)
    return pl.pallas_call(
        functools.partial(exchange_kernel, offsets),
        out_shape=[jax.ShapeDtypeStruct(b.shape, b.dtype) for b in blocks],
        in_specs=[VMEM] * n,
        out_specs=[VMEM] * n,
        scratch_shapes=[pltpu.SemaphoreType.DMA((n,)), pltpu.SemaphoreType.DMA((n,))],
        compiler_params=pltpu.CompilerParams(
            collective_id=ident, has_side_effects=True, vmem_limit_bytes=4 * 1024 * 1024
        ),
    )(*blocks)


def plan(pair_list, count):
    pairs = pair_list.shape[1]
    slots = -(-(pairs + CLASSES * (CHUNK - 1)) // LANES) * LANES
    slot = jnp.arange(pairs, dtype=jnp.int32)
    sx, sy = pair_list[2], pair_list[3]
    flat_x = jnp.where(sx > 0, 1, 2)
    flat_y = jnp.where(sy > 0, 3, 4)
    slant = 5 + 2 * (sx < 0) + (sy < 0)
    kind = jnp.where(sx == 0, jnp.where(sy == 0, 0, flat_y), jnp.where(sy == 0, flat_x, slant))
    kind = jnp.where(slot < count, kind, 15).astype(jnp.int32)
    ids = jnp.arange(16, dtype=jnp.int32)
    earlier = (kind[:, None] == kind[None, :]) & (slot[:, None] < slot[None, :])
    rank = jnp.sum(earlier.astype(jnp.int32), axis=0)
    before = (kind[:, None] < ids[None, :]) & (ids[None, :] < 15)
    member = kind[:, None] == ids[None, :]
    chunks = (jnp.sum(member.astype(jnp.int32), axis=0) + CHUNK - 1) // CHUNK
    start = jnp.sum(jnp.where(ids[:, None] < ids[None, :], chunks[:, None], 0), axis=0)
    place = rank + CHUNK * jnp.sum(jnp.where(member, start[None, :], 0), axis=1)
    place = jnp.where(kind < CLASSES, place, -1)
    hit = place[:, None] == jnp.arange(slots, dtype=jnp.int32)[None, :]
    order = jnp.sum(jnp.where(hit, slot[:, None] + 1, 0), axis=0) - 1
    owner = jnp.sum(jnp.where(hit, pair_list[0][:, None] + 1, 0), axis=0) - 1
    return order, start, owner.reshape(slots // LANES, LANES)


def tangents(pairs, order, bounds, owner, send, words, tables, shape_full, moved_full, swap):
    cap, points = send.shape[1], words.shape[2]
    tiles = shape_full.shape[0] // 8 - 9 * cap
    slots = order.shape[0]
    chunks = slots // CHUNK
    target = jnp.broadcast_to(send.reshape(-1)[:, None], (send.size, LANES))
    head = (pairs, order, bounds, owner, target, *tables)
    image_shape = jax.ShapeDtypeStruct((3, tiles, points), F32)
    kept = [
        jax.ShapeDtypeStruct((chunks, 8 * CHUNK, points), F32),
        jax.ShapeDtypeStruct((chunks, 8 * CHUNK, points), jnp.int32),
    ]
    scratch = [
        pltpu.VMEM((chunks, 3 * CHUNK, points), F32),
        pltpu.VMEM((3, slots, points), F32),
    ]
    limit = pltpu.CompilerParams(vmem_limit_bytes=16 * 1024 * 1024)
    first_image, field, *rest = pl.pallas_call(
        functools.partial(apply_kernel, True),
        out_shape=[image_shape] * 2 + [jax.ShapeDtypeStruct((3, cap, points), F32)] * 8 + kept,
        in_specs=[SMEM] * 3 + [VMEM] * 7,
        out_specs=[VMEM] * 12,
        scratch_shapes=scratch,
        compiler_params=limit,
    )(*head, words, shape_full, moved_full)
    image_sends, kept = rest[:8], rest[8:]
    image_ghosts = swap(image_sends)
    second_image = pl.pallas_call(
        functools.partial(apply_kernel, False),
        out_shape=image_shape,
        in_specs=[SMEM] * 3 + [VMEM] * 15,
        out_specs=VMEM,
        scratch_shapes=[pltpu.VMEM(moved_full.shape, F32)] + scratch,
        compiler_params=limit,
    )(*head, field, *image_ghosts, *kept)
    return first_image, second_image


def on_device(jitter, displacement, modulus, start_vec, old_home, ghost_send, pair_list, pair_count, broken):
    tiles = old_home.shape[0]
    points = jitter.shape[2]
    cap = ghost_send.shape[2]
    width_y = lax.axis_size("gy")
    anchor = old_home // tiles
    old_slot = old_home % tiles
    off_x = anchor // width_y - lax.axis_index("gx")
    off_y = anchor % width_y - lax.axis_index("gy")
    side = jnp.where(off_x == -1, 0, jnp.where(off_x == 1, 1, jnp.where(off_y == -1, 2, jnp.where(off_y == 1, 3, 4))))
    index = jnp.arange(tiles, dtype=jnp.int32)
    earlier = (side[:, None] == side[None, :]) & (index[:, None] < index[None, :])
    ranked = jnp.sum(earlier.astype(jnp.int32), axis=0)
    cell = jnp.where(side < 4, side * CAP + ranked, -1)
    hit = cell[:, None] == jnp.arange(4 * CAP, dtype=jnp.int32)[None, :]
    wanted = jnp.sum(jnp.where(hit, old_slot[:, None], 0), axis=0)
    wanted = jnp.broadcast_to(wanted.reshape(4, CAP)[:, :, None], (4, CAP, LANES))
    pick = jnp.where(side < 4, tiles + cell, old_slot)
    send = jnp.maximum(jnp.concatenate([ghost_send[0, :4], ghost_send[0, 5:]], axis=0), 0)
    sent = send.reshape(-1)
    sent_pick = jnp.sum(jnp.where(sent[:, None] == index[None, :], pick[None, :], 0), axis=1)
    source = jnp.broadcast_to(jnp.concatenate([pick, sent_pick])[:, None], (tiles + sent.shape[0], LANES))
    turned = lambda value: jnp.transpose(value, (1, 0, 2))
    rows = tiles + 9 * cap
    full = pltpu.VMEM((rows * 8, points), F32)
    tables = all_tables()
    local = [turned(jitter), turned(displacement), modulus, turned(start_vec)]
    space = lambda value: pltpu.VMEM(value.shape, value.dtype)
    shape_full, moved_full, words, *tables = pl.pallas_call(
        gather_kernel,
        out_shape=[full, full] + [space(v) for v in (broken, *tables)],
        in_specs=[HBM] * 7 + [VMEM] * 2,
        out_specs=[VMEM] * 5,
        scratch_shapes=[space(value) for value in local]
        + [
            pltpu.VMEM((2 * tiles, FIELDS * points), BF16),
            pltpu.VMEM((tiles + 8 * cap, FIELDS * points), F32),
            pltpu.VMEM((4, CAP, LANES), jnp.int32),
            pltpu.VMEM((4, FIELDS, CAP, points), F32),
            pltpu.VMEM((4, FIELDS, CAP, points), F32),
            pltpu.VMEM((8, FIELDS, cap, points), F32),
            pltpu.VMEM((8, FIELDS, cap, points), F32),
            pltpu.SemaphoreType.DMA((16,)),
            pltpu.SemaphoreType.DMA((16,)),
            pltpu.SemaphoreType.DMA((7,)),
        ],
        compiler_params=pltpu.CompilerParams(
            collective_id=0, has_side_effects=True, vmem_limit_bytes=16 * 1024 * 1024
        ),
    )(*(pltpu.with_memory_space_constraint(v, pltpu.HBM) for v in (*local, broken, *tables)), wanted, source)
    order, bounds, owner = plan(pair_list[0], pair_count[0])
    first_image, second_image = tangents(
        pair_list[0], order, bounds, owner, send, words, tables, shape_full, moved_full, lambda sends: exchange(sends, AROUND, 1)
    )
    return turned(first_image), turned(second_image)


def solution(mesh):
    split = ("gx", "gy")
    spec3, spec2, spec1 = P(split, None, None), P(split, None), P(split)
    return jax.shard_map(
        on_device,
        mesh=mesh,
        in_specs=(spec3, spec3, spec2, spec3, spec1, spec3, spec3, spec1, spec3),
        out_specs=(spec3, spec3),
        check_vma=False,
    )
```

```python
import functools
import jax
import jax.numpy as jnp
import numpy as np
from jax import lax
from jax.experimental import pallas as pl
from jax.experimental.pallas import tpu as pltpu
from jax.sharding import PartitionSpec as P

CAP = 16
F32 = jnp.float32
BF16 = jnp.bfloat16
VMEM = pl.BlockSpec(memory_space=pltpu.VMEM)
SMEM = pl.BlockSpec(memory_space=pltpu.SMEM)
HBM = pl.BlockSpec(memory_space=pltpu.HBM)
DIRS = (0, 1, 2, 3, 5, 6, 7, 8)
SIDES = ((-1, 0), (1, 0), (0, -1), (0, 1))
AROUND = tuple((e // 3 - 1, e % 3 - 1) for e in DIRS)
CLASSES = 9
FIELDS = 10
SELF_CHUNKS = 4
CHUNK = 16
LANES = 128
FACE_WIDTH = 4
CORNER_WIDTH = 8


def near(dx, dy):
    return max(abs(dx) - 0.4, 0.0) ** 2 + max(abs(dy) - 0.4, 0.0) ** 2 < 9.0


def point(x, y, z):
    return x + 8 * y + 64 * z


HALF = [(dx, dy) for dy in range(4) for dx in range(-3, 4) if (dy > 0 or dx > 0) and near(dx, dy)]
OFFSETS = [(0, 0, 1)] + [(dx, dy, f) for dx, dy in HALF for f in (0, 1)]


def self_tables():
    sel = np.zeros((2 * LANES, len(OFFSETS) * LANES), np.float32)
    bits = np.zeros((-(-2 * len(OFFSETS) // 8) * 8, LANES), np.int32)
    for n, (dx, dy, f) in enumerate(OFFSETS):
        for lane in range(LANES):
            x, y, z = lane % 8, lane // 8 % 8, lane // 64
            if 0 <= x + dx < 8 and 0 <= y + dy < 8:
                for half in (0, LANES):
                    sel[half + point(x + dx, y + dy, z ^ f), n * LANES + lane] += 1
                    sel[half + lane, n * LANES + lane] -= 1
                bits[2 * n, lane] = 1 << (x + dx + 8 * (z ^ f))
            if 0 <= x - dx < 8 and 0 <= y - dy < 8:
                bits[2 * n + 1, lane] = 1 << (x - dx + 8 * (z ^ f))
    return sel, bits


OFFSET_LANES = (27, 28, 35)
NEAR = [(7, 0), (7, 1), (6, 0), (7, 2), (6, 1), (5, 0)]
FAR = [(7, 0, 2), (7, 1, 2), (6, 0, 2), (7, 0, 3), (7, 0, -2), (7, 1, -2), (6, 0, -2), (7, 0, -3)]


def fill(sel, col, a, b, shift):
    for half in (0, LANES):
        sel[half + point(*b), col] += 1
        sel[half + point(*a), col] -= 1
        for c in range(3):
            sel[half + OFFSET_LANES[c], col] = b[c] - a[c] + shift[c]


def face_tables():
    sels = np.zeros((4, 2 * LANES, 8 * LANES), np.float32)
    backs = np.zeros((4, 2 * LANES, LANES), np.float32)
    tabs = np.zeros((4, 16, LANES), np.int32)
    for k in range(4):
        axis, sign = k // 2, 1 - 2 * (k % 2)
        side = lambda u: u if sign > 0 else 7 - u
        place = lambda u, t, z: (u, t, z) if axis == 0 else (t, u, z)
        shift = place(8 * sign, 0, 0)
        sel, back, tab = sels[k], backs[k], tabs[k]
        for z in range(2):
            for t in range(8):
                for c in range(8):
                    lane = point(*place(c, t, z))
                    ua, ub, dt = FAR[c]
                    a = place(side(ua), t, z)
                    tab[9, lane] = point(*a)
                    tab[12, lane] = ub
                    tab[13, lane] = dt
                    back[LANES + lane, point(*a)] = 1
                    todo = [(6 + f, f, a, ub, dt) for f in range(2)]
                    if c < len(NEAR):
                        ua, ub = NEAR[c]
                        a = place(side(ua), t, z)
                        tab[8, lane] = point(*a)
                        tab[11, lane] = ub
                        back[lane, point(*a)] = 1
                        todo += [(2 * m + f, f, a, ub, m - 1) for m in range(3) for f in range(2)]
                    for v, f, a, ub, dt in todo:
                        if 0 <= t + dt < 8:
                            b = place(side(ub), t + dt, z ^ f)
                            fill(sel, v * LANES + lane, a, b, shift)
                            tab[v, lane] = 1 << (b[0] + 8 * b[2])
                for u in range(3):
                    tab[10, point(*place(side(7 - u), t, z))] = 1
                    tab[10, point(*place(side(u), t, z))] = 2
        for col in range(8 * LANES):
            if not sel[:, col].any():
                sel[OFFSET_LANES[0], col] = 4
    return sels, backs, tabs


def corner_tables():
    sels = np.zeros((4, 2 * LANES, LANES), np.float32)
    backs = np.zeros((4, 2 * LANES, LANES), np.float32)
    tabs = np.zeros((4, 8, LANES), np.int32)
    combos = []
    for (ua, ub) in NEAR:
        for (va, vb) in NEAR:
            if near(ub + 8 - ua, vb + 8 - va):
                combos.append((ua, va, ub, vb))
    for k in range(4):
        sign_x, sign_y = 1 - 2 * (k // 2), 1 - 2 * (k % 2)
        side_x = lambda u: u if sign_x > 0 else 7 - u
        side_y = lambda u: u if sign_y > 0 else 7 - u
        sel, back, tab = sels[k], backs[k], tabs[k]
        for n, (ua, va, ub, vb) in enumerate(combos):
            for z in range(2):
                for f in range(2):
                    lane = n + 16 * z + 32 * f
                    a, b = (side_x(ua), side_y(va), z), (side_x(ub), side_y(vb), z ^ f)
                    fill(sel, lane, a, b, (8 * sign_x, 8 * sign_y, 0))
                    back[lane, point(*a)] = 1
                    back[LANES + lane, point(*a)] = 1
                    tab[0, lane] = 1 << (b[0] + 8 * b[2])
                    tab[1, lane] = point(*a)
                    tab[3, lane] = vb
        for col in range(LANES):
            if not sel[:, col].any():
                sel[OFFSET_LANES[0], col] = 4
        for z in range(2):
            for u in range(3):
                for v in range(3):
                    tab[2, point(side_x(7 - u), side_y(7 - v), z)] = 1
                    tab[2, point(side_x(u), side_y(v), z)] = 2
    return sels, backs, tabs


SELF_AT = 0
FACE_AT = SELF_AT + len(OFFSETS)
FACE_BACK = FACE_AT + 4 * 8
CORNER_AT = FACE_BACK + 4
CORNER_BACK = CORNER_AT + 4
SELF_ROW = 0
FACE_ROW = SELF_ROW + -(-2 * len(OFFSETS) // 8) * 8
CORNER_ROW = FACE_ROW + 4 * 16
CODE_ROW = CORNER_ROW + 4 * 8


def all_tables():
    sel0, bits0 = self_tables()
    sel1, back1, tab1 = face_tables()
    sel2, back2, tab2 = corner_tables()
    blocks = [sel0[:, n * LANES : (n + 1) * LANES] for n in range(len(OFFSETS))]
    blocks += [sel1[k, :, n * LANES : (n + 1) * LANES] for k in range(4) for n in range(8)]
    blocks += list(back1) + list(sel2) + list(back2)
    rows = [bits0, tab1.reshape(-1, LANES), tab2.reshape(-1, LANES), tab1[:, 10], tab2[:, 2]]
    return jnp.asarray(np.stack(blocks), BF16), jnp.asarray(np.concatenate(rows, axis=0))


def split(value):
    high = value.astype(BF16)
    return high, (value - high.astype(F32)).astype(BF16)


def bond_shape(xi, y, moduli, keep):
    r2 = xi[0] * xi[0] + xi[1] * xi[1] + xi[2] * xi[2]
    l2 = y[0] * y[0] + y[1] * y[1] + y[2] * y[2]
    c = moduli * jnp.maximum(9.0 - r2, 0.0)
    if keep is not None:
        c = jnp.where(keep, c, 0.0)
    r_inv = lax.rsqrt(r2)
    l_inv = lax.rsqrt(l2)
    cl = c * l_inv
    return [c * r_inv - cl, cl * (l_inv * l_inv), *y]


def bond_pull(held, dv):
    k2, stretch, *y = held
    along = stretch * (y[0] * dv[0] + y[1] * dv[1] + y[2] * dv[2])
    return [k2 * dv[i] + along * y[i] for i in range(3)]


def bond_force(xi, y, moduli, dv, keep):
    return bond_pull(bond_shape(xi, y, moduli, keep), dv)


def plan_self(pairs, count, slots):
    total = pairs.shape[1]
    lanes = lambda shape, axis: lax.broadcasted_iota(jnp.int32, shape, axis)
    tile, sx, sy = pairs[0:1], pairs[2:3], pairs[3:4]
    inside = (sx == 0) & (sy == 0) & (lanes((1, total), 1) < count[0])
    member = jnp.where(inside, 1, 0)
    eight = (8, total)
    high_row = lanes(eight, 0) < 4
    turned = jnp.transpose(jnp.where(high_row, jnp.broadcast_to(member, eight), jnp.broadcast_to(tile, eight)))
    early = lanes((total, total), 0) < lanes((total, total), 1)
    rank = jnp.sum(jnp.where(early, turned[:, 0:1], 0), axis=0, keepdims=True)
    at = jnp.transpose(jnp.broadcast_to(jnp.where(inside, rank, -1), eight))[:, 0:1]
    hit = at == lanes((total, LANES), 1)
    slots[...] = jnp.zeros_like(slots)
    slots[0:1] = jnp.sum(jnp.where(hit, lanes((total, LANES), 0), 0), axis=0, keepdims=True)
    slots[8:9] = jnp.sum(jnp.where(hit, turned[:, 4:5], 0), axis=0, keepdims=True)


def tile_of(row, ref):
    if len(ref.shape) == 3:
        return ref[row]
    return ref[pl.ds(pl.multiple_of(row * 8, 8), 8)]


def packed(words, q):
    word = words[q]
    return jnp.bitwise_not(word[0:8] | jnp.left_shift(word[8:16], 8))


def slot_at(slots, kind, g, u):
    return slots[8 * kind + jnp.right_shift(g, 3), (g & 7) * CHUNK + u]


def self_shape(g, slots, words, shape_full, shape, flags):
    for u in range(CHUNK):
        shape[g, pl.ds(u, 8, stride=CHUNK)] = tile_of(slot_at(slots, 1, g, u), shape_full)
        flags[g, pl.ds(u, 8, stride=CHUNK)] = packed(words, slot_at(slots, 0, g, u))


def self_moved(g, slots, moved_full, moved):
    for u in range(CHUNK):
        moved[g, pl.ds(u, 3, stride=CHUNK)] = tile_of(slot_at(slots, 1, g, u), moved_full)[0:3]


def flag_rows(flags, g, h, y):
    start = y * CHUNK + 8 * h
    if not isinstance(start, int):
        start = pl.multiple_of(start, 8)
    return flags[g, pl.ds(start, 8)]


def turned_rows(flags, g, h):
    lane_y = lax.broadcasted_iota(jnp.int32, (8, LANES), 1) // 8 % 8
    held = [flag_rows(flags, g, h, y) for y in range(8)]
    for bit in (1, 2, 4):
        odd = (lane_y & bit) != 0
        held = [jnp.where(odd, held[(s + bit) % 8], held[s]) for s in range(8)]
    return held


def left_of(shape, moved, g):
    values = [] if shape is None else [shape[g, c * CHUNK : (c + 1) * CHUNK] for c in range(7)]
    values += [moved[g, c * CHUNK : (c + 1) * CHUNK] for c in range(3)]
    parts = [split(v) for v in values]
    high = jnp.concatenate([p[0] for p in parts], axis=0)
    low = jnp.concatenate([p[1] for p in parts], axis=0)
    return jnp.concatenate([high, low], axis=1)


def block(wide, c, h, v):
    return wide[c * CHUNK + 8 * h : c * CHUNK + 8 * h + 8, v * LANES : (v + 1) * LANES]


def joined_blocks(blocks_of, at):
    return jnp.concatenate([blocks_of[at], blocks_of[at + 1]], axis=1)


def store(force, g, c, value):
    force[c, pl.ds(pl.multiple_of(g * CHUNK, CHUNK), CHUNK)] = value


def self_bonds(g, shape, flags, moved, force, blocks_of, table):
    eight = (8, LANES)
    low_z = lax.broadcasted_iota(jnp.int32, eight, 1) < 64
    left = left_of(shape, moved, g)
    words_of = [turned_rows(flags, g, h) for h in range(2)]
    twice = [2.0 * shape[g, 6 * CHUNK + 8 * h : 6 * CHUNK + 8 * h + 8] for h in range(2)]
    acc = [[jnp.zeros(eight, F32)] * 3 for _ in range(2)]
    other = jnp.where(low_z, 1.0, -1.0)
    row_of = lambda at: jnp.broadcast_to(table[at : at + 1], eight)
    for start in range(0, len(OFFSETS), 2):
        some = OFFSETS[start : start + 2]
        right = joined_blocks(blocks_of, SELF_AT + start) if len(some) == 2 else blocks_of[SELF_AT + start]
        wide = jnp.dot(left, right, preferred_element_type=F32)
        for v, (dx, dy, f) in enumerate(some):
            n = start + v
            base = (float(dx), float(dy), other if f else 0.0)
            for h in range(2):
                part = lambda c: block(wide, c, h, v)
                xi = [part(c) + base[c] for c in range(3)]
                y = [part(3 + c) + base[c] for c in range(3)]
                dv = [part(7 + c) for c in range(3)]
                term = bond_force(xi, y, part(6) + twice[h], dv, None)
                keep = (words_of[h][dy % 8] & row_of(SELF_ROW + 2 * n)) != 0
                acc[h] = [acc[h][i] + jnp.where(keep, term[i], 0.0) for i in range(3)]
                if (dx, dy) != (0, 0):
                    keep = (words_of[h][-dy % 8] & row_of(SELF_ROW + 2 * n + 1)) != 0
                    off = (dx + 8 * dy + 64 * f) % LANES
                    acc[h] = [acc[h][i] - jnp.where(keep, pltpu.roll(term[i], off, 1), 0.0) for i in range(3)]
    for c in range(3):
        store(force, g, c, jnp.concatenate([acc[0][c], acc[1][c]], axis=0))


def plan(pairs, count, slots, bounds, owner):
    total = pairs.shape[1]
    lanes = lambda shape, axis: lax.broadcasted_iota(jnp.int32, shape, axis)
    one = (1, total)
    wide = (16, total)
    tile, partner, sx, sy = (pairs[n : n + 1] for n in range(4))
    slot = lanes(one, 1)
    flat_x = jnp.where(sx > 0, 1, 2)
    flat_y = jnp.where(sy > 0, 3, 4)
    slant = jnp.where(sx < 0, 7, 5) + jnp.where(sy < 0, 1, 0)
    kind = jnp.where(sx == 0, jnp.where(sy == 0, 0, flat_y), jnp.where(sy == 0, flat_x, slant))
    kind = jnp.where(slot < count[0], kind, 15)
    member = jnp.where(lanes(wide, 0) == kind, 1.0, 0.0)
    early = jnp.where(lanes((total, total), 0) < lanes((total, total), 1), 1.0, 0.0).astype(BF16)
    rank = jnp.dot(member.astype(BF16), early, preferred_element_type=F32)
    chunks = jnp.floor((jnp.sum(member, axis=1, keepdims=True) + float(CHUNK - 1)) * (1.0 / CHUNK))
    chunks = jnp.broadcast_to(chunks, (16, LANES))
    start = jnp.zeros((16, LANES), F32)
    for c in range(CLASSES):
        start = start + jnp.where(lanes((16, LANES), 0) > c, chunks[c : c + 1], 0.0)
    bounds[...] = start.astype(jnp.int32)
    at = rank + float(CHUNK) * jnp.broadcast_to(start[:, 0:1], wide)
    at = jnp.sum(member * at, axis=0, keepdims=True)
    at = jnp.where(kind < CLASSES, at, -1.0)
    at = jnp.transpose(jnp.broadcast_to(at, (8, total)))[:, 0:1]
    low = lambda value: (value & 255).astype(F32)
    high = lambda value: jnp.right_shift(value, 8).astype(F32)
    rows = [low(slot), high(slot), tile.astype(F32), low(partner), high(partner), jnp.ones(one, F32)]
    rows = jnp.concatenate(rows + [jnp.zeros((10, total), F32)], axis=0).astype(BF16)
    slots[...] = jnp.zeros_like(slots)
    owner[...] = jnp.full_like(owner, -1)
    for b in range(-(-(total + CLASSES * (CHUNK - 1)) // LANES)):
        here = (lanes((total, LANES), 1) + b * LANES).astype(F32)
        hit = jnp.where(jnp.broadcast_to(at, (total, LANES)) == here, 1.0, 0.0).astype(BF16)
        out = jnp.dot(rows, hit, preferred_element_type=F32).astype(jnp.int32)
        slots[b : b + 1] = out[0:1] + 256 * out[1:2]
        slots[8 + b : 9 + b] = out[2:3]
        slots[16 + b : 17 + b] = out[3:4] + 256 * out[4:5]
        owner[b : b + 1] = out[2:3] + out[5:6] - 1


def gather_kernel(*refs):
    far, count = refs[:10], refs[10]
    (shape_full, moved_full), near_copy, (slots, bounds, owner, target) = refs[11:13], refs[13:16], refs[16:20]
    shape, flags, done, refs = *refs[20:23], refs[23:]
    jit, disp, mod, vec, home, pairs, state, own, wanted, asked, hand, arrived, ghost, landed, moved, own_slots, near_slots = refs[:17]
    shape_own, moved_own, sending, sent, got, fetched = refs[17:]
    fetches = [
        pltpu.make_async_copy(a, b, fetched.at[n]) for n, (a, b) in enumerate(zip(far, (home, jit, disp, mod, vec, pairs) + near_copy + (sending,)))
    ]
    for fetch in fetches:
        fetch.start()
    n_x, n_y = lax.axis_size("gx"), lax.axis_size("gy")
    x, y = lax.axis_index("gx"), lax.axis_index("gy")
    tiles, points = mod.shape
    cap = landed.shape[2]

    def exists(offset):
        ox, oy = offset
        return (x + ox >= 0) & (x + ox < n_x) & (y + oy >= 0) & (y + oy < n_y)

    barrier = pltpu.get_barrier_semaphore()
    for offset in AROUND:

        @pl.when(exists(offset))
        def _():
            pl.semaphore_signal(
                barrier, inc=1, device_id=(x + offset[0], y + offset[1]), device_id_type=pl.DeviceIdType.MESH
            )

    pl.semaphore_wait(barrier, sum(jnp.where(exists(offset), 1, 0) for offset in AROUND))

    def copy(offsets, base, source_ref, target_ref, d):
        ox, oy = offsets[d]
        back = offsets.index((-ox, -oy))
        return pltpu.make_async_remote_copy(
            src_ref=source_ref.at[d],
            dst_ref=target_ref.at[back],
            send_sem=sent.at[base + d],
            recv_sem=got.at[base + back],
            device_id=(x + ox, y + oy),
            device_id_type=pl.DeviceIdType.MESH,
        )

    def start(*args):
        for d, offset in enumerate(args[0]):

            @pl.when(exists(offset))
            def _():
                copy(*args, d).start()

    def finish(*args):
        for d, (ox, oy) in enumerate(args[0]):

            @pl.when(exists((ox, oy)))
            def _():
                copy(*args, d).wait_send()
                copy(*args, args[0].index((-ox, -oy))).wait_recv()

    def lanes(shape, axis=1):
        return lax.broadcasted_iota(jnp.int32, shape, axis)

    def column(row):
        return jnp.transpose(jnp.broadcast_to(row, (LANES, LANES)))

    fetches[0].wait()
    anchor = jnp.right_shift(home[...], tiles.bit_length() - 1)
    off_x = jnp.right_shift(anchor, n_y.bit_length() - 1) - x
    off_y = (anchor & (n_y - 1)) - y
    side = jnp.where(off_x == -1, 0, jnp.where(off_x == 1, 1, jnp.where(off_y == -1, 2, jnp.where(off_y == 1, 3, 4))))
    square = (LANES, LANES)
    early = jnp.where(lanes(square, 0) < lanes(square), 1.0, 0.0).astype(BF16)
    member = jnp.where(lanes((CAP, LANES), 0) == jnp.broadcast_to(side, (CAP, LANES)), 1.0, 0.0)
    rank = jnp.dot(member.astype(BF16), early, preferred_element_type=F32)
    cell = jnp.sum(jnp.where(lanes((CAP, LANES), 0) < 4, member, 0.0) * rank, axis=0, keepdims=True)
    cell = jnp.where(side < 4, cell + (side * CAP).astype(F32), -1.0)
    old_slot = (home[...] & (tiles - 1)).astype(F32)
    origin = jnp.where(side < 4, cell + float(tiles), old_slot)
    ask = lanes((4 * CAP, LANES), 0).astype(F32) == cell
    ask = jnp.sum(jnp.where(ask, old_slot, 0.0), axis=1, keepdims=True)
    for d in range(4):
        wanted[d] = jnp.broadcast_to(ask[d * CAP : (d + 1) * CAP], (CAP, LANES))
    asking = (SIDES, 0, wanted, asked)
    handing = (SIDES, 4, hand, arrived)
    ghosting = (AROUND, 8, ghost, landed)
    start(*asking)
    for offsets, refs in ((SIDES, (asked, arrived)), (AROUND, (landed,))):
        for d, offset in enumerate(offsets):

            @pl.when(jnp.logical_not(exists(offset)))
            def _():
                for ref in refs:
                    ref[d] = jnp.zeros_like(ref[d])

    for fetch in fetches[1:5]:
        fetch.wait()
    for c in range(FIELDS):
        if c < 3:
            value = jit[c]
        elif c < 6:
            value = jit[c - 3] + disp[c - 3]
        elif c == 6:
            value = mod[...] * (0.05 / 9.0)
        else:
            value = vec[c - 7]
        high, low = split(value)
        state[0:tiles, c * points : (c + 1) * points] = high
        state[tiles : 2 * tiles, c * points : (c + 1) * points] = low

    def hot(index, base, width):
        ids = (lanes(index.shape) & (width - 1)) + base
        return jnp.where(index == ids.astype(F32), 1.0, 0.0).astype(BF16)

    def twice(value):
        return jnp.concatenate([value, value], axis=1)

    fetches[9].wait()
    corner_of = lanes((cap, cap), 0) == lanes((cap, cap))
    sent_tile = []
    for e in DIRS:
        row = jnp.maximum(jnp.broadcast_to(sending[e], (cap, cap)), 0).astype(F32)
        row = jnp.sum(jnp.where(corner_of, row, 0.0), axis=1, keepdims=True)
        sent_tile.append(jnp.broadcast_to(row, (cap, LANES)))
    sent_tile = jnp.concatenate(sent_tile, axis=0)
    target[...] = sent_tile.astype(jnp.int32)
    sent_from = jnp.where(sent_tile == lanes(square).astype(F32), origin, 0.0)
    sent_from = jnp.broadcast_to(jnp.sum(sent_from, axis=1, keepdims=True), square)
    source = jnp.concatenate([column(origin), sent_from], axis=0)
    finish(*asking)
    left = twice(jnp.concatenate([hot(asked[d], 0, tiles) for d in range(4)], axis=0))
    for p in range(FIELDS // 2):
        out = jnp.dot(left, state[:, 2 * p * points : 2 * (p + 1) * points], preferred_element_type=F32)
        for f in range(2):
            for d in range(4):
                hand[d, 2 * p + f] = out[d * CAP : (d + 1) * CAP, f * points : (f + 1) * points]
    start(*handing)
    left = twice(hot(source, 0, tiles))
    for p in range(FIELDS // 2):
        at = slice(2 * p * points, 2 * (p + 1) * points)
        own[:, at] = jnp.dot(left, state[:, at], preferred_element_type=F32)
    fetches[5].wait()
    plan(pairs, count, slots, bounds, owner)
    plan_self(pairs, count, own_slots)
    placing = pltpu.make_async_copy(own_slots, near_slots, fetched.at[10])
    placing.start()
    finish(*handing)
    left = hot(source, tiles, 4 * CAP)
    right = []
    for c in range(FIELDS):
        right.append(jnp.concatenate(split(jnp.concatenate([arrived[d, c] for d in range(4)], axis=0)), axis=0))

    def settled(low_row, p):
        rows = slice(low_row, low_row + tiles)
        both = jnp.concatenate([right[2 * p], right[2 * p + 1]], axis=1)
        return own[rows, 2 * p * points : 2 * (p + 1) * points] + jnp.dot(left[rows], both, preferred_element_type=F32)

    for p in range(FIELDS // 2):
        out = settled(tiles, p)
        for f in range(2):
            for n in range(8):
                ghost[n, 2 * p + f] = out[n * cap : (n + 1) * cap, f * points : (f + 1) * points]
    start(*ghosting)

    def spread(row, c, value):
        target = shape_full if c < 7 else moved_full
        for j in range(0, value.shape[0], 8):
            target[pl.ds((row + j) * 8 + c % 7, 8, stride=8)] = value[j : j + 8]

    for p in range(FIELDS // 2):
        out = settled(0, p)
        for f in range(2):
            value = out[:, f * points : (f + 1) * points]
            spread(0, 2 * p + f, value)
            own_tiles = shape_own if 2 * p + f < 7 else moved_own
            own_tiles[:, (2 * p + f) % 7] = value
    placing.wait()
    for fetch in fetches[6:9]:
        fetch.wait()
    words, blocks_of, table = near_copy

    def same(g, carry):
        self_shape(g, near_slots, words, shape_own, shape, flags)
        self_moved(g, near_slots, moved_own, moved)
        self_bonds(g, shape, flags, moved, done, blocks_of, table)
        return carry

    lax.fori_loop(0, SELF_CHUNKS, same, 0)
    finish(*ghosting)
    for n, e in enumerate(DIRS):
        for c in range(FIELDS):
            spread(tiles + e * cap, c, landed[n, c])


def apply_kernel(first, slots, starts, owner, target, blocks_of, table, *rest):
    if first:
        words, shape_full, moved_full, done, image, echo, sends, shape, flags, geometry, moved, force = *rest[:6], rest[6:14], *rest[14:]
    else:
        field, field_ghosts, done, shape, flags, geometry, image, moved_full, moved, force = rest[0], rest[1:9], *rest[9:]
    _, rows, points = image.shape
    bounds = [starts[c, 0] for c in range(CLASSES + 1)]
    if first:
        cap = sends[0].shape[1]
    else:
        cap = field_ghosts[0].shape[1]
        for c in range(3):
            for j in range(0, rows, 8):
                moved_full[pl.ds(j * 8 + c, 8, stride=8)] = field[c, j : j + 8]
            for e, ghost in zip(DIRS, field_ghosts):
                for j in range(0, cap, 8):
                    moved_full[pl.ds((rows + e * cap + j) * 8 + c, 8, stride=8)] = ghost[c, j : j + 8]

    lane = lax.broadcasted_iota(jnp.int32, (8, points), 1)
    sub = lax.broadcasted_iota(jnp.int32, (8, points), 0)
    unit = jnp.zeros((8, points), F32)
    for c in range(6):
        unit = jnp.where((sub == c) & (lane == OFFSET_LANES[c % 3]), 1.0, unit)
    turn = jnp.where(sub == 6, -1.0, 1.0)

    def build(g, carry):
        k = sum(jnp.where(g >= bounds[c], 1, 0) for c in range(2, 9))
        held = jnp.broadcast_to(table[pl.ds(CODE_ROW + k, 1)], (8, points))
        take_a, take_b = held == 1, held == 2
        block_of = jnp.right_shift(g, 3)
        base = (g & 7) * CHUNK
        for u in range(CHUNK):
            tile, partner = slots[8 + block_of, base + u], slots[16 + block_of, base + u]
            if first:
                state = jnp.where(take_b, tile_of(partner, shape_full), unit)
                shape[g, pl.ds(u, 8, stride=CHUNK)] = jnp.where(take_a, tile_of(tile, shape_full) * turn, state)
                flags[g, pl.ds(u, 8, stride=CHUNK)] = packed(words, slots[block_of, base + u])
            state = jnp.where(take_a, tile_of(tile, moved_full), jnp.where(take_b, tile_of(partner, moved_full), 0.0))
            moved[g, pl.ds(u, 3, stride=CHUNK)] = state[0:3]
        return carry

    def build_same(g, carry):
        if first:
            self_shape(g, slots, words, shape_full, shape, flags)
        self_moved(g, slots, moved_full, moved)
        return carry

    force[:, 0 : SELF_CHUNKS * CHUNK] = done[...]
    lax.fori_loop(SELF_CHUNKS, bounds[1], build_same, 0)
    lax.fori_loop(bounds[1], bounds[9], build, 0)

    def row_of(at):
        return jnp.broadcast_to(table[pl.ds(at, 1)], (8, points))

    two_blocks = functools.partial(joined_blocks, blocks_of)

    def pick(value, index):
        return jnp.take_along_axis(value, index, axis=1, mode="promise_in_bounds")

    word_of = functools.partial(flag_rows, flags)
    by_row = functools.partial(turned_rows, flags)
    put = functools.partial(store, force)

    def of_block(g, at, wide, h, v, keep):
        if not first:
            return bond_pull([geometry[g, 5 * at + n] for n in range(5)], [block(wide, c, h, v) for c in range(3)])
        part = lambda c: block(wide, c, h, v)
        held = bond_shape([part(c) for c in range(3)], [part(3 + c) for c in range(3)], part(6), keep)
        for n in range(5):
            geometry[g, 5 * at + n] = held[n]
        return bond_pull(held, [part(7 + c) for c in range(3)])

    def left_side(g):
        return left_of(shape if first else None, moved, g)

    def face_words(axis, k, g):
        index_near = row_of(FACE_ROW + 16 * k + 8)
        index_far = row_of(FACE_ROW + 16 * k + 9)
        near_words, far_words = [], []
        for h in range(2):
            if axis == 0:
                rel = by_row(g, h)
                dt = row_of(FACE_ROW + 16 * k + 13)
                near_words.append([pick(rel[(m - 1) % 8], index_near) for m in range(3)])
                chosen = pick(rel[2], index_far)
                for d in (3, -2, -3):
                    chosen = jnp.where(dt == d, pick(rel[d % 8], index_far), chosen)
                far_words.append(chosen)
            else:
                for at, index, into in ((11, index_near, near_words), (12, index_far, far_words)):
                    row = row_of(FACE_ROW + 16 * k + at)
                    chosen = None
                    for j in range(3):
                        word = pick(word_of(g, h, jnp.where(k == 3, 7 - j, j)), index)
                        chosen = word if j == 0 else jnp.where(row == j, word, chosen)
                    into.append([chosen] * 3 if at == 11 else chosen)
        return near_words, far_words

    def face(axis, g):
        if first:
            k = 2 * axis + jnp.where(g >= bounds[2 * axis + 2], 1, 0)
            near_words, far_words = face_words(axis, k, g)
        else:
            k = sum(jnp.where(g >= bounds[c], 1, 0) for c in (2, 3, 4))
        left = left_side(g)
        close = [[jnp.zeros((8, points), F32)] * 3 for _ in range(2)]
        distant = [[jnp.zeros((8, points), F32)] * 3 for _ in range(2)]
        for m in range(4):
            wide = jnp.dot(left, two_blocks(FACE_AT + 8 * k + 2 * m), preferred_element_type=F32)
            for f in range(2):
                for h in range(2):
                    keep = None
                    if first:
                        word = near_words[h][m] if m < 3 else far_words[h]
                        keep = (word & row_of(FACE_ROW + 16 * k + 2 * m + f)) != 0
                    term = of_block(g, 4 * m + 2 * f + h, wide, h, f, keep)
                    acc = close if m < 3 else distant
                    acc[h] = [acc[h][i] + term[i] for i in range(3)]
        total = []
        for acc in (close, distant):
            stacked = jnp.concatenate([acc[h][c] for c in range(3) for h in range(2)], axis=0)
            high, low = split(stacked)
            total.append(jnp.concatenate([high, low], axis=0))
        back = jnp.dot(jnp.concatenate(total, axis=1), blocks_of[FACE_BACK + k], preferred_element_type=F32)
        for c in range(3):
            at = c * CHUNK
            put(g, c, back[at : at + CHUNK] + back[3 * CHUNK + at : 3 * CHUNK + at + CHUNK])

    def corner(g):
        k = sum(jnp.where(g >= bounds[c], 1, 0) for c in (6, 7, 8))
        left = left_side(g)
        if first:
            index = row_of(CORNER_ROW + 8 * k + 1)
            row = row_of(CORNER_ROW + 8 * k + 3)
        wide = jnp.dot(left, blocks_of[CORNER_AT + k], preferred_element_type=F32)
        terms = []
        for h in range(2):
            keep = None
            if first:
                for j in range(3):
                    word = pick(word_of(g, h, jnp.where((k & 1) == 1, 7 - j, j)), index)
                    chosen = word if j == 0 else jnp.where(row == j, word, chosen)
                keep = (chosen & row_of(CORNER_ROW + 8 * k)) != 0
            terms.append(of_block(g, h, wide, h, 0, keep))
        stacked = jnp.concatenate([terms[h][c] for c in range(3) for h in range(2)], axis=0)
        back = jnp.dot(jnp.concatenate(split(stacked), axis=1), blocks_of[CORNER_BACK + k], preferred_element_type=F32)
        for c in range(3):
            put(g, c, back[c * CHUNK : (c + 1) * CHUNK])

    def over(low, high, width, body):
        def step(i, carry):
            for u in range(width):
                body(jnp.minimum(low + i * width + u, high - 1))
            return carry

        lax.fori_loop(0, (high - low + width - 1) // width, step, 0)

    if first:
        over(bounds[1], bounds[3], FACE_WIDTH, functools.partial(face, 0))
        over(bounds[3], bounds[5], FACE_WIDTH, functools.partial(face, 1))
    else:
        over(bounds[1], bounds[5], FACE_WIDTH, functools.partial(face, None))
    over(bounds[5], bounds[9], CORNER_WIDTH, corner)

    blocks = (bounds[9] * CHUNK + LANES - 1) // LANES

    def clear(g, carry):
        for c in range(3):
            put(g, c, jnp.zeros((CHUNK, points), F32))
        return carry

    lax.fori_loop(bounds[9], blocks * (LANES // CHUNK), clear, 0)
    image[...] = jnp.zeros_like(image)
    if first:
        for out in sends:
            out[...] = jnp.zeros_like(out)
    tile_at = lax.broadcasted_iota(jnp.int32, (rows, LANES), 0)
    if first:
        tile_at = jnp.concatenate([tile_at, target[...]], axis=0)

    def gather_tiles(b, carry):
        hot = jnp.where(tile_at == owner[pl.ds(b, 1)], 1.0, 0.0).astype(BF16)
        parts = [split(force[c, pl.ds(pl.multiple_of(b * LANES, LANES), LANES)]) for c in range(3)]
        high = jnp.concatenate([p[0] for p in parts], axis=1)
        low = jnp.concatenate([p[1] for p in parts], axis=1)
        out = jnp.dot(
            jnp.concatenate([hot, hot], axis=1), jnp.concatenate([high, low], axis=0), preferred_element_type=F32
        )
        for c in range(3):
            image[c] += out[:rows, c * points : (c + 1) * points]
            if first:
                for n, send in enumerate(sends):
                    send[c] += out[rows + n * cap : rows + (n + 1) * cap, c * points : (c + 1) * points]
        return carry

    lax.fori_loop(0, blocks, gather_tiles, 0)
    if first:
        echo[...] = image[...]


def exchange_kernel(offsets, *refs):
    n = len(offsets)
    ins, (field, slots, shape, flags, blocks_of, table), refs = refs[:n], refs[n : n + 6], refs[n + 6 :]
    outs, (done, moved_full, moved, send_sem, recv_sem) = refs[:n], refs[n:]
    n_x, n_y = lax.axis_size("gx"), lax.axis_size("gy")
    x, y = lax.axis_index("gx"), lax.axis_index("gy")

    def exists(ox, oy):
        return (x + ox >= 0) & (x + ox < n_x) & (y + oy >= 0) & (y + oy < n_y)

    barrier = pltpu.get_barrier_semaphore()
    for ox, oy in offsets:

        @pl.when(exists(ox, oy))
        def _():
            pl.semaphore_signal(
                barrier, inc=1, device_id=(x + ox, y + oy), device_id_type=pl.DeviceIdType.MESH
            )

    peers = sum(jnp.where(exists(ox, oy), 1, 0) for ox, oy in offsets)
    pl.semaphore_wait(barrier, peers)

    def copy(d):
        ox, oy = offsets[d]
        back = offsets.index((-ox, -oy))
        return pltpu.make_async_remote_copy(
            src_ref=ins[d],
            dst_ref=outs[back],
            send_sem=send_sem.at[d],
            recv_sem=recv_sem.at[back],
            device_id=(x + ox, y + oy),
            device_id_type=pl.DeviceIdType.MESH,
        )

    for d, (ox, oy) in enumerate(offsets):

        @pl.when(exists(ox, oy))
        def _():
            copy(d).start()

        @pl.when(jnp.logical_not(exists(ox, oy)))
        def _():
            outs[d][...] = jnp.zeros_like(outs[d])

    for c in range(3):
        for j in range(0, field.shape[1], 8):
            moved_full[j : j + 8, c] = field[c, j : j + 8]

    def same(g, carry):
        self_moved(g, slots, moved_full, moved)
        self_bonds(g, shape, flags, moved, done, blocks_of, table)
        return carry

    lax.fori_loop(0, SELF_CHUNKS, same, 0)
    for d, (ox, oy) in enumerate(offsets):

        @pl.when(exists(ox, oy))
        def _():
            copy(d).wait_send()
            copy(offsets.index((-ox, -oy))).wait_recv()


def exchange(blocks, field, slots, shape, flags, tables, offsets, ident):
    n = len(offsets)
    _, tiles, points = field.shape
    return pl.pallas_call(
        functools.partial(exchange_kernel, offsets),
        out_shape=[jax.ShapeDtypeStruct(b.shape, b.dtype) for b in blocks]
        + [jax.ShapeDtypeStruct((3, SELF_CHUNKS * CHUNK, points), F32)],
        in_specs=[VMEM] * (n + 1) + [SMEM] + [VMEM] * 4,
        out_specs=[VMEM] * (n + 1),
        scratch_shapes=[
            pltpu.VMEM((tiles, 8, points), F32),
            pltpu.VMEM((SELF_CHUNKS, 3 * CHUNK, points), F32),
            pltpu.SemaphoreType.DMA((n,)),
            pltpu.SemaphoreType.DMA((n,)),
        ],
        compiler_params=pltpu.CompilerParams(
            collective_id=ident, has_side_effects=True, vmem_limit_bytes=4 * 1024 * 1024
        ),
    )(*blocks, field, slots, shape, flags, *tables)


def tangents(slots, bounds, owner, target, words, tables, shape_full, moved_full, same, swap):
    points = words.shape[2]
    cap = target.shape[0] // 8
    tiles = shape_full.shape[0] // 8 - 9 * cap
    room = -(-(words.shape[0] + CLASSES * (CHUNK - 1)) // LANES) * LANES
    chunks = room // CHUNK
    head = (slots, bounds, owner, target, *tables)
    image_shape = jax.ShapeDtypeStruct((3, tiles, points), F32)
    kept = [
        jax.ShapeDtypeStruct((chunks, 8 * CHUNK, points), F32),
        jax.ShapeDtypeStruct((chunks, 8 * CHUNK, points), jnp.int32),
        pltpu.VMEM((-(-(words.shape[0] + CLASSES * (CHUNK - 1)) // CHUNK), 16 * 5, 8, points), F32),
    ]
    scratch = [
        pltpu.VMEM((chunks, 3 * CHUNK, points), F32),
        pltpu.VMEM((3, room, points), F32),
    ]
    limit = pltpu.CompilerParams(vmem_limit_bytes=8 * 1024 * 1024)
    first_image, field, *rest = pl.pallas_call(
        functools.partial(apply_kernel, True),
        out_shape=[image_shape] * 2 + [jax.ShapeDtypeStruct((3, cap, points), F32)] * 8 + kept,
        in_specs=[SMEM] * 2 + [VMEM] * 8,
        out_specs=[VMEM] * 13,
        scratch_shapes=scratch,
        compiler_params=limit,
    )(*head, words, shape_full, moved_full, same[2])
    image_sends, kept = rest[:8], rest[8:]
    *image_ghosts, done = swap(image_sends, field, slots, same[0], same[1], tables)
    second_image = pl.pallas_call(
        functools.partial(apply_kernel, False),
        out_shape=image_shape,
        in_specs=[SMEM] * 2 + [VMEM] * 17,
        out_specs=VMEM,
        scratch_shapes=[pltpu.VMEM(moved_full.shape, F32)] + scratch,
        compiler_params=limit,
    )(*head, field, *image_ghosts, done, *kept)
    return first_image, second_image


def on_device(jitter, displacement, modulus, start_vec, old_home, ghost_send, pair_list, pair_count, broken):
    tiles = old_home.shape[0]
    points = jitter.shape[2]
    cap = ghost_send.shape[2]
    sends = jnp.transpose(ghost_send, (1, 0, 2))
    turned = lambda value: jnp.transpose(value, (1, 0, 2))
    rows = tiles + 9 * cap
    full = pltpu.VMEM((rows * 8, points), F32)
    tables = all_tables()
    local = [turned(jitter), turned(displacement), modulus, turned(start_vec)]
    inner = [old_home[None, :], *local, pair_list[0]]
    space = lambda value: pltpu.VMEM(value.shape, value.dtype)
    shape_full, moved_full, words, *tables, slots, bounds, owner, target, shape, flags, done = pl.pallas_call(
        gather_kernel,
        out_shape=[full, full] + [space(v) for v in (broken, *tables)]
        + [jax.ShapeDtypeStruct((n, LANES), jnp.int32) for n in (24, 16, 8, 8 * cap)]
        + [jax.ShapeDtypeStruct((SELF_CHUNKS, 8 * CHUNK, points), t) for t in (F32, jnp.int32)]
        + [jax.ShapeDtypeStruct((3, SELF_CHUNKS * CHUNK, points), F32)],
        in_specs=[HBM] * 10 + [SMEM],
        out_specs=[VMEM] * 12,
        scratch_shapes=[space(value) for value in (*local, inner[0], inner[-1])]
        + [
            pltpu.VMEM((2 * tiles, FIELDS * points), BF16),
            pltpu.VMEM((tiles + 8 * cap, FIELDS * points), F32),
            pltpu.VMEM((4, CAP, LANES), F32),
            pltpu.VMEM((4, CAP, LANES), F32),
            pltpu.VMEM((4, FIELDS, CAP, points), F32),
            pltpu.VMEM((4, FIELDS, CAP, points), F32),
            pltpu.VMEM((8, FIELDS, cap, points), F32),
            pltpu.VMEM((8, FIELDS, cap, points), F32),
            pltpu.VMEM((SELF_CHUNKS, 3 * CHUNK, points), F32),
            pltpu.VMEM((16, LANES), jnp.int32),
            pltpu.SMEM((16, LANES), jnp.int32),
            pltpu.VMEM((tiles, 8, points), F32),
            pltpu.VMEM((tiles, 8, points), F32),
            pltpu.VMEM(sends.shape, jnp.int32),
            pltpu.SemaphoreType.DMA((16,)),
            pltpu.SemaphoreType.DMA((16,)),
            pltpu.SemaphoreType.DMA((11,)),
        ],
        compiler_params=pltpu.CompilerParams(
            collective_id=0, has_side_effects=True, vmem_limit_bytes=16 * 1024 * 1024
        ),
    )(*(pltpu.with_memory_space_constraint(v, pltpu.HBM) for v in (*inner, broken, *tables, sends)), pair_count)
    first_image, second_image = tangents(
        slots, bounds, owner, target, words, tables, shape_full, moved_full, (shape, flags, done),
        lambda *args: exchange(*args, AROUND, 1)
    )
    return turned(first_image), turned(second_image)


def solution(mesh):
    split = ("gx", "gy")
    spec3, spec2, spec1 = P(split, None, None), P(split, None), P(split)
    return jax.shard_map(
        on_device,
        mesh=mesh,
        in_specs=(spec3, spec3, spec2, spec3, spec1, spec3, spec3, spec1, spec3),
        out_specs=(spec3, spec3),
        check_vma=False,
    )
```

```python
import functools
import jax
import jax.numpy as jnp
import numpy as np
from jax import lax
from jax.experimental import pallas as pl
from jax.experimental.pallas import tpu as pltpu
from jax.sharding import PartitionSpec as P

CAP = 16
F32 = jnp.float32
BF16 = jnp.bfloat16
VMEM = pl.BlockSpec(memory_space=pltpu.VMEM)
SMEM = pl.BlockSpec(memory_space=pltpu.SMEM)
HBM = pl.BlockSpec(memory_space=pltpu.HBM)
DIRS = (0, 1, 2, 3, 5, 6, 7, 8)
SIDES = ((-1, 0), (1, 0), (0, -1), (0, 1))
AROUND = tuple((e // 3 - 1, e % 3 - 1) for e in DIRS)
CLASSES = 9
FIELDS = 10
SELF_CHUNKS = 4
CHUNK = 16
LANES = 128
FACE_WIDTH = 4
CORNER_WIDTH = 8


def near(dx, dy):
    return max(abs(dx) - 0.4, 0.0) ** 2 + max(abs(dy) - 0.4, 0.0) ** 2 < 9.0


def point(x, y, z):
    return x + 8 * y + 64 * z


HALF = [(dx, dy) for dy in range(4) for dx in range(-3, 4) if (dy > 0 or dx > 0) and near(dx, dy)]
OFFSETS = [(0, 0, 1)] + [(dx, dy, f) for dx, dy in HALF for f in (0, 1)]


def self_tables():
    sel = np.zeros((2 * LANES, len(OFFSETS) * LANES), np.float32)
    bits = np.zeros((-(-2 * len(OFFSETS) // 8) * 8, LANES), np.int32)
    for n, (dx, dy, f) in enumerate(OFFSETS):
        for lane in range(LANES):
            x, y, z = lane % 8, lane // 8 % 8, lane // 64
            if 0 <= x + dx < 8 and 0 <= y + dy < 8:
                for half in (0, LANES):
                    sel[half + point(x + dx, y + dy, z ^ f), n * LANES + lane] += 1
                    sel[half + lane, n * LANES + lane] -= 1
                bits[2 * n, lane] = 1 << (x + dx + 8 * (z ^ f))
            if 0 <= x - dx < 8 and 0 <= y - dy < 8:
                bits[2 * n + 1, lane] = 1 << (x - dx + 8 * (z ^ f))
    return sel, bits


OFFSET_LANES = (27, 28, 35)
NEAR = [(7, 0), (7, 1), (6, 0), (7, 2), (6, 1), (5, 0)]
FAR = [(7, 0, 2), (7, 1, 2), (6, 0, 2), (7, 0, 3), (7, 0, -2), (7, 1, -2), (6, 0, -2), (7, 0, -3)]


def fill(sel, col, a, b, shift):
    for half in (0, LANES):
        sel[half + point(*b), col] += 1
        sel[half + point(*a), col] -= 1
        for c in range(3):
            sel[half + OFFSET_LANES[c], col] = b[c] - a[c] + shift[c]


def face_tables():
    sels = np.zeros((4, 2 * LANES, 8 * LANES), np.float32)
    backs = np.zeros((4, 2 * LANES, LANES), np.float32)
    tabs = np.zeros((4, 16, LANES), np.int32)
    for k in range(4):
        axis, sign = k // 2, 1 - 2 * (k % 2)
        side = lambda u: u if sign > 0 else 7 - u
        place = lambda u, t, z: (u, t, z) if axis == 0 else (t, u, z)
        shift = place(8 * sign, 0, 0)
        sel, back, tab = sels[k], backs[k], tabs[k]
        for z in range(2):
            for t in range(8):
                for c in range(8):
                    lane = point(*place(c, t, z))
                    ua, ub, dt = FAR[c]
                    a = place(side(ua), t, z)
                    tab[9, lane] = point(*a)
                    tab[12, lane] = ub
                    tab[13, lane] = dt
                    back[LANES + lane, point(*a)] = 1
                    todo = [(6 + f, f, a, ub, dt) for f in range(2)]
                    if c < len(NEAR):
                        ua, ub = NEAR[c]
                        a = place(side(ua), t, z)
                        tab[8, lane] = point(*a)
                        tab[11, lane] = ub
                        back[lane, point(*a)] = 1
                        todo += [(2 * m + f, f, a, ub, m - 1) for m in range(3) for f in range(2)]
                    for v, f, a, ub, dt in todo:
                        if 0 <= t + dt < 8:
                            b = place(side(ub), t + dt, z ^ f)
                            fill(sel, v * LANES + lane, a, b, shift)
                            tab[v, lane] = 1 << (b[0] + 8 * b[2])
                for u in range(3):
                    tab[10, point(*place(side(7 - u), t, z))] = 1
                    tab[10, point(*place(side(u), t, z))] = 2
        for col in range(8 * LANES):
            if not sel[:, col].any():
                sel[OFFSET_LANES[0], col] = 4
    return sels, backs, tabs


def corner_tables():
    sels = np.zeros((4, 2 * LANES, LANES), np.float32)
    backs = np.zeros((4, 2 * LANES, LANES), np.float32)
    tabs = np.zeros((4, 8, LANES), np.int32)
    combos = []
    for (ua, ub) in NEAR:
        for (va, vb) in NEAR:
            if near(ub + 8 - ua, vb + 8 - va):
                combos.append((ua, va, ub, vb))
    for k in range(4):
        sign_x, sign_y = 1 - 2 * (k // 2), 1 - 2 * (k % 2)
        side_x = lambda u: u if sign_x > 0 else 7 - u
        side_y = lambda u: u if sign_y > 0 else 7 - u
        sel, back, tab = sels[k], backs[k], tabs[k]
        for n, (ua, va, ub, vb) in enumerate(combos):
            for z in range(2):
                for f in range(2):
                    lane = n + 16 * z + 32 * f
                    a, b = (side_x(ua), side_y(va), z), (side_x(ub), side_y(vb), z ^ f)
                    fill(sel, lane, a, b, (8 * sign_x, 8 * sign_y, 0))
                    back[lane, point(*a)] = 1
                    back[LANES + lane, point(*a)] = 1
                    tab[0, lane] = 1 << (b[0] + 8 * b[2])
                    tab[1, lane] = point(*a)
                    tab[3, lane] = vb
        for col in range(LANES):
            if not sel[:, col].any():
                sel[OFFSET_LANES[0], col] = 4
        for z in range(2):
            for u in range(3):
                for v in range(3):
                    tab[2, point(side_x(7 - u), side_y(7 - v), z)] = 1
                    tab[2, point(side_x(u), side_y(v), z)] = 2
    return sels, backs, tabs


SELF_AT = 0
FACE_AT = SELF_AT + len(OFFSETS)
FACE_BACK = FACE_AT + 4 * 8
CORNER_AT = FACE_BACK + 4
CORNER_BACK = CORNER_AT + 4
SELF_ROW = 0
FACE_ROW = SELF_ROW + -(-2 * len(OFFSETS) // 8) * 8
CORNER_ROW = FACE_ROW + 4 * 16
CODE_ROW = CORNER_ROW + 4 * 8


def all_tables():
    sel0, bits0 = self_tables()
    sel1, back1, tab1 = face_tables()
    sel2, back2, tab2 = corner_tables()
    blocks = [sel0[:, n * LANES : (n + 1) * LANES] for n in range(len(OFFSETS))]
    blocks += [sel1[k, :, n * LANES : (n + 1) * LANES] for k in range(4) for n in range(8)]
    blocks += list(back1) + list(sel2) + list(back2)
    rows = [bits0, tab1.reshape(-1, LANES), tab2.reshape(-1, LANES), tab1[:, 10], tab2[:, 2]]
    return jnp.asarray(np.stack(blocks), BF16), jnp.asarray(np.concatenate(rows, axis=0))


def split(value):
    high = value.astype(BF16)
    return high, (value - high.astype(F32)).astype(BF16)


def bond_shape(xi, y, moduli, keep):
    r2 = xi[0] * xi[0] + xi[1] * xi[1] + xi[2] * xi[2]
    l2 = y[0] * y[0] + y[1] * y[1] + y[2] * y[2]
    c = moduli * jnp.maximum(9.0 - r2, 0.0)
    if keep is not None:
        c = jnp.where(keep, c, 0.0)
    r_inv = lax.rsqrt(r2)
    l_inv = lax.rsqrt(l2)
    cl = c * l_inv
    return [c * r_inv - cl, cl * (l_inv * l_inv), *y]


def bond_pull(held, dv):
    k2, stretch, *y = held
    along = stretch * (y[0] * dv[0] + y[1] * dv[1] + y[2] * dv[2])
    return [k2 * dv[i] + along * y[i] for i in range(3)]


def bond_force(xi, y, moduli, dv, keep):
    return bond_pull(bond_shape(xi, y, moduli, keep), dv)


def kinds_of(pairs, count):
    sx, sy = pairs[2:3], pairs[3:4]
    flat_x = jnp.where(sx > 0, 1, 2)
    flat_y = jnp.where(sy > 0, 3, 4)
    slant = jnp.where(sx < 0, 7, 5) + jnp.where(sy < 0, 1, 0)
    kind = jnp.where(sx == 0, jnp.where(sy == 0, 0, flat_y), jnp.where(sy == 0, flat_x, slant))
    return jnp.where(lax.broadcasted_iota(jnp.int32, kind.shape, 1) < count[0], kind, 15)


def plan_words(pairs, count, slots):
    total = pairs.shape[1]
    lanes = lambda shape, axis: lax.broadcasted_iota(jnp.int32, shape, axis)
    kind = kinds_of(pairs, count)
    eight = (8, total)
    high_row = lanes(eight, 0) < 4
    tile = jnp.broadcast_to(pairs[0:1], eight)
    turned = jnp.transpose(jnp.where(high_row, jnp.broadcast_to(kind, eight), tile))
    early = (lanes((total, total), 0) < lanes((total, total), 1)) & (turned[:, 0:1] == kind)
    at = jnp.sum(jnp.where(early, 1, 0), axis=0, keepdims=True)
    start = jnp.zeros((1, 1), jnp.int32)
    for c in range(CLASSES):
        member = jnp.where(kind == c, 1, 0)
        at = at + member * start
        size = jnp.sum(member, axis=1, keepdims=True)
        start = start + (jnp.right_shift(size + (CHUNK - 1), 4) << 4)
    at = jnp.where(kind < CLASSES, at, -1)
    at = jnp.transpose(jnp.broadcast_to(at, eight))[:, 0:1]
    slots[...] = jnp.zeros_like(slots)
    for b in range(-(-(total + CLASSES * (CHUNK - 1)) // LANES)):
        hit = at == lanes((total, LANES), 1) + b * LANES
        slots[b : b + 1] = jnp.sum(jnp.where(hit, lanes((total, LANES), 0), 0), axis=0, keepdims=True)
        if b == 0:
            slots[8:9] = jnp.sum(jnp.where(hit, turned[:, 4:5], 0), axis=0, keepdims=True)


def tile_of(row, ref):
    if len(ref.shape) == 3:
        return ref[row]
    return ref[pl.ds(pl.multiple_of(row * 8, 8), 8)]


def packed(words, q):
    word = words[q]
    return jnp.bitwise_not(word[0:8] | jnp.left_shift(word[8:16], 8))


def slot_at(slots, kind, g, u):
    return slots[8 * kind + jnp.right_shift(g, 3), (g & 7) * CHUNK + u]


def self_shape(g, slots, shape_full, shape):
    for u in range(CHUNK):
        shape[g, pl.ds(u, 8, stride=CHUNK)] = tile_of(slot_at(slots, 1, g, u), shape_full)


def put_flags(g, slots, words, flags):
    for u in range(CHUNK):
        flags[g, pl.ds(u, 8, stride=CHUNK)] = packed(words, slot_at(slots, 0, g, u))


def self_moved(g, slots, moved_full, moved):
    for u in range(CHUNK):
        moved[g, pl.ds(u, 3, stride=CHUNK)] = tile_of(slot_at(slots, 1, g, u), moved_full)[0:3]


def flag_rows(flags, g, h, y):
    start = y * CHUNK + 8 * h
    if not isinstance(start, int):
        start = pl.multiple_of(start, 8)
    return flags[g, pl.ds(start, 8)]


def turned_rows(flags, g, h):
    lane_y = lax.broadcasted_iota(jnp.int32, (8, LANES), 1) // 8 % 8
    held = [flag_rows(flags, g, h, y) for y in range(8)]
    for bit in (1, 2, 4):
        odd = (lane_y & bit) != 0
        held = [jnp.where(odd, held[(s + bit) % 8], held[s]) for s in range(8)]
    return held


def left_of(shape, moved, g):
    values = [] if shape is None else [shape[g, c * CHUNK : (c + 1) * CHUNK] for c in range(7)]
    values += [moved[g, c * CHUNK : (c + 1) * CHUNK] for c in range(3)]
    parts = [split(v) for v in values]
    high = jnp.concatenate([p[0] for p in parts], axis=0)
    low = jnp.concatenate([p[1] for p in parts], axis=0)
    return jnp.concatenate([high, low], axis=1)


def block(wide, c, h, v):
    return wide[c * CHUNK + 8 * h : c * CHUNK + 8 * h + 8, v * LANES : (v + 1) * LANES]


def joined_blocks(blocks_of, at):
    return jnp.concatenate([blocks_of[at], blocks_of[at + 1]], axis=1)


def store(force, g, c, value):
    force[c, pl.ds(pl.multiple_of(g * CHUNK, CHUNK), CHUNK)] = value


def self_bonds(g, shape, flags, moved, force, blocks_of, table):
    eight = (8, LANES)
    low_z = lax.broadcasted_iota(jnp.int32, eight, 1) < 64
    left = left_of(shape, moved, g)
    words_of = [turned_rows(flags, g, h) for h in range(2)]
    twice = [2.0 * shape[g, 6 * CHUNK + 8 * h : 6 * CHUNK + 8 * h + 8] for h in range(2)]
    acc = [[jnp.zeros(eight, F32)] * 3 for _ in range(2)]
    other = jnp.where(low_z, 1.0, -1.0)
    row_of = lambda at: jnp.broadcast_to(table[at : at + 1], eight)
    for start in range(0, len(OFFSETS), 2):
        some = OFFSETS[start : start + 2]
        right = joined_blocks(blocks_of, SELF_AT + start) if len(some) == 2 else blocks_of[SELF_AT + start]
        wide = jnp.dot(left, right, preferred_element_type=F32)
        for v, (dx, dy, f) in enumerate(some):
            n = start + v
            base = (float(dx), float(dy), other if f else 0.0)
            for h in range(2):
                part = lambda c: block(wide, c, h, v)
                xi = [part(c) + base[c] for c in range(3)]
                y = [part(3 + c) + base[c] for c in range(3)]
                dv = [part(7 + c) for c in range(3)]
                term = bond_force(xi, y, part(6) + twice[h], dv, None)
                keep = (words_of[h][dy % 8] & row_of(SELF_ROW + 2 * n)) != 0
                acc[h] = [acc[h][i] + jnp.where(keep, term[i], 0.0) for i in range(3)]
                if (dx, dy) != (0, 0):
                    keep = (words_of[h][-dy % 8] & row_of(SELF_ROW + 2 * n + 1)) != 0
                    off = (dx + 8 * dy + 64 * f) % LANES
                    acc[h] = [acc[h][i] - jnp.where(keep, pltpu.roll(term[i], off, 1), 0.0) for i in range(3)]
    for c in range(3):
        store(force, g, c, jnp.concatenate([acc[0][c], acc[1][c]], axis=0))


def plan(pairs, count, slots, bounds, owner):
    total = pairs.shape[1]
    lanes = lambda shape, axis: lax.broadcasted_iota(jnp.int32, shape, axis)
    one = (1, total)
    wide = (16, total)
    tile, partner = pairs[0:1], pairs[1:2]
    slot = lanes(one, 1)
    kind = kinds_of(pairs, count)
    member = jnp.where(lanes(wide, 0) == kind, 1.0, 0.0)
    early = jnp.where(lanes((total, total), 0) < lanes((total, total), 1), 1.0, 0.0).astype(BF16)
    rank = jnp.dot(member.astype(BF16), early, preferred_element_type=F32)
    chunks = jnp.floor((jnp.sum(member, axis=1, keepdims=True) + float(CHUNK - 1)) * (1.0 / CHUNK))
    chunks = jnp.broadcast_to(chunks, (16, LANES))
    start = jnp.zeros((16, LANES), F32)
    for c in range(CLASSES):
        start = start + jnp.where(lanes((16, LANES), 0) > c, chunks[c : c + 1], 0.0)
    bounds[...] = start.astype(jnp.int32)
    at = rank + float(CHUNK) * jnp.broadcast_to(start[:, 0:1], wide)
    at = jnp.sum(member * at, axis=0, keepdims=True)
    at = jnp.where(kind < CLASSES, at, -1.0)
    at = jnp.transpose(jnp.broadcast_to(at, (8, total)))[:, 0:1]
    low = lambda value: (value & 255).astype(F32)
    high = lambda value: jnp.right_shift(value, 8).astype(F32)
    rows = [low(slot), high(slot), tile.astype(F32), low(partner), high(partner), jnp.ones(one, F32)]
    rows = jnp.concatenate(rows + [jnp.zeros((10, total), F32)], axis=0).astype(BF16)
    slots[...] = jnp.zeros_like(slots)
    owner[...] = jnp.full_like(owner, -1)
    for b in range(-(-(total + CLASSES * (CHUNK - 1)) // LANES)):
        here = (lanes((total, LANES), 1) + b * LANES).astype(F32)
        hit = jnp.where(jnp.broadcast_to(at, (total, LANES)) == here, 1.0, 0.0).astype(BF16)
        out = jnp.dot(rows, hit, preferred_element_type=F32).astype(jnp.int32)
        slots[b : b + 1] = out[0:1] + 256 * out[1:2]
        slots[8 + b : 9 + b] = out[2:3]
        slots[16 + b : 17 + b] = out[3:4] + 256 * out[4:5]
        owner[b : b + 1] = out[2:3] + out[5:6] - 1


def gather_kernel(*refs):
    far, count = refs[:10], refs[10]
    (shape_full, moved_full), near_copy, (slots, bounds, owner, target) = refs[11:13], refs[13:15], refs[15:19]
    shape, flags, done, words, refs = *refs[19:22], refs[22], refs[23:]
    near_copy = (words,) + near_copy
    jit, disp, mod, vec, home, pairs, state, own, wanted, asked, hand, arrived, ghost, landed, moved, own_slots, near_slots = refs[:17]
    shape_own, moved_own, sending, sent, got, fetched = refs[17:]
    fetches = [
        pltpu.make_async_copy(a, b, fetched.at[n]) for n, (a, b) in enumerate(zip(far, (home, jit, disp, mod, vec, pairs) + near_copy + (sending,)))
    ]
    for fetch in fetches:
        fetch.start()
    n_x, n_y = lax.axis_size("gx"), lax.axis_size("gy")
    x, y = lax.axis_index("gx"), lax.axis_index("gy")
    tiles, points = mod.shape
    cap = landed.shape[2]

    def exists(offset):
        ox, oy = offset
        return (x + ox >= 0) & (x + ox < n_x) & (y + oy >= 0) & (y + oy < n_y)

    barrier = pltpu.get_barrier_semaphore()
    for offset in AROUND:

        @pl.when(exists(offset))
        def _():
            pl.semaphore_signal(
                barrier, inc=1, device_id=(x + offset[0], y + offset[1]), device_id_type=pl.DeviceIdType.MESH
            )

    pl.semaphore_wait(barrier, sum(jnp.where(exists(offset), 1, 0) for offset in AROUND))

    def copy(offsets, base, source_ref, target_ref, d):
        ox, oy = offsets[d]
        back = offsets.index((-ox, -oy))
        return pltpu.make_async_remote_copy(
            src_ref=source_ref.at[d],
            dst_ref=target_ref.at[back],
            send_sem=sent.at[base + d],
            recv_sem=got.at[base + back],
            device_id=(x + ox, y + oy),
            device_id_type=pl.DeviceIdType.MESH,
        )

    def start(*args):
        for d, offset in enumerate(args[0]):

            @pl.when(exists(offset))
            def _():
                copy(*args, d).start()

    def finish(*args):
        for d, (ox, oy) in enumerate(args[0]):

            @pl.when(exists((ox, oy)))
            def _():
                copy(*args, d).wait_send()
                copy(*args, args[0].index((-ox, -oy))).wait_recv()

    def lanes(shape, axis=1):
        return lax.broadcasted_iota(jnp.int32, shape, axis)

    def column(row):
        return jnp.transpose(jnp.broadcast_to(row, (LANES, LANES)))

    fetches[0].wait()
    anchor = jnp.right_shift(home[...], tiles.bit_length() - 1)
    off_x = jnp.right_shift(anchor, n_y.bit_length() - 1) - x
    off_y = (anchor & (n_y - 1)) - y
    side = jnp.where(off_x == -1, 0, jnp.where(off_x == 1, 1, jnp.where(off_y == -1, 2, jnp.where(off_y == 1, 3, 4))))
    square = (LANES, LANES)
    early = jnp.where(lanes(square, 0) < lanes(square), 1.0, 0.0).astype(BF16)
    member = jnp.where(lanes((CAP, LANES), 0) == jnp.broadcast_to(side, (CAP, LANES)), 1.0, 0.0)
    rank = jnp.dot(member.astype(BF16), early, preferred_element_type=F32)
    cell = jnp.sum(jnp.where(lanes((CAP, LANES), 0) < 4, member, 0.0) * rank, axis=0, keepdims=True)
    cell = jnp.where(side < 4, cell + (side * CAP).astype(F32), -1.0)
    old_slot = (home[...] & (tiles - 1)).astype(F32)
    origin = jnp.where(side < 4, cell + float(tiles), old_slot)
    ask = lanes((4 * CAP, LANES), 0).astype(F32) == cell
    ask = jnp.sum(jnp.where(ask, old_slot, 0.0), axis=1, keepdims=True)
    for d in range(4):
        wanted[d] = jnp.broadcast_to(ask[d * CAP : (d + 1) * CAP], (CAP, LANES))
    asking = (SIDES, 0, wanted, asked)
    handing = (SIDES, 4, hand, arrived)
    ghosting = (AROUND, 8, ghost, landed)
    start(*asking)
    for offsets, refs in ((SIDES, (asked, arrived)), (AROUND, (landed,))):
        for d, offset in enumerate(offsets):

            @pl.when(jnp.logical_not(exists(offset)))
            def _():
                for ref in refs:
                    ref[d] = jnp.zeros_like(ref[d])

    for fetch in fetches[1:5]:
        fetch.wait()
    for c in range(FIELDS):
        if c < 3:
            value = jit[c]
        elif c < 6:
            value = jit[c - 3] + disp[c - 3]
        elif c == 6:
            value = mod[...] * (0.05 / 9.0)
        else:
            value = vec[c - 7]
        high, low = split(value)
        state[0:tiles, c * points : (c + 1) * points] = high
        state[tiles : 2 * tiles, c * points : (c + 1) * points] = low

    def hot(index, base, width):
        ids = (lanes(index.shape) & (width - 1)) + base
        return jnp.where(index == ids.astype(F32), 1.0, 0.0).astype(BF16)

    def twice(value):
        return jnp.concatenate([value, value], axis=1)

    fetches[9].wait()
    corner_of = lanes((cap, cap), 0) == lanes((cap, cap))
    sent_tile = []
    for e in DIRS:
        row = jnp.maximum(jnp.broadcast_to(sending[e], (cap, cap)), 0).astype(F32)
        row = jnp.sum(jnp.where(corner_of, row, 0.0), axis=1, keepdims=True)
        sent_tile.append(jnp.broadcast_to(row, (cap, LANES)))
    sent_tile = jnp.concatenate(sent_tile, axis=0)
    target[...] = sent_tile.astype(jnp.int32)
    sent_from = jnp.where(sent_tile == lanes(square).astype(F32), origin, 0.0)
    sent_from = jnp.broadcast_to(jnp.sum(sent_from, axis=1, keepdims=True), square)
    source = jnp.concatenate([column(origin), sent_from], axis=0)
    finish(*asking)
    left = twice(jnp.concatenate([hot(asked[d], 0, tiles) for d in range(4)], axis=0))
    for p in range(FIELDS // 2):
        out = jnp.dot(left, state[:, 2 * p * points : 2 * (p + 1) * points], preferred_element_type=F32)
        for f in range(2):
            for d in range(4):
                hand[d, 2 * p + f] = out[d * CAP : (d + 1) * CAP, f * points : (f + 1) * points]
    start(*handing)
    left = twice(hot(source, 0, tiles))
    for p in range(FIELDS // 2):
        at = slice(2 * p * points, 2 * (p + 1) * points)
        own[:, at] = jnp.dot(left, state[:, at], preferred_element_type=F32)
    finish(*handing)
    left = hot(source, tiles, 4 * CAP)
    right = []
    for c in range(FIELDS):
        right.append(jnp.concatenate(split(jnp.concatenate([arrived[d, c] for d in range(4)], axis=0)), axis=0))

    def settled(low_row, p):
        rows = slice(low_row, low_row + tiles)
        both = jnp.concatenate([right[2 * p], right[2 * p + 1]], axis=1)
        return own[rows, 2 * p * points : 2 * (p + 1) * points] + jnp.dot(left[rows], both, preferred_element_type=F32)

    for p in range(FIELDS // 2):
        out = settled(tiles, p)
        for f in range(2):
            for n in range(8):
                ghost[n, 2 * p + f] = out[n * cap : (n + 1) * cap, f * points : (f + 1) * points]
    start(*ghosting)
    fetches[5].wait()
    plan(pairs, count, slots, bounds, owner)
    plan_words(pairs, count, own_slots)
    placing = pltpu.make_async_copy(own_slots, near_slots, fetched.at[10])
    placing.start()

    def spread(row, c, value):
        target = shape_full if c < 7 else moved_full
        for j in range(0, value.shape[0], 8):
            target[pl.ds((row + j) * 8 + c % 7, 8, stride=8)] = value[j : j + 8]

    for p in range(FIELDS // 2):
        out = settled(0, p)
        for f in range(2):
            value = out[:, f * points : (f + 1) * points]
            spread(0, 2 * p + f, value)
            own_tiles = shape_own if 2 * p + f < 7 else moved_own
            own_tiles[:, (2 * p + f) % 7] = value
    placing.wait()
    for fetch in fetches[6:9]:
        fetch.wait()
    _, blocks_of, table = near_copy

    def same(g, carry):
        self_shape(g, near_slots, shape_own, shape)
        put_flags(g, near_slots, words, flags)
        self_moved(g, near_slots, moved_own, moved)
        self_bonds(g, shape, flags, moved, done, blocks_of, table)
        return carry

    def flagged(g, carry):
        put_flags(g, near_slots, words, flags)
        return carry

    lax.fori_loop(0, SELF_CHUNKS, same, 0)
    lax.fori_loop(SELF_CHUNKS, flags.shape[0], flagged, 0)
    finish(*ghosting)
    for n, e in enumerate(DIRS):
        for c in range(FIELDS):
            spread(tiles + e * cap, c, landed[n, c])


def apply_kernel(first, slots, starts, owner, target, blocks_of, table, flags, *rest):
    if first:
        shape_full, moved_full, done, image, echo, sends, shape, geometry, moved, force = *rest[:5], rest[5:13], *rest[13:]
    else:
        field, field_ghosts, done, shape, geometry, image, moved_full, moved, force = rest[0], rest[1:9], *rest[9:]
    _, rows, points = image.shape
    bounds = [starts[c, 0] for c in range(CLASSES + 1)]
    if first:
        cap = sends[0].shape[1]
    else:
        cap = field_ghosts[0].shape[1]
        for c in range(3):
            for j in range(0, rows, 8):
                moved_full[pl.ds(j * 8 + c, 8, stride=8)] = field[c, j : j + 8]
            for e, ghost in zip(DIRS, field_ghosts):
                for j in range(0, cap, 8):
                    moved_full[pl.ds((rows + e * cap + j) * 8 + c, 8, stride=8)] = ghost[c, j : j + 8]

    lane = lax.broadcasted_iota(jnp.int32, (8, points), 1)
    sub = lax.broadcasted_iota(jnp.int32, (8, points), 0)
    unit = jnp.zeros((8, points), F32)
    for c in range(6):
        unit = jnp.where((sub == c) & (lane == OFFSET_LANES[c % 3]), 1.0, unit)
    turn = jnp.where(sub == 6, -1.0, 1.0)

    def build(g, carry):
        k = sum(jnp.where(g >= bounds[c], 1, 0) for c in range(2, 9))
        held = jnp.broadcast_to(table[pl.ds(CODE_ROW + k, 1)], (8, points))
        take_a, take_b = held == 1, held == 2
        block_of = jnp.right_shift(g, 3)
        base = (g & 7) * CHUNK
        for u in range(CHUNK):
            tile, partner = slots[8 + block_of, base + u], slots[16 + block_of, base + u]
            if first:
                state = jnp.where(take_b, tile_of(partner, shape_full), unit)
                shape[g, pl.ds(u, 8, stride=CHUNK)] = jnp.where(take_a, tile_of(tile, shape_full) * turn, state)
            state = jnp.where(take_a, tile_of(tile, moved_full), jnp.where(take_b, tile_of(partner, moved_full), 0.0))
            moved[g, pl.ds(u, 3, stride=CHUNK)] = state[0:3]
        return carry

    def build_same(g, carry):
        if first:
            self_shape(g, slots, shape_full, shape)
        self_moved(g, slots, moved_full, moved)
        return carry

    force[:, 0 : SELF_CHUNKS * CHUNK] = done[...]
    lax.fori_loop(SELF_CHUNKS, bounds[1], build_same, 0)
    lax.fori_loop(bounds[1], bounds[9], build, 0)

    def row_of(at):
        return jnp.broadcast_to(table[pl.ds(at, 1)], (8, points))

    two_blocks = functools.partial(joined_blocks, blocks_of)

    def pick(value, index):
        return jnp.take_along_axis(value, index, axis=1, mode="promise_in_bounds")

    word_of = functools.partial(flag_rows, flags)
    by_row = functools.partial(turned_rows, flags)
    put = functools.partial(store, force)

    def same_tile(g, carry):
        self_bonds(g, shape, flags, moved, force, blocks_of, table)
        return carry

    lax.fori_loop(SELF_CHUNKS, bounds[1], same_tile, 0)

    def of_block(g, at, wide, h, v, keep):
        if not first:
            return bond_pull([geometry[g, 5 * at + n] for n in range(5)], [block(wide, c, h, v) for c in range(3)])
        part = lambda c: block(wide, c, h, v)
        held = bond_shape([part(c) for c in range(3)], [part(3 + c) for c in range(3)], part(6), keep)
        for n in range(5):
            geometry[g, 5 * at + n] = held[n]
        return bond_pull(held, [part(7 + c) for c in range(3)])

    def left_side(g):
        return left_of(shape if first else None, moved, g)

    def face_words(axis, k, g):
        index_near = row_of(FACE_ROW + 16 * k + 8)
        index_far = row_of(FACE_ROW + 16 * k + 9)
        near_words, far_words = [], []
        for h in range(2):
            if axis == 0:
                rel = by_row(g, h)
                dt = row_of(FACE_ROW + 16 * k + 13)
                near_words.append([pick(rel[(m - 1) % 8], index_near) for m in range(3)])
                chosen = pick(rel[2], index_far)
                for d in (3, -2, -3):
                    chosen = jnp.where(dt == d, pick(rel[d % 8], index_far), chosen)
                far_words.append(chosen)
            else:
                for at, index, into in ((11, index_near, near_words), (12, index_far, far_words)):
                    row = row_of(FACE_ROW + 16 * k + at)
                    chosen = None
                    for j in range(3):
                        word = pick(word_of(g, h, jnp.where(k == 3, 7 - j, j)), index)
                        chosen = word if j == 0 else jnp.where(row == j, word, chosen)
                    into.append([chosen] * 3 if at == 11 else chosen)
        return near_words, far_words

    def face(axis, g):
        if first:
            k = 2 * axis + jnp.where(g >= bounds[2 * axis + 2], 1, 0)
            near_words, far_words = face_words(axis, k, g)
        else:
            k = sum(jnp.where(g >= bounds[c], 1, 0) for c in (2, 3, 4))
        left = left_side(g)
        close = [[jnp.zeros((8, points), F32)] * 3 for _ in range(2)]
        distant = [[jnp.zeros((8, points), F32)] * 3 for _ in range(2)]
        for m in range(4):
            wide = jnp.dot(left, two_blocks(FACE_AT + 8 * k + 2 * m), preferred_element_type=F32)
            for f in range(2):
                for h in range(2):
                    keep = None
                    if first:
                        word = near_words[h][m] if m < 3 else far_words[h]
                        keep = (word & row_of(FACE_ROW + 16 * k + 2 * m + f)) != 0
                    term = of_block(g, 4 * m + 2 * f + h, wide, h, f, keep)
                    acc = close if m < 3 else distant
                    acc[h] = [acc[h][i] + term[i] for i in range(3)]
        total = []
        for acc in (close, distant):
            stacked = jnp.concatenate([acc[h][c] for c in range(3) for h in range(2)], axis=0)
            high, low = split(stacked)
            total.append(jnp.concatenate([high, low], axis=0))
        back = jnp.dot(jnp.concatenate(total, axis=1), blocks_of[FACE_BACK + k], preferred_element_type=F32)
        for c in range(3):
            at = c * CHUNK
            put(g, c, back[at : at + CHUNK] + back[3 * CHUNK + at : 3 * CHUNK + at + CHUNK])

    def corner(g):
        k = sum(jnp.where(g >= bounds[c], 1, 0) for c in (6, 7, 8))
        left = left_side(g)
        if first:
            index = row_of(CORNER_ROW + 8 * k + 1)
            row = row_of(CORNER_ROW + 8 * k + 3)
        wide = jnp.dot(left, blocks_of[CORNER_AT + k], preferred_element_type=F32)
        terms = []
        for h in range(2):
            keep = None
            if first:
                for j in range(3):
                    word = pick(word_of(g, h, jnp.where((k & 1) == 1, 7 - j, j)), index)
                    chosen = word if j == 0 else jnp.where(row == j, word, chosen)
                keep = (chosen & row_of(CORNER_ROW + 8 * k)) != 0
            terms.append(of_block(g, h, wide, h, 0, keep))
        stacked = jnp.concatenate([terms[h][c] for c in range(3) for h in range(2)], axis=0)
        back = jnp.dot(jnp.concatenate(split(stacked), axis=1), blocks_of[CORNER_BACK + k], preferred_element_type=F32)
        for c in range(3):
            put(g, c, back[c * CHUNK : (c + 1) * CHUNK])

    def over(low, high, width, body):
        def step(i, carry):
            for u in range(width):
                body(jnp.minimum(low + i * width + u, high - 1))
            return carry

        lax.fori_loop(0, (high - low + width - 1) // width, step, 0)

    if first:
        over(bounds[1], bounds[3], FACE_WIDTH, functools.partial(face, 0))
        over(bounds[3], bounds[5], FACE_WIDTH, functools.partial(face, 1))
    else:
        over(bounds[1], bounds[5], FACE_WIDTH, functools.partial(face, None))
    over(bounds[5], bounds[9], CORNER_WIDTH, corner)

    blocks = (bounds[9] * CHUNK + LANES - 1) // LANES

    def clear(g, carry):
        for c in range(3):
            put(g, c, jnp.zeros((CHUNK, points), F32))
        return carry

    lax.fori_loop(bounds[9], blocks * (LANES // CHUNK), clear, 0)
    image[...] = jnp.zeros_like(image)
    if first:
        for out in sends:
            out[...] = jnp.zeros_like(out)
    tile_at = lax.broadcasted_iota(jnp.int32, (rows, LANES), 0)
    if first:
        tile_at = jnp.concatenate([tile_at, target[...]], axis=0)

    def gather_tiles(b, carry):
        hot = jnp.where(tile_at == owner[pl.ds(b, 1)], 1.0, 0.0).astype(BF16)
        parts = [split(force[c, pl.ds(pl.multiple_of(b * LANES, LANES), LANES)]) for c in range(3)]
        high = jnp.concatenate([p[0] for p in parts], axis=1)
        low = jnp.concatenate([p[1] for p in parts], axis=1)
        out = jnp.dot(
            jnp.concatenate([hot, hot], axis=1), jnp.concatenate([high, low], axis=0), preferred_element_type=F32
        )
        for c in range(3):
            image[c] += out[:rows, c * points : (c + 1) * points]
            if first:
                for n, send in enumerate(sends):
                    send[c] += out[rows + n * cap : rows + (n + 1) * cap, c * points : (c + 1) * points]
        return carry

    lax.fori_loop(0, blocks, gather_tiles, 0)
    if first:
        echo[...] = image[...]


def exchange_kernel(offsets, *refs):
    n = len(offsets)
    ins, (field, slots, shape, flags, blocks_of, table), refs = refs[:n], refs[n : n + 6], refs[n + 6 :]
    outs, (done, moved_full, moved, send_sem, recv_sem) = refs[:n], refs[n:]
    n_x, n_y = lax.axis_size("gx"), lax.axis_size("gy")
    x, y = lax.axis_index("gx"), lax.axis_index("gy")

    def exists(ox, oy):
        return (x + ox >= 0) & (x + ox < n_x) & (y + oy >= 0) & (y + oy < n_y)

    barrier = pltpu.get_barrier_semaphore()
    for ox, oy in offsets:

        @pl.when(exists(ox, oy))
        def _():
            pl.semaphore_signal(
                barrier, inc=1, device_id=(x + ox, y + oy), device_id_type=pl.DeviceIdType.MESH
            )

    peers = sum(jnp.where(exists(ox, oy), 1, 0) for ox, oy in offsets)
    pl.semaphore_wait(barrier, peers)

    def copy(d):
        ox, oy = offsets[d]
        back = offsets.index((-ox, -oy))
        return pltpu.make_async_remote_copy(
            src_ref=ins[d],
            dst_ref=outs[back],
            send_sem=send_sem.at[d],
            recv_sem=recv_sem.at[back],
            device_id=(x + ox, y + oy),
            device_id_type=pl.DeviceIdType.MESH,
        )

    for d, (ox, oy) in enumerate(offsets):

        @pl.when(exists(ox, oy))
        def _():
            copy(d).start()

        @pl.when(jnp.logical_not(exists(ox, oy)))
        def _():
            outs[d][...] = jnp.zeros_like(outs[d])

    for c in range(3):
        for j in range(0, field.shape[1], 8):
            moved_full[j : j + 8, c] = field[c, j : j + 8]

    def same(g, carry):
        self_moved(g, slots, moved_full, moved)
        self_bonds(g, shape, flags, moved, done, blocks_of, table)
        return carry

    lax.fori_loop(0, SELF_CHUNKS, same, 0)
    for d, (ox, oy) in enumerate(offsets):

        @pl.when(exists(ox, oy))
        def _():
            copy(d).wait_send()
            copy(offsets.index((-ox, -oy))).wait_recv()


def exchange(blocks, field, slots, shape, flags, tables, offsets, ident):
    n = len(offsets)
    _, tiles, points = field.shape
    return pl.pallas_call(
        functools.partial(exchange_kernel, offsets),
        out_shape=[jax.ShapeDtypeStruct(b.shape, b.dtype) for b in blocks]
        + [jax.ShapeDtypeStruct((3, SELF_CHUNKS * CHUNK, points), F32)],
        in_specs=[VMEM] * (n + 1) + [SMEM] + [VMEM] * 4,
        out_specs=[VMEM] * (n + 1),
        scratch_shapes=[
            pltpu.VMEM((tiles, 8, points), F32),
            pltpu.VMEM((SELF_CHUNKS, 3 * CHUNK, points), F32),
            pltpu.SemaphoreType.DMA((n,)),
            pltpu.SemaphoreType.DMA((n,)),
        ],
        compiler_params=pltpu.CompilerParams(
            collective_id=ident, has_side_effects=True, vmem_limit_bytes=4 * 1024 * 1024
        ),
    )(*blocks, field, slots, shape, flags, *tables)


def tangents(slots, bounds, owner, target, tables, shape_full, moved_full, same, swap):
    chunks, _, points = same[1].shape
    cap = target.shape[0] // 8
    tiles = shape_full.shape[0] // 8 - 9 * cap
    room = -(-chunks * CHUNK // LANES) * LANES
    head = (slots, bounds, owner, target, *tables)
    image_shape = jax.ShapeDtypeStruct((3, tiles, points), F32)
    kept = [
        jax.ShapeDtypeStruct((chunks, 8 * CHUNK, points), F32),
        pltpu.VMEM((chunks, 16 * 5, 8, points), F32),
    ]
    scratch = [
        pltpu.VMEM((chunks, 3 * CHUNK, points), F32),
        pltpu.VMEM((3, room, points), F32),
    ]
    limit = pltpu.CompilerParams(vmem_limit_bytes=8 * 1024 * 1024)
    first_image, field, *rest = pl.pallas_call(
        functools.partial(apply_kernel, True),
        out_shape=[image_shape] * 2 + [jax.ShapeDtypeStruct((3, cap, points), F32)] * 8 + kept,
        in_specs=[SMEM] * 2 + [VMEM] * 8,
        out_specs=[VMEM] * 12,
        scratch_shapes=scratch,
        compiler_params=limit,
    )(*head, same[1], shape_full, moved_full, same[2])
    image_sends, kept = rest[:8], rest[8:]
    *image_ghosts, done = swap(image_sends, field, slots, same[0], same[1], tables)
    second_image = pl.pallas_call(
        functools.partial(apply_kernel, False),
        out_shape=image_shape,
        in_specs=[SMEM] * 2 + [VMEM] * 17,
        out_specs=VMEM,
        scratch_shapes=[pltpu.VMEM(moved_full.shape, F32)] + scratch,
        compiler_params=limit,
    )(*head, same[1], field, *image_ghosts, done, *kept)
    return first_image, second_image


def on_device(jitter, displacement, modulus, start_vec, old_home, ghost_send, pair_list, pair_count, broken):
    tiles = old_home.shape[0]
    points = jitter.shape[2]
    cap = ghost_send.shape[2]
    sends = jnp.transpose(ghost_send, (1, 0, 2))
    turned = lambda value: jnp.transpose(value, (1, 0, 2))
    rows = tiles + 9 * cap
    full = pltpu.VMEM((rows * 8, points), F32)
    tables = all_tables()
    local = [turned(jitter), turned(displacement), modulus, turned(start_vec)]
    inner = [old_home[None, :], *local, pair_list[0]]
    space = lambda value: pltpu.VMEM(value.shape, value.dtype)
    chunks = -(-(pair_list.shape[2] + CLASSES * (CHUNK - 1)) // CHUNK)
    shape_full, moved_full, *tables, slots, bounds, owner, target, shape, flags, done = pl.pallas_call(
        gather_kernel,
        out_shape=[full, full] + [space(v) for v in tables]
        + [jax.ShapeDtypeStruct((n, LANES), jnp.int32) for n in (24, 16, 8, 8 * cap)]
        + [jax.ShapeDtypeStruct((SELF_CHUNKS, 8 * CHUNK, points), F32), pltpu.VMEM((chunks, 8 * CHUNK, points), jnp.int32)]
        + [jax.ShapeDtypeStruct((3, SELF_CHUNKS * CHUNK, points), F32)],
        in_specs=[HBM] * 10 + [SMEM],
        out_specs=[VMEM] * 11,
        scratch_shapes=[space(value) for value in (broken, *local, inner[0], inner[-1])]
        + [
            pltpu.VMEM((2 * tiles, FIELDS * points), BF16),
            pltpu.VMEM((tiles + 8 * cap, FIELDS * points), F32),
            pltpu.VMEM((4, CAP, LANES), F32),
            pltpu.VMEM((4, CAP, LANES), F32),
            pltpu.VMEM((4, FIELDS, CAP, points), F32),
            pltpu.VMEM((4, FIELDS, CAP, points), F32),
            pltpu.VMEM((8, FIELDS, cap, points), F32),
            pltpu.VMEM((8, FIELDS, cap, points), F32),
            pltpu.VMEM((SELF_CHUNKS, 3 * CHUNK, points), F32),
            pltpu.VMEM((16, LANES), jnp.int32),
            pltpu.SMEM((16, LANES), jnp.int32),
            pltpu.VMEM((tiles, 8, points), F32),
            pltpu.VMEM((tiles, 8, points), F32),
            pltpu.VMEM(sends.shape, jnp.int32),
            pltpu.SemaphoreType.DMA((16,)),
            pltpu.SemaphoreType.DMA((16,)),
            pltpu.SemaphoreType.DMA((11,)),
        ],
        compiler_params=pltpu.CompilerParams(
            collective_id=0, has_side_effects=True, vmem_limit_bytes=16 * 1024 * 1024
        ),
    )(*(pltpu.with_memory_space_constraint(v, pltpu.HBM) for v in (*inner, broken, *tables, sends)), pair_count)
    first_image, second_image = tangents(
        slots, bounds, owner, target, tables, shape_full, moved_full, (shape, flags, done),
        lambda *args: exchange(*args, AROUND, 1)
    )
    return turned(first_image), turned(second_image)


def solution(mesh):
    split = ("gx", "gy")
    spec3, spec2, spec1 = P(split, None, None), P(split, None), P(split)
    return jax.shard_map(
        on_device,
        mesh=mesh,
        in_specs=(spec3, spec3, spec2, spec3, spec1, spec3, spec3, spec1, spec3),
        out_specs=(spec3, spec3),
        check_vma=False,
    )
```
